32 devices in a mesh: rep: 4 (over z), fsdp: 8 (over y, x, core).
Axes of the slice: x: 2, y: 2, z: 4, core: 2. Of those that a mesh axis runs over, the one named last changes fastest.
Arguments:
- tokens: bfloat16 [4, 8, 2048, 1024], P('rep', None, 'fsdp'), may hold values from -6 to 6
- cotangent: bfloat16 [4, 8, 2048, 1024], P('rep', None, 'fsdp'), may hold values from -6 to 6
- lengths: int32 [4, 8], P('rep'), may hold values from 1 to 2048, 8192 in all within a row
- dealing: int32 [4, 8], P('rep'), may hold values from 0 to 7, each once within a row
- norm_gain: bfloat16 [1024], P('fsdp'), may hold values from 0.5 to 1.5
- in_weight: bfloat16 [1024, 4384], P('fsdp'), may hold values from -0.1875 to 0.1875
- conv_weight: bfloat16 [4, 2304], P(None, 'fsdp'), may hold values from -3 to 3
- conv_bias: bfloat16 [2304], P('fsdp'), may hold values from -3 to 3
- dt_bias: float32 [32], replicated, may hold values from -5 to -1
- a_log: float32 [32], replicated, may hold values from -3 to 1
- skip_gain: float32 [32], replicated, may hold values from 0.5 to 2
- out_gain: bfloat16 [2048], P('fsdp'), may hold values from 0.5 to 1.5
- out_weight: bfloat16 [2048, 1024], P('fsdp'), may hold values from -0.125 to 0.125
Outputs:
- output: bfloat16 [4, 8, 2048, 1024], P('rep', None, 'fsdp')
- token_grad: bfloat16 [4, 8, 2048, 1024], P('rep', None, 'fsdp')
- norm_gain_grad: float32 [1024], P('fsdp')
- in_weight_grad: float32 [1024, 4384], P('fsdp')
- conv_weight_grad: float32 [4, 2304], P(None, 'fsdp')
- conv_bias_grad: float32 [2304], P('fsdp')
- dt_bias_grad: float32 [32], replicated
- a_log_grad: float32 [32], replicated
- skip_gain_grad: float32 [32], replicated
- out_gain_grad: float32 [2048], P('fsdp')
- out_weight_grad: float32 [2048, 1024], P('fsdp')
The draws below stay inside these ranges and needn't reach their ends.
Inputs may be any that keep to these rules, and one draw needn't show every extreme that they name: Each group's lengths sum to 8192 and one of them is exactly 2048. `dealing`: each group's row is a permutation of the dealt positions.
All inputs are finite; a program needn't handle non-finite values.
Results may differ from the reference program's by a relative error of at most 0.007.
Values may be sent and summed in bfloat16 or wider, within the bound.
A program may use at most 448 MiB of HBM per device.

```python
import math
import jax
import jax.numpy as jnp
import numpy as np
from jax import lax

D = 1024
STATE = 128
HEADS = 32
HEADDIM = 64
CONV = 4
SPAN = 256
L = 2048
INNER = 2048
CHAN = 2304
PROJ = 4384
SEQS_G = 8
GROUPS = 4


def steps_of(rng, dims, shards, smallest, largest):
    level, own = 1.0, jax.random.fold_in(rng, 6)
    for dim, blocks in shards:
        steps = jnp.exp(jax.random.uniform(jax.random.fold_in(own, dim), (blocks,), jnp.float32, smallest / len(shards), largest / len(shards)))
        level = level * jnp.repeat(steps, dims[dim] // blocks).reshape([-1 if axis == dim else 1 for axis in range(len(dims))])
    return level


def profile(number_of, total, bound, lean):
    loads = [(1 << 20) // math.isqrt(grade ** lean) + 1 for grade in range(2, number_of + 1)]
    rest, given = total - bound - (number_of - 1), [1] * (number_of - 1)
    while rest > 0:
        movable = [i for i in range(number_of - 1) if given[i] < bound]
        whole, left = sum([loads[i] for i in movable]), rest
        for i in movable:
            extra = min(bound - given[i], max(1, left * loads[i] // whole), rest)
            given[i] = given[i] + extra
            rest = rest - extra
    return np.array([bound] + given)


def ragged(own_key, number_of, total, bound, lean):
    if number_of == 2:
        one = jax.random.randint(own_key, (), max(1, total - bound), min(bound, total - 1) + 1)
        return jnp.stack([one, total - one])
    sizes = jnp.asarray(profile(number_of, total, bound, lean), jnp.int32)
    pairs = (number_of - 1) // 2
    donor, taker = sizes[1:1 + 2 * pairs:2], sizes[2:2 + 2 * pairs:2]
    margin = jnp.minimum(donor - 1, bound - taker)
    shifted = jax.random.randint(jax.random.fold_in(own_key, 1), (pairs,), 0, 1 << 20) % (margin + 1)
    sizes = sizes.at[1:1 + 2 * pairs:2].set(donor - shifted).at[2:2 + 2 * pairs:2].set(taker + shifted)
    return sizes[jax.random.permutation(jax.random.fold_in(own_key, 2), number_of)]


def normal_values(key, dims, spread, limit, split=(), held_as=jnp.bfloat16):
    drawn = spread * jax.random.normal(key, dims, jnp.float32)
    if split:
        drawn = drawn * steps_of(key, dims, split, -0.22, 0.18)
    return jnp.clip(drawn, -limit, limit).astype(held_as)


def setup_inputs(seed: int = 0) -> dict:
    keys = jax.random.split(jax.random.key(seed), 14)
    tokens = normal_values(keys[0], (GROUPS, SEQS_G, L, D), 1.0, 6.0, ((0, 4), (2, 8)))
    cotangent = normal_values(keys[1], (GROUPS, SEQS_G, L, D), 1.0, 6.0, ((0, 4), (2, 8)))
    lengths = jax.vmap(lambda own: ragged(own, SEQS_G, SEQS_G * L // 2, L, 2))(jax.random.split(keys[2], GROUPS)).reshape((GROUPS, SEQS_G)).astype(jnp.int32)
    dealing = jax.vmap(lambda own: jax.random.permutation(own, SEQS_G))(jax.random.split(keys[3], GROUPS)).reshape((GROUPS, SEQS_G)).astype(jnp.int32)
    norm_gain = jnp.clip(1.0 + 0.1 * jax.random.normal(keys[4], (D,), jnp.float32), 0.5, 1.5).astype(jnp.bfloat16)
    in_weight = normal_values(keys[5], (D, PROJ), D ** -0.5, 0.1875, ((0, 8),))
    conv_weight = normal_values(keys[6], (CONV, CHAN), CONV ** -0.5, 3.0, ((1, 8),))
    conv_bias = normal_values(keys[7], (CHAN,), 0.5, 3.0, ((0, 8),))
    dt_bias = jnp.clip(jax.random.uniform(keys[8], (HEADS,), jnp.float32, -5.0, -1.0), -5.0, -1.0)
    a_log = jnp.clip(jax.random.uniform(keys[9], (HEADS,), jnp.float32, -3.0, 1.0), -3.0, 1.0)
    skip_gain = jnp.clip(jax.random.uniform(keys[10], (HEADS,), jnp.float32, 0.5, 2.0), 0.5, 2.0)
    out_gain = jnp.clip(1.0 + 0.1 * jax.random.normal(keys[11], (INNER,), jnp.float32), 0.5, 1.5).astype(jnp.bfloat16)
    out_weight = normal_values(keys[12], (INNER, D), INNER ** -0.5, 0.125, ((0, 8),))
    return dict(tokens=tokens, cotangent=cotangent, lengths=lengths, dealing=dealing, norm_gain=norm_gain, in_weight=in_weight, conv_weight=conv_weight, conv_bias=conv_bias, dt_bias=dt_bias, a_log=a_log, skip_gain=skip_gain, out_gain=out_gain, out_weight=out_weight)


@jax.custom_vjp
def low(v):
    return lax.optimization_barrier(v.astype(jnp.bfloat16)).astype(jnp.float32)

@jax.custom_vjp
def low_back(v):
    return v

def low_keep(v):
    return (low(v), None)

def low_pass(kept, grad):
    return (grad,)

def back_keep(v):
    return (v, None)

def backward_lowered(kept, grad):
    return (low(grad),)
low.defvjp(low_keep, low_pass)
low_back.defvjp(back_keep, backward_lowered)
epsilon = 1e-05
largest_value = lax.Precision.HIGHEST

def front_norm(hidden, gain):
    return hidden * lax.rsqrt(lax.optimization_barrier(jnp.mean(hidden * hidden, axis=-1, keepdims=True)) + epsilon) * gain

def block_step(state, block):
    values, state_in, state_out, step_sizes, log_decay = block
    summed = jnp.cumsum(log_decay, axis=0)
    by_head = summed.T
    width = summed.shape[0]
    causal = (jnp.arange(width)[:, None] >= jnp.arange(width)[None, :])[None]
    gaps = by_head[:, :, None] - by_head[:, None, :]
    decay = jnp.where(causal, jnp.exp(jnp.where(causal, gaps, 0.0)), 0.0)
    intersection = jnp.dot(state_out, state_in.T, precision=largest_value)
    weights = intersection[None] * decay * step_sizes.T[:, None, :]
    inside = jnp.einsum('hts,shp->thp', weights, values, precision=largest_value)
    carried = jnp.exp(summed)[:, :, None] * jnp.einsum('tn,hpn->thp', state_out, state, precision=largest_value)
    last_sum = summed[-1]
    tail = jnp.exp(last_sum[None, :] - summed) * step_sizes
    update = jnp.einsum('shp,sn->hpn', tail[:, :, None] * values, state_in, precision=largest_value)
    fresh = jnp.exp(last_sum)[:, None, None] * state + update
    return (fresh, inside + carried)

def scan_blocks(values, state_in, state_out, step_sizes, log_decay):
    length = values.shape[0]
    count = length // SPAN
    blocks = (values.reshape(count, SPAN, HEADS, HEADDIM), state_in.reshape(count, SPAN, STATE), state_out.reshape(count, SPAN, STATE), step_sizes.reshape(count, SPAN, HEADS), log_decay.reshape(count, SPAN, HEADS))
    start = jnp.zeros((HEADS, HEADDIM, STATE), jnp.float32)
    final, outputs = lax.scan(jax.checkpoint(block_step), start, blocks)
    return outputs.reshape(length, HEADS, HEADDIM)

def middle_part(projected, conv_w, conv_b, step_bias, decay_log, direct, gated_gain):
    length = projected.shape[0]
    channels = INNER + 2 * STATE
    gate = projected[:, :INNER]
    conv_in = projected[:, INNER:INNER + channels]
    raw_step = projected[:, INNER + channels:]
    padded = jnp.concatenate([jnp.zeros((CONV - 1, channels), jnp.float32), conv_in], axis=0)
    mixed = jnp.zeros((length, channels), jnp.float32) + conv_b
    for offset in range(CONV):
        mixed = mixed + conv_w[offset] * padded[offset:offset + length]
    mixed = jax.nn.silu(mixed)
    values = mixed[:, :INNER].reshape(length, HEADS, HEADDIM)
    state_in = mixed[:, INNER:INNER + STATE]
    state_out = mixed[:, INNER + STATE:]
    step_sizes = jax.nn.softplus(raw_step + step_bias)
    log_decay = -step_sizes * jnp.exp(decay_log)
    result = scan_blocks(values, state_in, state_out, step_sizes, log_decay) + direct[None, :, None] * values
    result = result.reshape(length, INNER) * jax.nn.silu(gate)
    return front_norm(result, gated_gain)

def branch_of(params, hidden, seq_length):
    first_gain, weight_in, conv_w, conv_b, step_bias, decay_log, direct, gated_gain, weight_out = params
    positions = jnp.arange(hidden.shape[0])
    hidden = low_back(hidden)
    normalized_rows = low(front_norm(hidden, first_gain))
    projected = low_back(jnp.dot(normalized_rows, weight_in, precision=largest_value))
    mixed = low(middle_part(projected, conv_w, conv_b, step_bias, decay_log, direct, gated_gain))
    keep = (positions < seq_length).astype(jnp.float32)[:, None]
    return low(jnp.dot(mixed, weight_out, precision=largest_value) * keep)

def reference(tokens, cotangent, lengths, dealing, norm_gain, in_weight, conv_weight, conv_bias, dt_bias, a_log, skip_gain, out_gain, out_weight):
    seq_lengths = jnp.take_along_axis(lengths, dealing, axis=1).reshape(-1).astype(jnp.int32)
    flat_tokens = tokens.astype(jnp.float32).reshape(-1, L, D)
    flat_grad = cotangent.astype(jnp.float32).reshape(-1, L, D)
    params = (norm_gain.astype(jnp.float32), in_weight.astype(jnp.float32), conv_weight.astype(jnp.float32), conv_bias.astype(jnp.float32), dt_bias.astype(jnp.float32), a_log.astype(jnp.float32), skip_gain.astype(jnp.float32), out_gain.astype(jnp.float32), out_weight.astype(jnp.float32))

    def forward(weights, flat):

        def lone_sequence(pair):
            return jax.checkpoint(branch_of)(weights, pair[0], pair[1])
        return flat + lax.map(lone_sequence, (flat, seq_lengths))
    output, pullback = jax.vjp(forward, params, flat_tokens)
    weight_grads, token_grads = pullback(flat_grad)
    return (output.astype(jnp.bfloat16).reshape(tokens.shape), token_grads.astype(jnp.bfloat16).reshape(tokens.shape), weight_grads[0], weight_grads[1], weight_grads[2], weight_grads[3], weight_grads[4], weight_grads[5], weight_grads[6], weight_grads[7], weight_grads[8])
```

```python
import functools
import jax
import jax.numpy as jnp
from jax import lax
from jax.experimental import pallas as pl
from jax.experimental.pallas import tpu as pltpu
from jax.sharding import PartitionSpec as P

STATE = 128
HEADDIM = 64
HEADS = 32
INNER = 2048
CONV = 4
BLOCK = 256
CHUNK = 128
LANES = 128
MESH = pl.DeviceIdType.MESH
EPS = 1e-05
F32 = jnp.float32
BF16 = jnp.bfloat16
FAR = -1e9
NT = (((1,), (1,)), ((), ()))
TN = (((0,), (0,)), ((), ()))


def mm(a, b, dims=(((1,), (0,)), ((), ()))):
    return lax.dot_general(a, b, dims, preferred_element_type=F32)


def two_parts(v):
    high = v.astype(BF16)
    return high, (v - high.astype(F32)).astype(BF16)


def spread(v, expand):
    high, low = two_parts(v)
    return mm(jnp.concatenate([high, low], axis=1), expand)


def gather_heads(v, collect):
    high, low = two_parts(v)
    return mm(high, collect) + mm(low, collect)


def sigmoid(v):
    return 0.5 + 0.5 * jnp.tanh(0.5 * v)


def mm_state(rows, state):
    return mm(jnp.concatenate([rows, rows], axis=1), jnp.concatenate(two_parts(state), axis=0))


def softplus(v):
    return jnp.maximum(v, 0.0) + jnp.log1p(jnp.exp(-jnp.abs(v)))


def causal_sum(log_decay):
    rows = lax.broadcasted_iota(jnp.int32, (CHUNK, CHUNK), 0)
    cols = lax.broadcasted_iota(jnp.int32, (CHUNK, CHUNK), 1)
    tri = (rows >= cols).astype(F32)
    return lax.dot_general(
        tri, log_decay, (((1,), (0,)), ((), ())),
        precision=lax.Precision.HIGHEST, preferred_element_type=F32,
    )


def reverse_sum(v):
    rows = lax.broadcasted_iota(jnp.int32, (CHUNK, CHUNK), 0)
    cols = lax.broadcasted_iota(jnp.int32, (CHUNK, CHUNK), 1)
    tri = (cols >= rows).astype(F32)
    return lax.dot_general(
        tri, v, (((1,), (0,)), ((), ())),
        precision=lax.Precision.HIGHEST, preferred_element_type=F32,
    )


def convolve(cbuf, cw_ref, cb_ref, cols):
    total = cb_ref[0:1, cols] + cw_ref[3:4, cols] * cbuf[8 : 8 + BLOCK, cols]
    for k in range(CONV - 1):
        total = total + cw_ref[k : k + 1, cols] * cbuf[5 + k : 5 + k + BLOCK, cols]
    return total


def normalize(tok_ref, gain_ref):
    hidden = tok_ref[0].astype(F32)
    scale = lax.rsqrt(jnp.mean(hidden * hidden, axis=1, keepdims=True) + EPS)
    return (hidden * scale * gain_ref[0:1, :]).astype(BF16)


def fwd_kernel(
    inner, heads,
    nb_ref, tok_ref, gain_ref, win_ref, cw_ref, cb_ref, hp_ref, dwide_ref, og_ref, expand_ref,
    gate_ref, cin_ref, raw_ref, y_ref, s_ref, ss_ref, sc_ref,
    cbuf, xbuf, state,
):
    seq, blk = pl.program_id(0), pl.program_id(1)
    chan = inner + 2 * STATE

    @pl.when(blk < nb_ref[seq])
    def _():
        @pl.when(blk == 0)
        def _():
            cbuf[0:8, :] = jnp.zeros((8, chan), F32)
            state[...] = jnp.zeros_like(state)

        @pl.when(blk > 0)
        def _():
            cbuf[0:8, :] = cbuf[BLOCK : BLOCK + 8, :]

        normed = normalize(tok_ref, gain_ref)
        for j in range(0, inner, 256):
            gate_ref[0, :, j : j + 256] = mm(normed, win_ref[:, j : j + 256])
        for j in range(0, chan, 256):
            part = mm(normed, win_ref[:, inner + j : inner + j + 256])
            cin_ref[0, :, j : j + 256] = part
            cbuf[8 : 8 + BLOCK, j : j + 256] = part
        raw = mm(normed, win_ref[:, inner + chan :])
        raw_ref[0] = raw
        for j in range(0, chan, 256):
            u = convolve(cbuf, cw_ref, cb_ref, slice(j, j + 256))
            xbuf[:, j : j + 256] = u * sigmoid(u)
        step = softplus(raw + hp_ref[0:1, :])
        log_decay = -step * hp_ref[1:2, :]
        rows = lax.broadcasted_iota(jnp.int32, (CHUNK, CHUNK), 0)
        cols = lax.broadcasted_iota(jnp.int32, (CHUNK, CHUNK), 1)
        causal = rows >= cols
        left = cols < HEADDIM
        for c in range(BLOCK // CHUNK):
            at = slice(c * CHUNK, (c + 1) * CHUNK)
            dt = step[at]
            cum = causal_sum(log_decay[at])
            cum_t = cum.T
            last = cum[CHUNK - 1 : CHUNK]
            three = jnp.concatenate([jnp.exp(cum), dt, jnp.exp(last - cum) * dt], axis=0)
            wide = spread(three, expand_ref[...])
            e_wide, dt_wide, w_wide = wide[:CHUNK], wide[CHUNK : 2 * CHUNK], wide[2 * CHUNK :]
            s_in = xbuf[at, inner : inner + STATE].astype(BF16)
            s_out = xbuf[at, inner + STATE :].astype(BF16)
            cross = mm(s_out, s_in, NT)
            x = xbuf[at, :inner]
            xd = (x * dt_wide).astype(BF16)
            xw = (x * w_wide).astype(BF16)
            held = state[...]
            s_ref[0, c] = held
            carried = e_wide * mm_state(s_out, held)
            for p in range(heads // 2):
                lanes = slice(p * 128, (p + 1) * 128)
                pair = xd[:, lanes]
                zero = jnp.zeros_like(pair)
                both = jnp.concatenate([jnp.where(left, pair, zero), jnp.where(left, zero, pair)], axis=0)
                parts = []
                for h in (2 * p, 2 * p + 1):
                    gap = cum[:, h : h + 1] - cum_t[h : h + 1, :]
                    parts.append((cross * jnp.exp(jnp.where(causal, gap, FAR))).astype(BF16))
                y_ref[0, at, lanes] = carried[:, lanes] + mm(jnp.concatenate(parts, axis=1), both)
            state[...] = e_wide[CHUNK - 1 : CHUNK] * held + mm(s_in, xw, TN)
        total = jnp.zeros((BLOCK, 1), F32)
        for j in range(0, inner, 256):
            at = slice(j, j + 256)
            gate = gate_ref[0, :, at]
            gated = (y_ref[0, :, at] + dwide_ref[0:1, at] * xbuf[:, at]) * (gate * sigmoid(gate))
            total = total + jnp.sum(gated * gated, axis=1, keepdims=True)
            sc_ref[0, :, at] = gated * og_ref[0:1, at]
        ss_ref[...] = jnp.broadcast_to(total, (BLOCK, LANES)).T[0:8]


def fixed(shape):
    return pl.BlockSpec(shape, lambda *_: (0,) * len(shape), pipeline_mode=pl.Buffered(1))


def fwd_call(nb, tok, gain, win, cw, cb, hp, dwide, og, expand):
    nseq, length, width = tok.shape
    inner = dwide.shape[1]
    heads = inner // HEADDIM
    chan = inner + 2 * STATE
    blocks = length // BLOCK

    def rows(s, b, nb):
        return (s, jnp.maximum(jnp.minimum(b, nb[s] - 1), 0), 0)

    def srows(s, b, nb):
        return (s, jnp.maximum(jnp.minimum(b, nb[s] - 1), 0), 0, 0)

    def ssrows(s, b, nb):
        return (s * blocks + jnp.maximum(jnp.minimum(b, nb[s] - 1), 0), 0)

    grid_spec = pltpu.PrefetchScalarGridSpec(
        num_scalar_prefetch=1,
        grid=(nseq, blocks),
        in_specs=[
            pl.BlockSpec((1, BLOCK, width), rows),
            fixed(gain.shape), fixed(win.shape), fixed(cw.shape), fixed(cb.shape),
            fixed(hp.shape), fixed(dwide.shape), fixed(og.shape), fixed(expand.shape),
        ],
        out_specs=[
            pl.BlockSpec((1, BLOCK, inner), rows),
            pl.BlockSpec((1, BLOCK, chan), rows),
            pl.BlockSpec((1, BLOCK, LANES), rows),
            pl.BlockSpec((1, BLOCK, inner), rows),
            pl.BlockSpec((1, BLOCK // CHUNK, STATE, inner), srows),
            pl.BlockSpec((8, BLOCK), ssrows),
            pl.BlockSpec((1, BLOCK, inner), rows),
        ],
        scratch_shapes=[
            pltpu.VMEM((BLOCK + 8, chan), F32),
            pltpu.VMEM((BLOCK, chan), F32),
            pltpu.VMEM((STATE, inner), F32),
        ],
    )
    shapes = [
        jax.ShapeDtypeStruct((nseq, length, inner), F32),
        jax.ShapeDtypeStruct((nseq, length, chan), F32),
        jax.ShapeDtypeStruct((nseq, length, LANES), F32),
        jax.ShapeDtypeStruct((nseq, length, inner), F32),
        jax.ShapeDtypeStruct((nseq, length // CHUNK, STATE, inner), F32),
        jax.ShapeDtypeStruct((nseq * blocks * 8, BLOCK), F32),
        jax.ShapeDtypeStruct((nseq, length, inner), F32),
    ]
    return pl.pallas_call(
        functools.partial(fwd_kernel, inner, heads),
        grid_spec=grid_spec,
        out_shape=shapes,
        compiler_params=pltpu.CompilerParams(
            dimension_semantics=("arbitrary", "arbitrary"), vmem_limit_bytes=60 * 1024 * 1024
        ),
        cost_estimate=pl.CostEstimate(
            flops=nseq * length * width * (3 * inner + 400), bytes_accessed=60 << 20, transcendentals=0
        ),
        name="layer_forward",
    )(nb, tok, gain, win, cw, cb, hp, dwide, og, expand)


def mid_kernel(nb_ref, len_ref, cot_ref, sc_ref, wout_ref, gm_ref, v_ref, bp_ref):
    seq, blk = pl.program_id(0), pl.program_id(1)

    @pl.when(blk < nb_ref[seq])
    def _():
        cot = cot_ref[0]
        position = blk * BLOCK + lax.broadcasted_iota(jnp.int32, cot.shape, 0)
        gb = jnp.where(position < len_ref[seq], cot, jnp.zeros_like(cot))
        total = jnp.zeros((BLOCK, 1), F32)
        for j in range(0, sc_ref.shape[2], 256):
            at = slice(j, j + 256)
            gm = mm(gb, wout_ref[at, :], NT)
            gm_ref[0, :, at] = gm
            total = total + jnp.sum(gm * sc_ref[0, :, at], axis=1, keepdims=True)
        v_ref[...] = jnp.broadcast_to(total, (BLOCK, LANES)).T[0:8]
        scaled = sc_ref[0].astype(BF16)
        for j in range(0, cot.shape[1], 256):
            bp_ref[0, :, j : j + 256] = mm(scaled, wout_ref[:, j : j + 256]).astype(BF16)


def mid_call(nb, lens, cot, scaled, wout):
    nseq, length, width = cot.shape
    inner = wout.shape[0]
    blocks = length // BLOCK

    def place(s, b, nb):
        return jnp.maximum(jnp.minimum(b, nb[s] - 1), 0)

    def rows(s, b, nb, lens):
        return (s, place(s, b, nb), 0)

    def vrows(s, b, nb, lens):
        return (s * blocks + place(s, b, nb), 0)

    return pl.pallas_call(
        mid_kernel,
        grid_spec=pltpu.PrefetchScalarGridSpec(
            num_scalar_prefetch=2,
            grid=(nseq, blocks),
            in_specs=[pl.BlockSpec((1, BLOCK, width), rows), pl.BlockSpec((1, BLOCK, inner), rows), fixed(wout.shape)],
            out_specs=[
                pl.BlockSpec((1, BLOCK, inner), rows), pl.BlockSpec((8, BLOCK), vrows),
                pl.BlockSpec((1, BLOCK, width), rows),
            ],
        ),
        out_shape=[
            jax.ShapeDtypeStruct((nseq, length, inner), F32),
            jax.ShapeDtypeStruct((nseq * blocks * 8, BLOCK), F32),
            jax.ShapeDtypeStruct((nseq, length, width), BF16),
        ],
        compiler_params=pltpu.CompilerParams(
            dimension_semantics=("arbitrary", "arbitrary"), vmem_limit_bytes=40 * 1024 * 1024
        ),
        cost_estimate=pl.CostEstimate(flops=10**10, bytes_accessed=30 << 20, transcendentals=0),
        name="layer_middle",
    )(nb, lens, cot, scaled, wout)


def bwd_kernel(
    inner, heads, blocks,
    nb_ref, len_ref,
    tok_ref, cot_ref, gain_ref, win_ref, gm_ref, cw_ref, cb_ref, hp_ref, dwide_ref, og_ref, expand_ref,
    collect_ref, gate_ref, cin_ref, halo_ref, raw_ref, y_ref, s_ref, rv_ref,
    gn_ref, win_out, wout_out, dcw_ref, dhp_ref, dog_ref, ddw_ref,
    cbuf, ubuf, dbuf, xbuf, dybuf, dproj, dstate, later, dwin_ref, dwout_ref,
):
    seq, step_id = pl.program_id(0), pl.program_id(1)
    chan = inner + 2 * STATE
    width = tok_ref.shape[2]
    nb = nb_ref[seq]
    blk = nb - 1 - step_id

    @pl.when((seq == 0) & (step_id == 0))
    def _():
        dwin_ref[...] = jnp.zeros_like(dwin_ref)
        dwout_ref[...] = jnp.zeros_like(dwout_ref)
        dcw_ref[...] = jnp.zeros_like(dcw_ref)
        dhp_ref[...] = jnp.zeros_like(dhp_ref)
        dog_ref[...] = jnp.zeros_like(dog_ref)
        ddw_ref[...] = jnp.zeros_like(ddw_ref)

    @pl.when(blk >= 0)
    def _():
        @pl.when(step_id == 0)
        def _():
            dbuf[BLOCK : BLOCK + 8, :] = jnp.zeros((8, chan), F32)
            dstate[...] = jnp.zeros_like(dstate)
            later[...] = jnp.zeros_like(later)

        @pl.when(step_id > 0)
        def _():
            dbuf[BLOCK : BLOCK + 8, :] = dbuf[0:8, :]

        @pl.when(blk == 0)
        def _():
            cbuf[0:8, :] = jnp.zeros((8, chan), F32)

        @pl.when(blk > 0)
        def _():
            cbuf[0:8, :] = halo_ref[0]

        cbuf[8 : 8 + BLOCK, :] = cin_ref[0]
        position = blk * BLOCK + lax.broadcasted_iota(jnp.int32, (BLOCK, width), 0)
        cot = cot_ref[0]
        gb = jnp.where(position < len_ref[seq], cot, jnp.zeros_like(cot))
        rv = jnp.concatenate([rv_ref[...], jnp.zeros((LANES - 8, BLOCK), F32)], axis=0).T
        scale, coef = rv[:, 0:1], rv[:, 1:2]
        for j in range(0, chan, 256):
            at = slice(j, j + 256)
            u = convolve(cbuf, cw_ref, cb_ref, at)
            sig = sigmoid(u)
            xbuf[:, at] = u * sig
            ubuf[:, at] = sig * (1.0 + u * (1.0 - sig))
        for j in range(0, inner, 256):
            at = slice(j, j + 256)
            gm = gm_ref[0, :, at]
            gate = gate_ref[0, :, at]
            sig = sigmoid(gate)
            x = xbuf[:, at]
            ysum = y_ref[0, :, at] + dwide_ref[0:1, at] * x
            gated = ysum * (gate * sig)
            normal = gated * scale
            mixed = (normal * og_ref[0:1, at]).astype(BF16)
            dwout_ref[at, :] += mm(mixed, gb, TN)
            dog_ref[0:1, at] += jnp.sum(gm * normal, axis=0, keepdims=True)
            dgated = scale * (gm * og_ref[0:1, at]) - gated * coef
            dproj[:, at] = (dgated * ysum * (sig * (1.0 + gate * (1.0 - sig)))).astype(BF16)
            dy = dgated * (gate * sig)
            ddw_ref[0:1, at] += jnp.sum(dy * x, axis=0, keepdims=True)
            dybuf[:, at] = dy
        raw = raw_ref[0] + hp_ref[0:1, :]
        step = softplus(raw)
        log_decay = -step * hp_ref[1:2, :]
        rows = lax.broadcasted_iota(jnp.int32, (CHUNK, CHUNK), 0)
        cols = lax.broadcasted_iota(jnp.int32, (CHUNK, CHUNK), 1)
        causal = cols >= rows
        left = cols < HEADDIM
        for c in reversed(range(BLOCK // CHUNK)):
            at = slice(c * CHUNK, (c + 1) * CHUNK)
            dt = step[at]
            cum = causal_sum(log_decay[at])
            cum_t = cum.T
            last = cum[CHUNK - 1 : CHUNK]
            tail = jnp.exp(last - cum)
            four = jnp.concatenate([jnp.exp(cum), dt, tail], axis=0)
            wide = spread(four, expand_ref[...])
            e_wide, dt_wide, t_wide = wide[:CHUNK], wide[CHUNK : 2 * CHUNK], wide[2 * CHUNK :]
            s_in = xbuf[at, inner : inner + STATE].astype(BF16)
            s_out = xbuf[at, inner + STATE :].astype(BF16)
            cross = mm(s_in, s_out, NT)
            x = xbuf[at, :inner]
            dy = dybuf[at, :]
            dy16 = dy.astype(BF16)
            xd32 = x * dt_wide
            xd = xd32.astype(BF16)
            xw = (xd32 * t_wide).astype(BF16)
            held32 = s_ref[0, c]
            held = held32.astype(BF16)
            dheld = dstate[...]
            dheld16 = dheld.astype(BF16)
            edy = (e_wide * dy).astype(BF16)
            back = mm_state(s_in, dheld)
            reach = mm_state(s_out, held32)
            dcross = jnp.zeros((CHUNK, CHUNK), F32)
            dxd_parts = []
            for p in range(heads // 2):
                lanes = slice(p * 128, (p + 1) * 128)
                pair = xd[:, lanes]
                dpair = dy16[:, lanes]
                zero = jnp.zeros_like(pair)
                both = jnp.concatenate([jnp.where(left, dpair, zero), jnp.where(left, zero, dpair)], axis=0)
                dweights = mm(pair, both, NT)
                parts = []
                for i, h in enumerate((2 * p, 2 * p + 1)):
                    gap = cum_t[h : h + 1, :] - cum[:, h : h + 1]
                    decay = jnp.exp(jnp.where(causal, gap, FAR))
                    parts.append((cross * decay).astype(BF16))
                    dcross = dcross + dweights[:, i * CHUNK : (i + 1) * CHUNK] * decay
                dxd_parts.append(mm(jnp.concatenate(parts, axis=1), both))
            inside = jnp.concatenate(dxd_parts, axis=1)
            dxd = inside + t_wide * back
            fold = jnp.sum(dheld * later[...], axis=0, keepdims=True)
            direct = x * dxd
            scanned = (y_ref[0, at, :] - e_wide * reach) * dy16.astype(F32) + edy.astype(F32) * reach
            scanned = scanned - xd.astype(F32) * inside - xw.astype(F32) * back
            stacked = jnp.concatenate([direct, scanned, jnp.broadcast_to(fold, (8, inner))], axis=0)
            small = gather_heads(stacked, collect_ref[...])
            ddirect, dcum = small[:CHUNK], small[CHUNK : 2 * CHUNK]
            dlog = reverse_sum(dcum) + small[2 * CHUNK : 2 * CHUNK + 1]
            dstep = ddirect - dlog * hp_ref[1:2, :]
            draw = dstep * sigmoid(raw[at])
            dhp_ref[0:1, :] += jnp.sum(draw, axis=0, keepdims=True)
            dhp_ref[1:2, :] += jnp.sum(dlog * log_decay[at], axis=0, keepdims=True)
            dproj[at, inner + chan :] = draw.astype(BF16)
            dybuf[at, :] = dt_wide * dxd + dwide_ref[0:1, :] * dy
            dcross16 = dcross.astype(BF16)
            ds_in = mm(dcross16, s_out) + mm(xw, dheld16, NT)
            ds_out = mm(dcross16, s_in, TN) + mm(edy, held, NT)
            dbuf[at, inner : inner + STATE] = ds_in
            dbuf[at, inner + STATE :] = ds_out
            later[...] = held32
            dstate[...] = e_wide[CHUNK - 1 : CHUNK] * dheld + mm(s_out, edy, TN)
        for j in range(0, chan, 256):
            at = slice(j, j + 256)
            grad = dybuf[:, at] if j < inner else dbuf[0:BLOCK, at]
            du = grad * ubuf[:, at]
            dbuf[0:BLOCK, at] = du
            dcw_ref[CONV : CONV + 1, at] += jnp.sum(du, axis=0, keepdims=True)
            for k in range(CONV):
                dcw_ref[k : k + 1, at] += jnp.sum(du * cbuf[5 + k : 5 + k + BLOCK, at], axis=0, keepdims=True)
            dcin = cw_ref[CONV - 1 : CONV, at] * du
            for k in range(CONV - 1):
                dcin = dcin + cw_ref[k : k + 1, at] * dbuf[3 - k : 3 - k + BLOCK, at]
            dproj[:, inner + j : inner + j + 256] = dcin.astype(BF16)
        normed = normalize(tok_ref, gain_ref)
        count = dproj.shape[1]
        for j in range(0, count, 256):
            at = slice(j, min(j + 256, count))
            dwin_ref[:, at] += mm(normed, dproj[:, at], TN)
        for j in range(0, width, 256):
            gn_ref[0, :, j : j + 256] = mm(dproj[...], win_ref[j : j + 256, :], NT).astype(BF16)

    @pl.when((seq == pl.num_programs(0) - 1) & (step_id == blocks - 1))
    def _():
        win_out[...] = dwin_ref[...].astype(BF16)
        wout_out[...] = dwout_ref[...].astype(BF16)


def bwd_call(nb, lens, tok, cot, gain, win, gm, cw, cb, hp, dwide, og, expand, collect, gate, cin, raw, y, s, rv):
    nseq, length, width = tok.shape
    inner = gm.shape[2]
    heads = inner // HEADDIM
    chan = inner + 2 * STATE
    blocks = length // BLOCK

    def place(s, b, nb):
        return jnp.maximum(nb[s] - 1 - b, 0)

    def rows(s, b, nb, lens):
        return (s, place(s, b, nb), 0)

    def srows(s, b, nb, lens):
        return (s, place(s, b, nb), 0, 0)

    def halo(s, b, nb, lens):
        return (s, jnp.maximum(place(s, b, nb) * (BLOCK // 8) - 1, 0), 0)

    def rvrows(s, b, nb, lens):
        return (s * blocks + place(s, b, nb), 0)

    def whole(shape):
        return pl.BlockSpec(shape, lambda *_: (0,) * len(shape), pipeline_mode=pl.Buffered(1))

    grid_spec = pltpu.PrefetchScalarGridSpec(
        num_scalar_prefetch=2,
        grid=(nseq, blocks),
        in_specs=[
            pl.BlockSpec((1, BLOCK, width), rows),
            pl.BlockSpec((1, BLOCK, width), rows),
            fixed(gain.shape), fixed(win.shape), pl.BlockSpec((1, BLOCK, inner), rows), fixed(cw.shape), fixed(cb.shape),
            fixed(hp.shape), fixed(dwide.shape), fixed(og.shape), fixed(expand.shape), fixed(collect.shape),
            pl.BlockSpec((1, BLOCK, inner), rows),
            pl.BlockSpec((1, BLOCK, chan), rows),
            pl.BlockSpec((1, 8, chan), halo),
            pl.BlockSpec((1, BLOCK, LANES), rows),
            pl.BlockSpec((1, BLOCK, inner), rows),
            pl.BlockSpec((1, BLOCK // CHUNK, STATE, inner), srows),
            pl.BlockSpec((8, BLOCK), rvrows),
        ],
        out_specs=[
            pl.BlockSpec((1, BLOCK, width), rows),
            whole(win.shape), whole((inner, width)), whole((8, chan)), whole((8, LANES)), whole((8, inner)),
            whole((8, inner)),
        ],
        scratch_shapes=[
            pltpu.VMEM((BLOCK + 8, chan), F32),
            pltpu.VMEM((BLOCK, chan), F32),
            pltpu.VMEM((BLOCK + 8, chan), F32),
            pltpu.VMEM((BLOCK, chan), F32),
            pltpu.VMEM((BLOCK, inner), F32),
            pltpu.VMEM((BLOCK, win.shape[1]), BF16),
            pltpu.VMEM((STATE, inner), F32),
            pltpu.VMEM((STATE, inner), F32),
            pltpu.VMEM(win.shape, F32),
            pltpu.VMEM((inner, width), F32),
        ],
    )
    shapes = [
        jax.ShapeDtypeStruct((nseq, length, width), BF16),
        jax.ShapeDtypeStruct(win.shape, BF16),
        jax.ShapeDtypeStruct((inner, width), BF16),
        jax.ShapeDtypeStruct((8, chan), F32),
        jax.ShapeDtypeStruct((8, LANES), F32),
        jax.ShapeDtypeStruct((8, inner), F32),
        jax.ShapeDtypeStruct((8, inner), F32),
    ]
    return pl.pallas_call(
        functools.partial(bwd_kernel, inner, heads, blocks),
        grid_spec=grid_spec,
        out_shape=shapes,
        compiler_params=pltpu.CompilerParams(
            dimension_semantics=("arbitrary", "arbitrary"), vmem_limit_bytes=63 * 1024 * 1024
        ),
        cost_estimate=pl.CostEstimate(
            flops=2 * nseq * length * width * (3 * inner + 400), bytes_accessed=100 << 20, transcendentals=0
        ),
        name="layer_backward",
    )(nb, lens, tok, cot, gain, win, gm, cw, cb, hp, dwide, og, expand, collect, gate, cin, cin, raw, y, s, rv)


def matrices(inner):
    heads = inner // HEADDIM
    owner = jnp.arange(inner, dtype=jnp.int32) // HEADDIM
    head = jnp.arange(LANES, dtype=jnp.int32)
    one = (head[:, None] == owner[None, :]).astype(BF16)
    return jnp.concatenate([one, one], axis=0), one.T


def combine_kernel(place_ref, count_ref, base_ref, part_ref, out_ref):
    kept = count_ref[pl.program_id(0)]
    base = base_ref[0]
    row = lax.broadcasted_iota(jnp.int32, base.shape, 0)
    part = jnp.where(row < kept, part_ref[0].astype(F32), 0.0)
    out_ref[0] = (base.astype(F32) + part).astype(BF16)


def combine_call(place, kept, base, part):
    count, span, width = base.shape
    block = (1, span, width)
    return pl.pallas_call(
        combine_kernel,
        grid_spec=pltpu.PrefetchScalarGridSpec(
            num_scalar_prefetch=2,
            grid=(count,),
            in_specs=[
                pl.BlockSpec(block, lambda s, place, kept: (s, 0, 0)),
                pl.BlockSpec(block, lambda s, place, kept: (place[s], 0, 0)),
            ],
            out_specs=pl.BlockSpec(block, lambda s, place, kept: (s, 0, 0)),
        ),
        out_shape=jax.ShapeDtypeStruct(base.shape, BF16),
        name="combine",
    )(place, kept, base, part)


def peers_of(n):
    return [(away, turn) for away in range(n // 2) for turn in range(2) if away or turn]


def enter(n, me):
    barrier = pltpu.get_barrier_semaphore()
    for away, turn in peers_of(n):
        pl.semaphore_signal(barrier, inc=1, device_id={"fsdp": peer_at(n, me, away, turn)}, device_id_type=MESH)
    pl.semaphore_wait(barrier, n - 1)


def peer_at(n, me, away, turn):
    chip = lax.rem(lax.div(me, 2) + away, n // 2)
    return 2 * chip + lax.rem(lax.rem(me, 2) + turn, 2)


def sender_at(n, me, away, turn):
    chip = lax.rem(lax.div(me, 2) + n // 2 - away, n // 2)
    return 2 * chip + lax.rem(lax.rem(me, 2) + turn, 2)


def rows_at(index, size):
    return pl.ds(pl.multiple_of(index * size, size), size)


def start_kernel(
    n, sent, shards, small, tok, win, smalls, here, w_send, w_recv, t_send, t_recv, f_send, f_recv, s_send, s_recv
):
    me = lax.axis_index("fsdp")
    core = lax.rem(me, 2)
    chip = lax.div(me, 2)
    partner = 2 * chip + 1 - core
    span, rows = sent.shape[1], shards.shape[1]
    enter(n, me)
    pending = []
    for index, (away, turn) in enumerate(peers_of(n)):
        peer = peer_at(n, me, away, turn)
        theirs = lax.rem(core + turn, 2)

        def push(src, dst, send, recv):
            copy = pltpu.make_async_remote_copy(
                src_ref=src, dst_ref=dst, send_sem=send, recv_sem=recv, device_id={"fsdp": peer}, device_id_type=MESH
            )
            copy.start()
            pending.append(copy)

        push(sent.at[peer], tok.at[theirs, rows_at(me, span)], t_send.at[index], t_recv.at[index])
        push(shards.at[theirs], win.at[rows_at(me, rows)], w_send.at[index], w_recv.at[index])
        push(small, smalls.at[me], s_send.at[index], s_recv.at[index])
    local = [
        pltpu.make_async_copy(sent.at[me], tok.at[core, rows_at(me, span)], here.at[0]),
        pltpu.make_async_copy(sent.at[partner], tok.at[1 - core, rows_at(me, span)], here.at[1]),
        pltpu.make_async_copy(shards.at[core], win.at[rows_at(me, rows)], here.at[2]),
        pltpu.make_async_copy(small, smalls.at[me], here.at[3]),
    ]
    for copy in local:
        copy.start()

    def forward(index, src, owner):
        copy = pltpu.make_async_remote_copy(
            src_ref=src, dst_ref=tok.at[core, rows_at(owner, span)], send_sem=f_send.at[index],
            recv_sem=f_recv.at[index], device_id={"fsdp": partner}, device_id_type=MESH,
        )
        copy.start()
        return copy

    passed = [forward(0, sent.at[me], me)]
    for index, (away, turn) in enumerate(peers_of(n)):
        owner = sender_at(n, me, away, turn)
        block = tok.at[core, rows_at(owner, span)]
        pltpu.make_async_remote_copy(
            src_ref=block, dst_ref=block, send_sem=t_send.at[index], recv_sem=t_recv.at[index],
            device_id={"fsdp": partner}, device_id_type=MESH,
        ).wait_recv()
        if away:
            passed.append(forward(index, block, owner))
    for copy in passed:
        copy.wait()
    for copy in pending:
        copy.wait_send()
    for index, (away, turn) in enumerate(peers_of(n)):
        owner = sender_at(n, me, away, turn)
        checks = [(win.at[rows_at(owner, rows)], w_send, w_recv), (smalls.at[owner], s_send, s_recv)]
        for block, send, recv in checks:
            pltpu.make_async_remote_copy(
                src_ref=block, dst_ref=block, send_sem=send.at[index], recv_sem=recv.at[index],
                device_id={"fsdp": partner}, device_id_type=MESH,
            ).wait_recv()
    for copy in local:
        copy.wait()


def start_call(n, sent, shards, small):
    span, width = sent.shape[1:]
    _, rows, wide = shards.shape
    count = n - 1
    anywhere = pl.BlockSpec(memory_space=pl.ANY)
    return pl.pallas_call(
        functools.partial(start_kernel, n),
        out_shape=[
            jax.ShapeDtypeStruct((2, n * span, width), BF16),
            jax.ShapeDtypeStruct((n * rows, wide), BF16),
            jax.ShapeDtypeStruct((n,) + small.shape, BF16),
        ],
        in_specs=[anywhere] * 3,
        out_specs=[anywhere] * 3,
        scratch_shapes=[pltpu.SemaphoreType.DMA((4,))] + [pltpu.SemaphoreType.DMA((count,))] * 8,
        compiler_params=pltpu.CompilerParams(collective_id=0, has_side_effects=True),
        name="start",
    )(sent, shards, small)


def exchange_kernel(
    bp, ss_ref, v_ref, branch, rv_ref, mine, theirs, ss_in, v_in, here, put, b_send, b_recv, s_send, s_recv
):
    me = lax.axis_index("fsdp")
    core = lax.rem(me, 2)
    partner = 2 * lax.div(me, 2) + 1 - core
    length, width = mine.shape
    blocks = length // BLOCK
    barrier = pltpu.get_barrier_semaphore()
    pl.semaphore_signal(barrier, inc=1, device_id={"fsdp": partner}, device_id_type=MESH)
    pl.semaphore_wait(barrier, 1)

    def remote(src, dst, send, recv):
        return pltpu.make_async_remote_copy(
            src_ref=src, dst_ref=dst, send_sem=send, recv_sem=recv, device_id={"fsdp": partner}, device_id_type=MESH
        )

    load = pltpu.make_async_copy(bp.at[core], mine, here.at[0])
    load.start()
    copies = [
        remote(ss_ref, ss_in, s_send.at[0], s_recv.at[0]),
        remote(v_ref, v_in, s_send.at[1], s_recv.at[1]),
    ]
    for b in range(blocks):
        at = pl.ds(b * BLOCK, BLOCK)
        copies.append(remote(bp.at[1 - core, at], theirs.at[at], b_send.at[b], b_recv.at[b]))
    for copy in copies:
        copy.start()
    for copy in copies[:2]:
        copy.wait_recv()
    scale = lax.rsqrt((ss_ref[...] + ss_in[...]) * (1.0 / INNER) + EPS)
    coef = scale * scale * scale * (v_ref[...] + v_in[...]) * (1.0 / INNER)
    sub = lax.rem(lax.broadcasted_iota(jnp.int32, scale.shape, 0), 8)
    rv_ref[...] = jnp.where(sub == 0, scale, coef)
    load.wait()
    puts = []
    for b in range(blocks):
        at = pl.ds(b * BLOCK, BLOCK)
        copies[2 + b].wait_recv()
        rows = rv_ref[pl.ds(pl.multiple_of((core * blocks + b) * 8, 8), 8), :]
        column = jnp.concatenate([rows, jnp.zeros((LANES - 8, BLOCK), F32)], axis=0).T[:, 0:1]
        mine[at, :] = ((mine[at, :].astype(F32) + theirs[at, :].astype(F32)) * column).astype(BF16)
        copy = pltpu.make_async_copy(mine.at[at], branch.at[at], put.at[b])
        copy.start()
        puts.append(copy)
    for copy in copies:
        copy.wait_send()
    for copy in puts:
        copy.wait()


def exchange_call(bp, ss, v):
    _, length, width = bp.shape
    blocks = length // BLOCK
    vmem = pl.BlockSpec(memory_space=pltpu.VMEM)
    anywhere = pl.BlockSpec(memory_space=pl.ANY)
    dma = pltpu.SemaphoreType.DMA
    return pl.pallas_call(
        exchange_kernel,
        out_shape=[jax.ShapeDtypeStruct((length, width), BF16), jax.ShapeDtypeStruct(ss.shape, F32)],
        in_specs=[anywhere, vmem, vmem],
        out_specs=[anywhere, vmem],
        scratch_shapes=[
            pltpu.VMEM((length, width), BF16), pltpu.VMEM((length, width), BF16),
            pltpu.VMEM(ss.shape, F32), pltpu.VMEM(ss.shape, F32),
            dma((1,)), dma((blocks,)), dma((blocks,)), dma((blocks,)), dma((2,)), dma((2,)),
        ],
        compiler_params=pltpu.CompilerParams(
            collective_id=2, has_side_effects=True, vmem_limit_bytes=30 * 1024 * 1024
        ),
        name="exchange",
    )(bp, ss, v)


def finish_kernel(
    n, planes, cuts, groups, length_ref, gn, tok, gain_ref, dwin, dwout, sums,
    back, w_ref, o_ref, sums_ref,
    gn_mine, gn_theirs, hidden, grad, dgain, w_own, w_in, o_own, o_in, w_give, w_pair, w_chip, z_in, oz_in, z_out,
    oz_out, w_all, o_all, s_own, s_in, d_in, s_tot, s_up,
    here, g_send, g_recv, b_send, b_recv, w_send, w_recv, o_send, o_recv, p_send, p_recv,
    z_send, z_recv, oz_send, oz_recv, y_send, y_recv, oy_send, oy_recv, s_send, s_recv, d_send, d_recv,
    u_send, u_recv,
):
    me = lax.axis_index("fsdp")
    level = lax.axis_index("rep")
    core = lax.rem(me, 2)
    chip = lax.div(me, 2)
    partner = 2 * chip + 1 - core
    span = back.shape[1]
    chip_rows = w_own.shape[0]
    rows = chip_rows // 2
    outs = o_own.shape[0]
    part, opart = rows // planes, outs // planes
    others = n // 2 - 1
    tile = 16
    barrier = pltpu.get_barrier_semaphore()
    for away, turn in peers_of(n):
        pl.semaphore_signal(barrier, inc=1, device_id={"fsdp": peer_at(n, me, away, turn)}, device_id_type=MESH)
    for up in range(1, planes):
        pl.semaphore_signal(barrier, inc=1, device_id={"rep": lax.rem(level + up, planes)}, device_id_type=MESH)
    pl.semaphore_wait(barrier, n - 1 + planes - 1)

    def remote(src, dst, send, recv, where):
        return pltpu.make_async_remote_copy(
            src_ref=src, dst_ref=dst, send_sem=send, recv_sem=recv, device_id=where, device_id_type=MESH
        )

    def arrived(block, send, recv):
        remote(block, block, send, recv, {"fsdp": partner}).wait_recv()

    pending = []

    def push(src, dst, send, recv, where):
        copy = remote(src, dst, send, recv, where)
        copy.start()
        pending.append(copy)

    def above(up):
        return lax.rem(level + up, planes)

    loads = [
        pltpu.make_async_copy(dwin.at[rows_at(chip, chip_rows)], w_own, here.at[0]),
        pltpu.make_async_copy(dwout.at[rows_at(chip, outs)], o_own, here.at[1]),
        pltpu.make_async_copy(gn.at[core], gn_mine, here.at[2]),
        pltpu.make_async_copy(tok.at[core], hidden, here.at[3]),
        pltpu.make_async_copy(sums.at[me], s_own, here.at[4]),
    ]
    for copy in loads:
        copy.start()
    everyone = [(0, 0)] + peers_of(n)
    for index, (away, turn) in enumerate(everyone):
        block = rows_at(peer_at(n, me, away, turn), span)
        push(gn.at[1 - core, block], gn_theirs.at[block], g_send.at[index], g_recv.at[index], {"fsdp": partner})
    for c, cols in enumerate(cuts):
        for i in range(others):
            target = {"fsdp": peer_at(n, me, i + 1, 0)}
            other = lax.rem(chip + i + 1, n // 2)
            k = c * others + i
            push(
                dwin.at[rows_at(other, chip_rows), cols], w_in.at[i, :, cols], w_send.at[k], w_recv.at[k], target
            )
    for i in range(others):
        target = {"fsdp": peer_at(n, me, i + 1, 0)}
        other = lax.rem(chip + i + 1, n // 2)
        push(dwout.at[rows_at(other, outs)], o_in.at[i], o_send.at[i], o_recv.at[i], target)
    for index, (away, turn) in enumerate(everyone):
        if index:
            peer = peer_at(n, me, away, turn)
            push(sums.at[peer], s_in.at[index - 1], s_send.at[index], s_recv.at[index], {"fsdp": peer})
    for copy in loads[2:]:
        copy.wait()
    dgain[...] = jnp.zeros_like(dgain)
    step = 64

    def norm_back(index):
        away, turn = everyone[index]
        target = peer_at(n, me, away, turn)
        block = rows_at(target, span)
        sender_index = everyone.index((away, 1 - turn))
        arrived(gn_theirs.at[block], g_send.at[sender_index], g_recv.at[sender_index])
        first = target * span

        @pl.loop(0, span // step)
        def _(i):
            at = pl.ds(pl.multiple_of(first + i * step, step), step)
            position = first + i * step + lax.broadcasted_iota(jnp.int32, (step, gn_mine.shape[1]), 0)
            total = gn_mine[at, :].astype(F32) + gn_theirs[at, :].astype(F32)
            total = jnp.where(position < length_ref[0], total, 0.0)
            h = hidden[at, :].astype(F32)
            inv = lax.rsqrt(jnp.mean(h * h, axis=1, keepdims=True) + EPS)
            normal = h * inv
            dgain[0:1, :] += jnp.sum(total * normal, axis=0, keepdims=True)
            scaled = total * gain_ref[0:1, :]
            mean = jnp.mean(scaled * normal, axis=1, keepdims=True)
            grad[at, :] = (inv * (scaled - normal * mean)).astype(BF16)

    for index in range(n):
        norm_back(index)
    seg = dgain.shape[1] // n
    for index, (away, turn) in enumerate(everyone):
        if index:
            peer = peer_at(n, me, away, turn)
            cols = pl.ds(pl.multiple_of(peer * seg, seg), seg)
            push(dgain.at[:, cols], d_in.at[index - 1], d_send.at[index], d_recv.at[index], {"fsdp": peer})

    own_block = pltpu.make_async_copy(grad.at[rows_at(me, span)], back.at[me], here.at[5])
    own_block.start()
    waiting = list(range(1, n))

    def give_back(count):
        for index in waiting[:count]:
            away, turn = everyone[index]
            peer = peer_at(n, me, away, turn)
            push(grad.at[rows_at(peer, span)], back.at[me], b_send.at[index], b_recv.at[index], {"fsdp": peer})
        del waiting[:count]

    def add_up(own, pieces, at, cols):
        total = own[at, cols].astype(F32)
        for i in range(pieces.shape[0]):
            total = total + pieces[i, at, cols].astype(F32)
        return total.astype(BF16)

    def stage_sum(c):
        cols = cuts[c]
        for i in range(others):
            k = c * others + i
            arrived(w_in.at[i, :, cols], w_send.at[k], w_recv.at[k])

        @pl.loop(0, rows // tile)
        def _(i):
            at = pl.ds(pl.multiple_of((1 - core) * rows + i * tile, tile), tile)
            w_give[pl.ds(pl.multiple_of(i * tile, tile), tile), cols] = add_up(w_own, w_in, at, cols)

        push(w_give.at[:, cols], w_pair.at[:, cols], p_send.at[c], p_recv.at[c], {"fsdp": partner})

        @pl.loop(0, rows // tile)
        def _(i):
            at = pl.ds(pl.multiple_of(core * rows + i * tile, tile), tile)
            w_chip[core, pl.ds(pl.multiple_of(i * tile, tile), tile), cols] = add_up(w_own, w_in, at, cols)

    def stage_up(c):
        cols = cuts[c]
        arrived(w_pair.at[:, cols], p_send.at[c], p_recv.at[c])
        w_chip[1 - core, :, cols] = w_pair[:, cols]
        for up in range(1, planes):
            k = c * (planes - 1) + up - 1
            push(
                w_chip.at[:, rows_at(above(up), part), cols], z_in.at[up - 1, :, :, cols],
                z_send.at[k], z_recv.at[k], {"rep": above(up)},
            )

    def stage_total(c):
        cols = cuts[c]
        for up in range(1, planes):
            k = c * (planes - 1) + up - 1
            arrived(z_in.at[up - 1, :, :, cols], z_send.at[k], z_recv.at[k])
        at = rows_at(level, part)
        for q in range(2):
            total = w_chip[q, at, cols].astype(F32)
            for k in range(planes - 1):
                total = total + z_in[k, q, :, cols].astype(F32)
            z_out[q, :, cols] = total.astype(BF16)
            w_all[q, at, cols] = total.astype(BF16)
        for up in range(1, planes):
            k = c * (planes - 1) + up - 1
            push(z_out.at[:, :, cols], w_all.at[:, at, cols], y_send.at[k], y_recv.at[k], {"rep": above(up)})

    for copy in loads[:2]:
        copy.wait()
    count = len(cuts)
    for c in range(count + 2):
        if c < count:
            stage_sum(c)
            give_back(2)
        if c == count:
            give_back(n)
            for i in range(others):
                arrived(o_in.at[i], o_send.at[i], o_recv.at[i])

            @pl.loop(0, outs // tile)
            def _(i):
                at = pl.ds(pl.multiple_of(i * tile, tile), tile)
                o_own[at, :] = add_up(o_own, o_in, at, slice(None))

            for up in range(1, planes):
                push(
                    o_own.at[rows_at(above(up), opart)], oz_in.at[up - 1], oz_send.at[up - 1], oz_recv.at[up - 1],
                    {"rep": above(up)},
                )
        if 1 <= c <= count:
            stage_up(c - 1)
        if c >= 2:
            stage_total(c - 2)

    total = s_own[...]
    for index, (away, turn) in enumerate(everyone):
        if index:
            arrived(s_in.at[index - 1], s_send.at[index], s_recv.at[index])
            arrived(d_in.at[index - 1], d_send.at[index], d_recv.at[index])
            total = total + s_in[index - 1]
    heads = s_own.shape[0]
    s_tot[0:heads, :] = total
    mine = dgain[:, pl.ds(pl.multiple_of(me * seg, seg), seg)]
    for index in range(n - 1):
        mine = mine + d_in[index]
    s_tot[heads : heads + 8, :] = mine
    for up in range(1, planes):
        push(s_tot, s_up.at[up - 1], u_send.at[up - 1], u_recv.at[up - 1], {"rep": above(up)})
    for i in range(planes - 1):
        arrived(oz_in.at[i], oz_send.at[i], oz_recv.at[i])
    at = rows_at(level, opart)
    total = o_own[at, :].astype(F32)
    for k in range(planes - 1):
        total = total + oz_in[k].astype(F32)
    oz_out[...] = total.astype(BF16)
    o_all[at, :] = total.astype(BF16)
    for up in range(1, planes):
        push(oz_out, o_all.at[at], oy_send.at[up - 1], oy_recv.at[up - 1], {"rep": above(up)})
    for i in range(planes - 1):
        arrived(s_up.at[i], u_send.at[i], u_recv.at[i])
    total = s_tot[...]
    for k in range(planes - 1):
        total = total + s_up[k]
    sums_ref[...] = total
    for c, cols in enumerate(cuts):
        for up in range(1, planes):
            below = lax.rem(level + planes - up, planes)
            k = c * (planes - 1) + up - 1
            arrived(w_all.at[:, rows_at(below, part), cols], y_send.at[k], y_recv.at[k])
    inner, group, heads = groups
    for g in range(2 * inner // group):
        q, at = g % 2, g // 2 * group
        w_ref[:, g * group : (g + 1) * group] = w_all[q, :, at : at + group].astype(F32)
        w_ref[:, 2 * inner + g * group : 2 * inner + (g + 1) * group] = (
            w_all[q, :, inner + at : inner + at + group].astype(F32)
        )
    both = w_all[0, :, 2 * inner : 2 * inner + 2 * STATE].astype(F32)
    both = both + w_all[1, :, 2 * inner : 2 * inner + 2 * STATE].astype(F32)
    w_ref[:, 4 * inner : 4 * inner + 2 * STATE] = both
    first = 2 * inner + 2 * STATE
    tails = [w_all[q, :, first : first + LANES].astype(F32) for q in range(2)]
    size = group // HEADDIM
    pieces = [tails[g % 2][:, g // 2 * size : (g // 2 + 1) * size] for g in range(2 * inner // group)]
    w_ref[:, 4 * inner + 2 * STATE :] = jnp.concatenate(pieces, axis=1)
    for up in range(1, planes):
        below = lax.rem(level + planes - up, planes)
        arrived(o_all.at[rows_at(below, opart)], oy_send.at[up - 1], oy_recv.at[up - 1])
    o_ref[...] = o_all[...].astype(F32)
    for index, (away, turn) in enumerate(everyone):
        if index:
            owner = sender_at(n, me, away, turn)
            arrived(back.at[owner], b_send.at[index], b_recv.at[index])
    for copy in pending:
        copy.wait_send()
    own_block.wait()


def finish_call(n, planes, group, length, gn, tok, gain, dwin, dwout, sums):
    _, total, width = gn.shape
    span = total // n
    wide = dwin.shape[1]
    inner = dwout.shape[0]
    heads = inner // HEADDIM
    chip_rows, outs = dwin.shape[0] // (n // 2), inner // (n // 2)
    rows = chip_rows // 2
    others = n // 2 - 1
    lane_tiles = wide // LANES
    pieces = 4
    bounds = [(lane_tiles * i + pieces - 1) // pieces * LANES for i in range(pieces + 1)]
    cuts = [pl.ds(bounds[i], bounds[i + 1] - bounds[i]) for i in range(pieces)]
    anywhere = pl.BlockSpec(memory_space=pl.ANY)
    vmem = pl.BlockSpec(memory_space=pltpu.VMEM)
    dma = pltpu.SemaphoreType.DMA
    up = planes - 1
    held = sums.shape[1]
    return pl.pallas_call(
        functools.partial(finish_kernel, n, planes, cuts, (inner, group, heads)),
        out_shape=[
            jax.ShapeDtypeStruct((n, span, width), BF16),
            jax.ShapeDtypeStruct((rows, 4 * inner + 2 * STATE + 2 * heads), F32),
            jax.ShapeDtypeStruct((outs, width), F32),
            jax.ShapeDtypeStruct((held + 8, LANES), F32),
        ],
        in_specs=[pl.BlockSpec(memory_space=pltpu.SMEM), anywhere, anywhere, vmem, anywhere, anywhere, anywhere],
        out_specs=[anywhere, vmem, vmem, vmem],
        scratch_shapes=[
            pltpu.VMEM((total, width), BF16), pltpu.VMEM((total, width), BF16), pltpu.VMEM((total, width), BF16),
            pltpu.VMEM((total, width), BF16), pltpu.VMEM((8, width), F32),
            pltpu.VMEM((chip_rows, wide), BF16), pltpu.VMEM((others, chip_rows, wide), BF16),
            pltpu.VMEM((outs, width), BF16), pltpu.VMEM((others, outs, width), BF16),
            pltpu.VMEM((rows, wide), BF16), pltpu.VMEM((rows, wide), BF16), pltpu.VMEM((2, rows, wide), BF16),
            pltpu.VMEM((up, 2, rows // planes, wide), BF16), pltpu.VMEM((up, outs // planes, width), BF16),
            pltpu.VMEM((2, rows // planes, wide), BF16), pltpu.VMEM((outs // planes, width), BF16),
            pltpu.VMEM((2, rows, wide), BF16), pltpu.VMEM((outs, width), BF16),
            pltpu.VMEM((held, LANES), F32), pltpu.VMEM((n - 1, held, LANES), F32),
            pltpu.VMEM((n - 1, 8, LANES), F32), pltpu.VMEM((held + 8, LANES), F32),
            pltpu.VMEM((up, held + 8, LANES), F32),
            dma((6,)), dma((n,)), dma((n,)), dma((n,)), dma((n,)),
            dma((pieces * others,)), dma((pieces * others,)), dma((others,)), dma((others,)),
            dma((pieces,)), dma((pieces,)), dma((pieces * up,)), dma((pieces * up,)), dma((up,)), dma((up,)),
            dma((pieces * up,)), dma((pieces * up,)), dma((up,)), dma((up,)),
            dma((n,)), dma((n,)), dma((n,)), dma((n,)), dma((up,)), dma((up,)),
        ],
        compiler_params=pltpu.CompilerParams(
            collective_id=1, has_side_effects=True, vmem_limit_bytes=60 * 1024 * 1024
        ),
        name="finish",
    )(length, gn, tok, gain, dwin, dwout, sums)


def pairs_of(n):
    return [[2 * c, 2 * c + 1] for c in range(n // 2)]


def columns_of(n):
    return [list(range(q, n, 2)) for q in range(2)]


def halves(array, axis, group):
    shape = array.shape
    view = array.reshape(shape[:axis] + (shape[axis] // (2 * group), 2, group) + shape[axis + 1 :])
    out = []
    for q in range(2):
        part = lax.index_in_dim(view, q, axis + 1, keepdims=False)
        out.append(part.reshape(shape[:axis] + (shape[axis] // 2,) + shape[axis + 1 :]))
    return out


def interleave(first, second, axis, group):
    shape = first.shape
    views = [
        part.reshape(shape[:axis] + (shape[axis] // group, 1, group) + shape[axis + 1 :]) for part in (first, second)
    ]
    return jnp.concatenate(views, axis=axis + 1).reshape(shape[:axis] + (2 * shape[axis],) + shape[axis + 1 :])


def body(
    tokens, cotangent, lengths, dealing, norm_gain, in_weight, conv_weight, conv_bias, dt_bias, a_log, skip_gain,
    out_gain, out_weight,
):
    n = lax.axis_size("fsdp")
    me = lax.axis_index("fsdp")
    core = lax.rem(me, 2)
    pairs, columns = pairs_of(n), columns_of(n)
    local_tokens, local_grad = tokens[0], cotangent[0]
    count, span, width = local_tokens.shape
    length = span * n
    inner = INNER // 2
    heads = HEADS // 2
    group = max(HEADDIM, INNER // n)
    blocks = length // BLOCK
    rows = in_weight.shape[0]

    slots = jnp.arange(count, dtype=jnp.int32)
    own = jnp.sum(jnp.where(dealing[0][:, None] == slots[None, :], lengths[0][None, :], 0), axis=1)
    ahead = (own[None, :] > own[:, None]) | ((own[None, :] == own[:, None]) & (slots[None, :] < slots[:, None]))
    rank = jnp.sum(ahead.astype(jnp.int32), axis=1)
    place = jnp.where(rank < count // 2, 2 * rank, 2 * (count - 1 - rank) + 1)
    source = jnp.sum(jnp.where(place[None, :] == slots[:, None], slots[None, :], 0), axis=1)
    placed = jnp.sum(jnp.where(place[None, :] == slots[:, None], own[None, :], 0), axis=1)
    chip_lens = lax.dynamic_slice_in_dim(placed, me - core, 2)
    chip_blocks = (chip_lens + BLOCK - 1) // BLOCK

    main = INNER + INNER + 2 * STATE
    gates = halves(in_weight[:, :INNER], 1, group)
    vals = halves(in_weight[:, INNER : 2 * INNER], 1, group)
    both = in_weight[:, 2 * INNER : main]
    steps = halves(in_weight[:, main:], 1, group // HEADDIM)
    pad = jnp.zeros((rows, LANES - heads), BF16)
    shards = jnp.stack([jnp.concatenate([gates[q], vals[q], both, steps[q], pad], axis=1) for q in range(2)])
    aligned = INNER // n >= HEADDIM
    small = jnp.concatenate([norm_gain, conv_weight.reshape(-1), conv_bias, out_gain])
    room = -(-small.shape[0] // (16 * LANES)) * 16
    small = jnp.pad(small, (0, room * LANES - small.shape[0])).reshape(room, LANES)
    sent_grad = jnp.take(local_grad, source, axis=0)
    tok, win, smalls = start_call(n, jnp.take(local_tokens, source, axis=0), shards, small)
    tok, sent_grad, out_weight = lax.optimization_barrier((tok, sent_grad, out_weight))
    smalls = smalls.reshape(n, -1).astype(F32)
    own_grad = lax.all_to_all(sent_grad, "fsdp", split_axis=0, concat_axis=0, tiled=True)
    cot = lax.all_gather(own_grad.reshape(1, length, width), "fsdp", axis=0, tiled=True, axis_index_groups=pairs)
    if aligned:
        wout = lax.all_gather(out_weight, "fsdp", axis=0, tiled=True, axis_index_groups=columns)
    else:
        whole = lax.all_gather(out_weight, "fsdp", axis=0, tiled=True)
        wout = lax.dynamic_index_in_dim(jnp.stack(halves(whole, 0, group)), core, 0, keepdims=False)
    cuts = [norm_gain.shape[0], conv_weight.size, conv_bias.shape[0], out_gain.shape[0]]
    ends = [sum(cuts[: i + 1]) for i in range(4)]
    first_gain = smalls[:, : ends[0]].reshape(-1)
    conv_w = smalls[:, ends[0] : ends[1]].reshape(n, CONV, -1).transpose(1, 0, 2).reshape(CONV, -1)
    conv_b = smalls[:, ends[1] : ends[2]].reshape(1, -1)
    gated_gain = smalls[:, ends[2] : ends[3]].reshape(1, -1)

    def half_of(array, axis, size):
        return lax.dynamic_index_in_dim(jnp.stack(halves(array, axis, size)), core, 0, keepdims=False)

    conv_all = jnp.concatenate([conv_w, conv_b, jnp.zeros((3, conv_w.shape[1]), F32)], axis=0)
    conv_all = jnp.concatenate([half_of(conv_all[:, :INNER], 1, group), conv_all[:, INNER:]], axis=1)
    head_rows = jnp.stack([dt_bias, jnp.exp(a_log), skip_gain] + [jnp.zeros_like(dt_bias)] * 5)
    head_rows = half_of(head_rows, 1, group // HEADDIM)
    dwide = jnp.broadcast_to(jnp.repeat(head_rows[2:3], HEADDIM, axis=1), (8, inner))
    hp = jnp.concatenate([head_rows, jnp.zeros((8, LANES - heads), F32)], axis=1)
    og = jnp.broadcast_to(half_of(gated_gain, 1, group), (8, inner))
    gain = jnp.broadcast_to(first_gain[None, :], (8, width))
    cb = jnp.broadcast_to(conv_all[CONV : CONV + 1], conv_all.shape)
    expand, collect = matrices(inner)
    args = (gain, win, conv_all, cb, hp, dwide, og, expand)
    gate, cin, raw, y, states, ss, mixing = fwd_call(chip_blocks, tok, *args)

    gm, v, bp = mid_call(chip_blocks, chip_lens, cot, mixing, wout)
    branch, rv = exchange_call(bp, ss, v)

    def restore(part):
        return lax.all_to_all(part.reshape(n, span, width), "fsdp", split_axis=0, concat_axis=0, tiled=True)

    kept = jnp.clip(own - me * span, 0, span)
    output = combine_call(place, kept, local_tokens, restore(branch))[None]
    gn, dwin, dwout, dcw, dhp, dog, ddw = bwd_call(
        chip_blocks, chip_lens, tok, cot, gain, win, gm, *args[2:], collect, gate, cin, raw, y, states, rv
    )
    def widen(half, axis, size):
        zero = jnp.zeros_like(half)
        return interleave(jnp.where(core == 0, half, zero), jnp.where(core == 1, half, zero), axis, size)

    own_len = lax.dynamic_slice_in_dim(chip_lens, core, 1)
    dconv = jnp.concatenate([widen(dcw[: CONV + 1, :inner], 1, group), dcw[: CONV + 1, inner:]], axis=1)
    dskip = jnp.sum(ddw[0].reshape(heads, HEADDIM), axis=1)
    dheads = widen(jnp.concatenate([dhp[:2, :heads], dskip[None]], axis=0), 1, group // HEADDIM)
    dog = widen(dog[0], 0, group)
    planes = lax.axis_size("rep")
    if aligned and rows % (16 * planes) == 0 and out_weight.shape[0] % (16 * planes) == 0:
        sums = jnp.concatenate(
            [
                dconv.reshape(CONV + 1, n, -1).transpose(1, 0, 2).reshape(n, -1),
                dog.reshape(n, -1),
                jnp.broadcast_to(dheads.reshape(1, -1), (n, dheads.size)),
            ],
            axis=1,
        )
        room = -(-sums.shape[1] // (8 * LANES)) * 8
        sums = jnp.pad(sums, ((0, 0), (0, room * LANES - sums.shape[1]))).reshape(n, room, LANES)
        back, dwin, dwout, sums = finish_call(n, planes, group, own_len, gn, tok, gain, dwin, dwout, sums)
        flat = sums.reshape(-1)
        c0 = dconv.size // n
        c1 = c0 + dog.size // n
        dheads = flat[c1 : c1 + dheads.size].reshape(dheads.shape)
        dog, dgain = flat[c0:c1], sums[room, : width // n]
        dconv = flat[:c0].reshape(CONV + 1, -1)
    else:
        other = lax.dynamic_index_in_dim(gn, 1 - core, 0, keepdims=False)
        other = lax.ppermute(other, "fsdp", [(2 * c + q, 2 * c + 1 - q) for c in range(n // 2) for q in range(2)])
        mine = lax.dynamic_index_in_dim(gn, core, 0, keepdims=False)
        hidden = lax.dynamic_index_in_dim(tok, core, 0, keepdims=False).astype(F32)
        inv = lax.rsqrt(jnp.mean(hidden * hidden, axis=-1, keepdims=True) + EPS)
        position = jnp.arange(length, dtype=jnp.int32)[:, None]
        grad_normed = jnp.where(position < own_len[0], mine.astype(F32) + other.astype(F32), 0.0)
        dgain = jnp.sum(grad_normed * hidden * inv, axis=0)
        scaled = grad_normed * first_gain[None, :]
        grad_hidden = inv * scaled - hidden * (inv * inv * inv) * jnp.mean(scaled * hidden, axis=-1, keepdims=True)
        back = restore(grad_hidden.astype(BF16))
        dwin = lax.psum_scatter(
            dwin.astype(F32), "fsdp", scatter_dimension=0, tiled=True, axis_index_groups=columns
        )
        dwin = lax.psum(dwin, "rep").reshape(2, rows, -1)
        dwin = lax.all_to_all(dwin, "fsdp", split_axis=0, concat_axis=0, tiled=True, axis_index_groups=pairs)
        if aligned:
            dwout = lax.psum_scatter(
                dwout.astype(F32), "fsdp", scatter_dimension=0, tiled=True, axis_index_groups=columns
            )
        else:
            wide_grad = widen(dwout.astype(F32), 0, group)
            dwout = lax.psum_scatter(wide_grad, "fsdp", scatter_dimension=0, tiled=True)
        dwout = lax.psum(dwout, "rep")
        c0, c1, c2 = inner, 2 * inner, 2 * inner + 2 * STATE
        dwin = jnp.concatenate(
            [
                interleave(dwin[0, :, :c0], dwin[1, :, :c0], 1, group),
                interleave(dwin[0, :, c0:c1], dwin[1, :, c0:c1], 1, group),
                dwin[0, :, c1:c2] + dwin[1, :, c1:c2],
                interleave(dwin[0, :, c2 : c2 + heads], dwin[1, :, c2 : c2 + heads], 1, group // HEADDIM),
            ],
            axis=1,
        )
        dconv, dheads, dog, dgain = lax.psum((dconv, dheads, dog, dgain), ("rep", "fsdp"))

        def shard(array):
            size = array.shape[-1] // n
            return lax.dynamic_slice_in_dim(array, me * size, size, axis=array.ndim - 1)

        dconv, dog, dgain = shard(dconv), shard(dog), shard(dgain)
    token_grad = combine_call(place, kept, local_grad, back)[None]
    return (
        output, token_grad, dgain, dwin, dconv[:CONV], dconv[CONV], dheads[0], dheads[1], dheads[2], dog, dwout,
    )


def solution(mesh):
    row = P("rep", None, "fsdp", None)
    per = P("rep", None)
    in_specs = (
        row, row, per, per, P("fsdp"), P("fsdp", None), P(None, "fsdp"), P("fsdp"), P(), P(), P(), P("fsdp"),
        P("fsdp", None),
    )
    out_specs = (
        row, row, P("fsdp"), P("fsdp", None), P(None, "fsdp"), P("fsdp"), P(), P(), P(), P("fsdp"), P("fsdp", None),
    )
    return jax.shard_map(body, mesh=mesh, in_specs=in_specs, out_specs=out_specs, check_vma=False)
```

```python
import functools
import jax
import jax.numpy as jnp
from jax import lax
from jax.experimental import pallas as pl
from jax.experimental.pallas import tpu as pltpu
from jax.sharding import PartitionSpec as P

STATE = 128
HEADDIM = 64
HEADS = 32
INNER = 2048
CONV = 4
BLOCK = 256
CHUNK = 128
LANES = 128
MESH = pl.DeviceIdType.MESH
EPS = 1e-05
F32 = jnp.float32
BF16 = jnp.bfloat16
FAR = -1e9
TILE = 32
NT = (((1,), (1,)), ((), ()))
TN = (((0,), (0,)), ((), ()))


def mm(a, b, dims=(((1,), (0,)), ((), ()))):
    return lax.dot_general(a, b, dims, preferred_element_type=F32)


def two_parts(v):
    high = v.astype(BF16)
    return high, (v - high.astype(F32)).astype(BF16)


def spread(v, expand):
    high, low = two_parts(v)
    return mm(jnp.concatenate([high, low], axis=1), expand)


def gather_heads(v, collect):
    high, low = two_parts(v)
    return mm(high, collect) + mm(low, collect)


def sigmoid(v):
    return 0.5 + 0.5 * jnp.tanh(0.5 * v)


def mm_state(rows, state):
    return mm(jnp.concatenate([rows, rows], axis=1), jnp.concatenate(two_parts(state), axis=0))


def softplus(v):
    return jnp.maximum(v, 0.0) + jnp.log1p(jnp.exp(-jnp.abs(v)))


def three_parts(v):
    high = v.astype(BF16)
    rest = v - high.astype(F32)
    middle = rest.astype(BF16)
    return jnp.concatenate([high, middle, (rest - middle.astype(F32)).astype(BF16)], axis=0)


def triangle(backward):
    rows = lax.broadcasted_iota(jnp.int32, (BLOCK, BLOCK), 0)
    cols = lax.broadcasted_iota(jnp.int32, (BLOCK, BLOCK), 1)
    keep = (cols >= rows) if backward else (rows >= cols)
    tri = (keep & (rows // CHUNK == cols // CHUNK)).astype(F32).astype(BF16)
    return jnp.concatenate([tri, tri, tri], axis=1)


def chunk_rows(c):
    return slice(c * CHUNK, (c + 1) * CHUNK)


def each_last(cum):
    return jnp.concatenate(
        [
            jnp.broadcast_to(cum[(c + 1) * CHUNK - 1 : (c + 1) * CHUNK], (CHUNK, cum.shape[1]))
            for c in range(BLOCK // CHUNK)
        ],
        axis=0,
    )


def causal_sum(log_decay):
    return mm(triangle(False), three_parts(log_decay))


def reverse_sum(v):
    return mm(triangle(True), three_parts(v))


def convolve(cbuf, cw_ref, cb_ref, cols):
    total = cb_ref[0:1, cols] + cw_ref[3:4, cols] * cbuf[8 : 8 + BLOCK, cols]
    for k in range(CONV - 1):
        total = total + cw_ref[k : k + 1, cols] * cbuf[5 + k : 5 + k + BLOCK, cols]
    return total


def where_at(i, nb):
    i = jnp.minimum(i, nb[0] + nb[1] - 1)
    seq = (i >= nb[0]).astype(jnp.int32)
    return seq, i - seq * nb[0]


def most_blocks(count, length):
    blocks, best = length // BLOCK, 0
    for r in range(count // 2):
        for a in range(1, blocks + 1):
            for b in range(1, a + 1):
                upper, lower = (a - 1) * BLOCK + 1, (b - 1) * BLOCK + 1
                if length + r * upper + (count - 1 - 2 * r) * lower + r <= count // 2 * length and (r or a == blocks):
                    best = max(best, a + b)
    return best


def normalize(tok_ref, gain_ref):
    hidden = tok_ref[0].astype(F32)
    scale = lax.rsqrt(jnp.mean(hidden * hidden, axis=1, keepdims=True) + EPS)
    return (hidden * scale * gain_ref[0:1, :]).astype(BF16)


def fwd_kernel(
    inner, heads,
    nb_ref, tok_ref, gain_ref, win_ref, cw_ref, cb_ref, hp_ref, dwide_ref, og_ref,
    gate_ref, cin_ref, raw_ref, y_ref, s_ref, ss_ref, sc_ref,
    cbuf, xbuf, state, expand_ref,
):
    step_id = pl.program_id(0)
    _, blk = where_at(step_id, nb_ref)
    chan = inner + 2 * STATE

    @pl.when(step_id == 0)
    def _():
        fill_expand(expand_ref)

    @pl.when(step_id < nb_ref[0] + nb_ref[1])
    def _():
        @pl.when(blk == 0)
        def _():
            cbuf[0:8, :] = jnp.zeros((8, chan), F32)
            state[...] = jnp.zeros_like(state)

        @pl.when(blk > 0)
        def _():
            cbuf[0:8, :] = cbuf[BLOCK : BLOCK + 8, :]

        normed = normalize(tok_ref, gain_ref)
        for j in range(0, inner, 256):
            gate_ref[0, :, j : j + 256] = mm(normed, win_ref[:, j : j + 256])
        for j in range(0, chan, 256):
            part = mm(normed, win_ref[:, inner + j : inner + j + 256])
            cin_ref[0, :, j : j + 256] = part
            cbuf[8 : 8 + BLOCK, j : j + 256] = part
        raw = mm(normed, win_ref[:, inner + chan :])
        raw_ref[0] = raw
        for j in range(0, chan, 256):
            u = convolve(cbuf, cw_ref, cb_ref, slice(j, j + 256))
            xbuf[:, j : j + 256] = u * sigmoid(u)
        step = softplus(raw + hp_ref[0:1, :])
        log_decay = -step * hp_ref[1:2, :]
        rows = lax.broadcasted_iota(jnp.int32, (CHUNK, CHUNK), 0)
        cols = lax.broadcasted_iota(jnp.int32, (CHUNK, CHUNK), 1)
        causal = rows >= cols
        left = cols < HEADDIM
        cum = causal_sum(log_decay)
        cum_t = cum.T
        three = jnp.concatenate([jnp.exp(cum), step, jnp.exp(each_last(cum) - cum) * step], axis=0)
        wide = spread(three, expand_ref[...])
        e_wide, dt_wide, w_wide = wide[:BLOCK], wide[BLOCK : 2 * BLOCK], wide[2 * BLOCK :]
        all_in = xbuf[:, inner : inner + STATE].astype(BF16)
        all_out = xbuf[:, inner + STATE :].astype(BF16)
        x = xbuf[:, :inner]
        xd = (x * dt_wide).astype(BF16)
        xw = (x * w_wide).astype(BF16)
        crosses = []
        for c in range(BLOCK // CHUNK):
            at = chunk_rows(c)
            crosses.append(mm(all_out[at], all_in[at], NT))
        for p in range(heads // 2):
            lanes = slice(p * 128, (p + 1) * 128)
            for c in range(BLOCK // CHUNK):
                at = chunk_rows(c)
                pair = xd[at, lanes]
                zero = jnp.zeros_like(pair)
                both = jnp.concatenate([jnp.where(left, pair, zero), jnp.where(left, zero, pair)], axis=0)
                parts = []
                for h in (2 * p, 2 * p + 1):
                    gap = cum[at, h : h + 1] - cum_t[h : h + 1, at]
                    parts.append((crosses[c] * jnp.exp(jnp.where(causal, gap, FAR))).astype(BF16))
                y_ref[0, at, lanes] = mm(jnp.concatenate(parts, axis=1), both)
        for c in range(BLOCK // CHUNK):
            at = chunk_rows(c)
            held = state[...]
            s_ref[0, c] = held
            y_ref[0, at, :] += e_wide[at] * mm_state(all_out[at], held)
            last = e_wide[(c + 1) * CHUNK - 1 : (c + 1) * CHUNK]
            state[...] = last * held + mm(all_in[at], xw[at], TN)
        total = jnp.zeros((BLOCK, 1), F32)
        for j in range(0, inner, 256):
            at = slice(j, j + 256)
            gate = gate_ref[0, :, at]
            summed = y_ref[0, :, at] + dwide_ref[0:1, at] * xbuf[:, at]
            y_ref[0, :, at] = summed
            gated = summed * (gate * sigmoid(gate))
            total = total + jnp.sum(gated * gated, axis=1, keepdims=True)
            sc_ref[0, :, at] = (gated * og_ref[0:1, at]).astype(BF16)
        ss_ref[...] = jnp.broadcast_to(total, (BLOCK, 8)).T


def fixed(shape):
    return pl.BlockSpec(shape, lambda *_: (0,) * len(shape), pipeline_mode=pl.Buffered(1))


def fwd_call(steps, nb, tok, gain, win, cw, cb, hp, dwide, og):
    nseq, length, width = tok.shape
    inner = dwide.shape[1]
    heads = inner // HEADDIM
    chan = inner + 2 * STATE
    blocks = length // BLOCK

    def rows(i, nb):
        seq, blk = where_at(i, nb)
        return (seq, blk, 0)

    def srows(i, nb):
        seq, blk = where_at(i, nb)
        return (seq, blk, 0, 0)

    def ssrows(i, nb):
        seq, blk = where_at(i, nb)
        return (seq * blocks + blk, 0)

    grid_spec = pltpu.PrefetchScalarGridSpec(
        num_scalar_prefetch=1,
        grid=(steps,),
        in_specs=[
            pl.BlockSpec((1, BLOCK, width), rows),
            fixed(gain.shape), fixed(win.shape), fixed(cw.shape), fixed(cb.shape),
            fixed(hp.shape), fixed(dwide.shape), fixed(og.shape),
        ],
        out_specs=[
            pl.BlockSpec((1, BLOCK, inner), rows),
            pl.BlockSpec((1, BLOCK, chan), rows),
            pl.BlockSpec((1, BLOCK, LANES), rows),
            pl.BlockSpec((1, BLOCK, inner), rows),
            pl.BlockSpec((1, BLOCK // CHUNK, STATE, inner), srows),
            pl.BlockSpec((8, BLOCK), ssrows),
            pl.BlockSpec((1, BLOCK, inner), rows),
        ],
        scratch_shapes=[
            pltpu.VMEM((BLOCK + 8, chan), F32),
            pltpu.VMEM((BLOCK, chan), F32),
            pltpu.VMEM((STATE, inner), F32),
            pltpu.VMEM((2 * LANES, inner), BF16),
        ],
    )
    shapes = [
        jax.ShapeDtypeStruct((nseq, length, inner), F32),
        jax.ShapeDtypeStruct((nseq, length, chan), F32),
        jax.ShapeDtypeStruct((nseq, length, LANES), F32),
        jax.ShapeDtypeStruct((nseq, length, inner), F32),
        jax.ShapeDtypeStruct((nseq, length // CHUNK, STATE, inner), F32),
        jax.ShapeDtypeStruct((nseq * blocks * 8, BLOCK), F32),
        jax.ShapeDtypeStruct((nseq, length, inner), BF16),
    ]
    return pl.pallas_call(
        functools.partial(fwd_kernel, inner, heads),
        grid_spec=grid_spec,
        out_shape=shapes,
        compiler_params=pltpu.CompilerParams(
            dimension_semantics=("arbitrary",), vmem_limit_bytes=60 * 1024 * 1024
        ),
        cost_estimate=pl.CostEstimate(
            flops=nseq * length * width * (3 * inner + 400), bytes_accessed=60 << 20, transcendentals=0
        ),
        name="layer_forward",
    )(nb, tok, gain, win, cw, cb, hp, dwide, og)


def mid_kernel(nb_ref, len_ref, cot_ref, sc_ref, wout_ref, gm_ref, v_ref, bp_ref):
    seq, blk = where_at(pl.program_id(0), nb_ref)

    @pl.when(pl.program_id(0) < nb_ref[0] + nb_ref[1])
    def _():
        cot = cot_ref[0]
        position = blk * BLOCK + lax.broadcasted_iota(jnp.int32, cot.shape, 0)
        gb = jnp.where(position < len_ref[seq], cot, jnp.zeros_like(cot))
        total = jnp.zeros((BLOCK, 1), F32)
        for j in range(0, sc_ref.shape[2], 256):
            at = slice(j, j + 256)
            gm = mm(gb, wout_ref[at, :], NT)
            gm_ref[0, :, at] = gm
            total = total + jnp.sum(gm * sc_ref[0, :, at].astype(F32), axis=1, keepdims=True)
        v_ref[...] = jnp.broadcast_to(total, (BLOCK, 8)).T
        scaled = sc_ref[0]
        for j in range(0, cot.shape[1], 256):
            bp_ref[0, :, j : j + 256] = mm(scaled, wout_ref[:, j : j + 256]).astype(BF16)


def mid_call(steps, nb, lens, cot, scaled, wout):
    nseq, length, width = cot.shape
    inner = wout.shape[0]
    blocks = length // BLOCK

    def rows(i, nb, lens):
        seq, blk = where_at(i, nb)
        return (seq, blk, 0)

    def vrows(i, nb, lens):
        seq, blk = where_at(i, nb)
        return (seq * blocks + blk, 0)

    return pl.pallas_call(
        mid_kernel,
        grid_spec=pltpu.PrefetchScalarGridSpec(
            num_scalar_prefetch=2,
            grid=(steps,),
            in_specs=[pl.BlockSpec((1, BLOCK, width), rows), pl.BlockSpec((1, BLOCK, inner), rows), fixed(wout.shape)],
            out_specs=[
                pl.BlockSpec((1, BLOCK, inner), rows), pl.BlockSpec((8, BLOCK), vrows),
                pl.BlockSpec((1, BLOCK, width), rows),
            ],
        ),
        out_shape=[
            jax.ShapeDtypeStruct((nseq, length, inner), F32),
            jax.ShapeDtypeStruct((nseq * blocks * 8, BLOCK), F32),
            jax.ShapeDtypeStruct((nseq, length, width), BF16),
        ],
        compiler_params=pltpu.CompilerParams(
            dimension_semantics=("arbitrary",), vmem_limit_bytes=60 * 1024 * 1024
        ),
        cost_estimate=pl.CostEstimate(flops=10**10, bytes_accessed=30 << 20, transcendentals=0),
        name="layer_middle",
    )(nb, lens, cot, scaled, wout)


def gate_kernel(
    parts,
    nb_ref, len_ref, chip_ref, tok_ref, cot_ref, gain_ref, wgate_ref, gm_ref, og_ref, gate_ref, y_ref, rv_ref,
    dy_ref, gp_ref, dog_ref, *refs,
):
    wgate_out, wout_out = refs[:parts], refs[parts : 2 * parts]
    normed_t, dgate_buf, mixed_buf, dwgate, dwout = refs[2 * parts :]
    step_id = pl.program_id(0)
    seq, blk = where_at(step_id, nb_ref)
    inner = gm_ref.shape[2]
    width = tok_ref.shape[2]

    @pl.when(step_id == 0)
    def _():
        dwgate[...] = jnp.zeros_like(dwgate)
        dwout[...] = jnp.zeros_like(dwout)
        dog_ref[...] = jnp.zeros_like(dog_ref)

    @pl.when(step_id < nb_ref[0] + nb_ref[1])
    def _():
        position = blk * BLOCK + lax.broadcasted_iota(jnp.int32, (BLOCK, width), 0)
        cot = cot_ref[0]
        gb = jnp.where(position < len_ref[seq], cot, jnp.zeros_like(cot))
        rv = rv_ref[...].T
        scale, coef = rv[:, 0:1], rv[:, 1:2]
        normed_t[...] = normalize(tok_ref, gain_ref).T
        for j in range(0, inner, 256):
            at = slice(j, j + 256)
            gain = og_ref[0:1, at]
            total = jnp.zeros((8, 256), F32)
            for r in range(0, BLOCK, TILE):
                row = slice(r, r + TILE)
                gm = gm_ref[0, row, at]
                gate = gate_ref[0, row, at]
                sig = sigmoid(gate)
                ysum = y_ref[0, row, at]
                silu = gate * sig
                gated = ysum * silu
                normal = gated * scale[row]
                mixed_buf[row, at] = (normal * gain).astype(BF16)
                product = gm * normal
                for k in range(0, TILE, 8):
                    total = total + product[k : k + 8]
                dgated = scale[row] * (gm * gain) - gated * coef[row]
                dgate_buf[row, at] = (dgated * ysum * (sig + silu * (1.0 - sig))).astype(BF16)
                dy_ref[0, row, at] = dgated * silu
            dog_ref[0:1, at] += jnp.sum(total, axis=0, keepdims=True)
            dwout[at, :] += mm(mixed_buf[:, at], gb, TN)
            dwgate[:, at] += mm(normed_t[...], dgate_buf[:, at])
        for j in range(0, width, 256):
            gp_ref[0, :, j : j + 256] = mm(dgate_buf[...], wgate_ref[j : j + 256, :], NT).astype(BF16)

    @pl.when(step_id == pl.num_programs(0) - 1)
    def _():
        for i in range(parts):
            chip = lax.rem(chip_ref[0] + i, parts)
            for out, total in ((wgate_out[i], dwgate), (wout_out[i], dwout)):
                size = out.shape[0]
                out[...] = total[pl.ds(pl.multiple_of(chip * size, size), size), :].astype(BF16)


def gate_call(steps, nb, lens, chip, parts, tok, cot, gain, win, gm, og, gate, y, rv):
    nseq, length, width = tok.shape
    inner = gm.shape[2]
    blocks = length // BLOCK

    def rows(i, nb, lens, chip):
        seq, blk = where_at(i, nb)
        return (seq, blk, 0)

    def rvrows(i, nb, lens, chip):
        seq, blk = where_at(i, nb)
        return (seq * blocks + blk, 0)

    tall, deep = pl.BlockSpec((1, BLOCK, width), rows), pl.BlockSpec((1, BLOCK, inner), rows)
    return pl.pallas_call(
        functools.partial(gate_kernel, parts),
        grid_spec=pltpu.PrefetchScalarGridSpec(
            num_scalar_prefetch=3,
            grid=(steps,),
            in_specs=[
                tall, tall, fixed(gain.shape), fixed((width, inner)), deep, fixed(og.shape), deep, deep,
                pl.BlockSpec((8, BLOCK), rvrows),
            ],
            out_specs=[deep, tall, fixed((8, inner))]
            + [fixed((width // parts, inner))] * parts
            + [fixed((inner // parts, width))] * parts,
            scratch_shapes=[
                pltpu.VMEM((width, BLOCK), BF16), pltpu.VMEM((BLOCK, inner), BF16), pltpu.VMEM((BLOCK, inner), BF16),
                pltpu.VMEM((width, inner), F32), pltpu.VMEM((inner, width), F32),
            ],
        ),
        out_shape=[
            jax.ShapeDtypeStruct((nseq, length, inner), F32),
            jax.ShapeDtypeStruct((nseq, length, width), BF16),
            jax.ShapeDtypeStruct((8, inner), F32),
        ]
        + [jax.ShapeDtypeStruct((width // parts, inner), BF16)] * parts
        + [jax.ShapeDtypeStruct((inner // parts, width), BF16)] * parts,
        compiler_params=pltpu.CompilerParams(
            dimension_semantics=("arbitrary",), vmem_limit_bytes=60 * 1024 * 1024
        ),
        cost_estimate=pl.CostEstimate(flops=2 * 10**10, bytes_accessed=60 << 20, transcendentals=0),
        name="layer_gate",
    )(nb, lens, chip, tok, cot, gain, win, gm, og, gate, y, rv)


def bwd_kernel(
    inner, heads,
    nb_ref,
    tok_ref, gain_ref, win_ref, cw_ref, cb_ref, hp_ref, dwide_ref, dog_ref, dy_ref, gp_ref, cin_ref, halo_ref, raw_ref, y_ref, s_ref,
    gn_ref, win_out, dcw_ref,
    cbuf, ubuf, dbuf, xbuf, dybuf, dproj, dstate, later, dwin_ref, normed_t, dhp_ref, ddw_ref, expand_ref, collect_ref,
):
    grid_id = pl.program_id(0)
    seq, step_id = where_at(grid_id, nb_ref)
    chan = inner + 2 * STATE
    width = tok_ref.shape[2]
    nb = nb_ref[seq]
    blk = nb - 1 - step_id

    @pl.when(grid_id == 0)
    def _():
        fill_expand(expand_ref)
        fill_collect(collect_ref)
        dwin_ref[...] = jnp.zeros_like(dwin_ref)
        dcw_ref[...] = jnp.zeros_like(dcw_ref)
        dhp_ref[...] = jnp.zeros_like(dhp_ref)
        ddw_ref[...] = jnp.zeros_like(ddw_ref)

    @pl.when(grid_id < nb_ref[0] + nb_ref[1])
    def _():
        @pl.when(step_id == 0)
        def _():
            dbuf[BLOCK : BLOCK + 8, :] = jnp.zeros((8, chan), F32)
            dstate[...] = jnp.zeros_like(dstate)
            later[...] = jnp.zeros_like(later)

        @pl.when(step_id > 0)
        def _():
            dbuf[BLOCK : BLOCK + 8, :] = dbuf[0:8, :]

        @pl.when(blk == 0)
        def _():
            cbuf[0:8, :] = jnp.zeros((8, chan), F32)

        @pl.when(blk > 0)
        def _():
            cbuf[0:8, :] = halo_ref[0]

        cbuf[8 : 8 + BLOCK, :] = cin_ref[0]
        normed_t[...] = normalize(tok_ref, gain_ref).T
        for j in range(0, chan, 256):
            at = slice(j, j + 256)
            u = convolve(cbuf, cw_ref, cb_ref, at)
            sig = sigmoid(u)
            xbuf[:, at] = u * sig
            ubuf[:, at] = sig * (1.0 + u * (1.0 - sig))
        raw = raw_ref[0] + hp_ref[0:1, :]
        step = softplus(raw)
        log_decay = -step * hp_ref[1:2, :]
        rows = lax.broadcasted_iota(jnp.int32, (CHUNK, CHUNK), 0)
        cols = lax.broadcasted_iota(jnp.int32, (CHUNK, CHUNK), 1)
        causal = cols >= rows
        left = cols < HEADDIM
        cum = causal_sum(log_decay)
        cum_t = cum.T
        four = jnp.concatenate([jnp.exp(cum), step, jnp.exp(each_last(cum) - cum)], axis=0)
        wide = spread(four, expand_ref[...])
        e_wide, dt_wide, t_wide = wide[:BLOCK], wide[BLOCK : 2 * BLOCK], wide[2 * BLOCK :]
        all_in = xbuf[:, inner : inner + STATE].astype(BF16)
        all_out = xbuf[:, inner + STATE :].astype(BF16)
        x = xbuf[:, :inner]
        dy = dy_ref[0]
        dy16 = dy.astype(BF16)
        ddw_ref[0:1, :] += jnp.sum(dy * x, axis=0, keepdims=True)
        xd32 = x * dt_wide
        xd = xd32.astype(BF16)
        xw = (xd32 * t_wide).astype(BF16)
        edy = (e_wide * dy).astype(BF16)
        count = BLOCK // CHUNK
        crosses, reaches, outers = [], [], []
        for c in range(count):
            at = chunk_rows(c)
            crosses.append(mm(all_in[at], all_out[at], NT))
            reaches.append(mm_state(all_out[at], s_ref[0, c]))
            outers.append(mm(all_out[at], edy[at], TN))
        dcrosses = [jnp.zeros((CHUNK, CHUNK), F32)] * count
        insides = [[] for _ in range(count)]
        for p in range(heads // 2):
            lanes = slice(p * 128, (p + 1) * 128)
            for c in range(count):
                at = chunk_rows(c)
                pair = xd[at, lanes]
                dpair = dy16[at, lanes]
                zero = jnp.zeros_like(pair)
                both = jnp.concatenate([jnp.where(left, dpair, zero), jnp.where(left, zero, dpair)], axis=0)
                dweights = mm(pair, both, NT)
                parts = []
                for i, h in enumerate((2 * p, 2 * p + 1)):
                    gap = cum_t[h : h + 1, at] - cum[at, h : h + 1]
                    decay = jnp.exp(jnp.where(causal, gap, FAR))
                    parts.append((crosses[c] * decay).astype(BF16))
                    dcrosses[c] = dcrosses[c] + dweights[:, i * CHUNK : (i + 1) * CHUNK] * decay
                insides[c].append(mm(jnp.concatenate(parts, axis=1), both))
        backs, folds = [None] * count, [None] * count
        for c in reversed(range(count)):
            at = chunk_rows(c)
            dheld = dstate[...]
            backs[c] = mm_state(all_in[at], dheld)
            folds[c] = jnp.sum(dheld * later[...], axis=0, keepdims=True)
            later[...] = s_ref[0, c]
            dstate[...] = e_wide[(c + 1) * CHUNK - 1 : (c + 1) * CHUNK] * dheld + outers[c]
            dcross16 = dcrosses[c].astype(BF16)
            ds_in = mm(dcross16, all_out[at]) + mm(xw[at], dheld.astype(BF16), NT)
            ds_out = mm(dcross16, all_in[at], TN) + mm(edy[at], s_ref[0, c].astype(BF16), NT)
            dbuf[at, inner : inner + STATE] = ds_in
            dbuf[at, inner + STATE :] = ds_out
        back = jnp.concatenate(backs, axis=0)
        reach = jnp.concatenate(reaches, axis=0)
        inside = jnp.concatenate([jnp.concatenate(part, axis=1) for part in insides], axis=0)
        dxd = inside + t_wide * back
        dybuf[...] = dt_wide * dxd + dwide_ref[0:1, :] * dy
        scanned = (y_ref[0] - dwide_ref[0:1, :] * x - e_wide * reach) * dy16.astype(F32) + edy.astype(F32) * reach
        scanned = scanned - xd.astype(F32) * inside - xw.astype(F32) * back
        high, low = two_parts(scanned)
        direct_high, direct_low = two_parts(x * dxd)
        rest = [part for fold in folds for part in two_parts(jnp.broadcast_to(fold, (16, inner)))]
        stacked = jnp.concatenate([direct_high, direct_low, high, low] + rest, axis=0)
        small = mm(stacked, collect_ref[...])
        ddirect = small[:BLOCK] + small[BLOCK : 2 * BLOCK]
        dcum = small[2 * BLOCK : 3 * BLOCK] + small[3 * BLOCK : 4 * BLOCK]
        dfold = jnp.concatenate(
            [
                jnp.broadcast_to(
                    small[4 * BLOCK + 32 * c : 4 * BLOCK + 32 * c + 1]
                    + small[4 * BLOCK + 32 * c + 16 : 4 * BLOCK + 32 * c + 17],
                    (CHUNK, LANES),
                )
                for c in range(count)
            ],
            axis=0,
        )
        dlog = reverse_sum(dcum) + dfold
        draw = (ddirect - dlog * hp_ref[1:2, :]) * sigmoid(raw)
        dhp_ref[0:1, :] += jnp.sum(draw, axis=0, keepdims=True)
        dhp_ref[1:2, :] += jnp.sum(dlog * log_decay, axis=0, keepdims=True)
        dproj[:, chan:] = draw.astype(BF16)
        for j in range(0, chan, 256):
            at = slice(j, j + 256)
            grad = dybuf[:, at] if j < inner else dbuf[0:BLOCK, at]
            du = grad * ubuf[:, at]
            dbuf[0:BLOCK, at] = du
            dcw_ref[CONV : CONV + 1, at] += jnp.sum(du, axis=0, keepdims=True)
            for k in range(CONV):
                dcw_ref[k : k + 1, at] += jnp.sum(du * cbuf[5 + k : 5 + k + BLOCK, at], axis=0, keepdims=True)
            dcin = cw_ref[CONV - 1 : CONV, at] * du
            for k in range(CONV - 1):
                dcin = dcin + cw_ref[k : k + 1, at] * dbuf[3 - k : 3 - k + BLOCK, at]
            dcin = dcin.astype(BF16)
            dproj[:, at] = dcin
            dwin_ref[:, at] += mm(normed_t[...], dcin)
        dwin_ref[:, chan:] += mm(normed_t[...], dproj[:, chan:])
        for j in range(0, width, 256):
            at = slice(j, j + 256)
            gn_ref[0, :, at] = (gp_ref[0, :, at].astype(F32) + mm(dproj[...], win_ref[at, inner:], NT)).astype(BF16)

    @pl.when(grid_id == pl.num_programs(0) - 1)
    def _():
        win_out[...] = dwin_ref[...].astype(BF16)
        dcw_ref[CONV + 1 : CONV + 2, :inner] = dog_ref[0:1, :]
        dcw_ref[CONV + 2 : CONV + 3, :LANES] = gather_heads(ddw_ref[...], collect_ref[...])[0:1]
        dcw_ref[CONV + 2 : CONV + 3, LANES : 2 * LANES] = dhp_ref[0:1, :]
        dcw_ref[CONV + 2 : CONV + 3, 2 * LANES : 3 * LANES] = dhp_ref[1:2, :]


def bwd_call(steps, nb, tok, gain, win, cw, cb, hp, dwide, dog, dy, gp, cin, raw, y, s):
    nseq, length, width = tok.shape
    inner = dy.shape[2]
    rest = win.shape[1] - inner
    heads = inner // HEADDIM
    chan = inner + 2 * STATE

    def place(i, nb):
        seq, back = where_at(i, nb)
        return seq, nb[seq] - 1 - back

    def rows(i, nb):
        seq, blk = place(i, nb)
        return (seq, blk, 0)

    def srows(i, nb):
        seq, blk = place(i, nb)
        return (seq, blk, 0, 0)

    def halo(i, nb):
        seq, blk = place(i, nb)
        return (seq, jnp.maximum(blk * (BLOCK // 8) - 1, 0), 0)

    def whole(shape):
        return pl.BlockSpec(shape, lambda *_: (0,) * len(shape), pipeline_mode=pl.Buffered(1))

    grid_spec = pltpu.PrefetchScalarGridSpec(
        num_scalar_prefetch=1,
        grid=(steps,),
        in_specs=[
            pl.BlockSpec((1, BLOCK, width), rows),
            fixed(gain.shape), fixed(win.shape), fixed(cw.shape), fixed(cb.shape),
            fixed(hp.shape), fixed(dwide.shape), fixed(dog.shape),
            pl.BlockSpec((1, BLOCK, inner), rows),
            pl.BlockSpec((1, BLOCK, width), rows),
            pl.BlockSpec((1, BLOCK, chan), rows),
            pl.BlockSpec((1, 8, chan), halo),
            pl.BlockSpec((1, BLOCK, LANES), rows),
            pl.BlockSpec((1, BLOCK, inner), rows),
            pl.BlockSpec((1, BLOCK // CHUNK, STATE, inner), srows),
        ],
        out_specs=[
            pl.BlockSpec((1, BLOCK, width), rows),
            whole((width, rest)), whole((8, chan)),
        ],
        scratch_shapes=[
            pltpu.VMEM((BLOCK + 8, chan), F32),
            pltpu.VMEM((BLOCK, chan), F32),
            pltpu.VMEM((BLOCK + 8, chan), F32),
            pltpu.VMEM((BLOCK, chan), F32),
            pltpu.VMEM((BLOCK, inner), F32),
            pltpu.VMEM((BLOCK, rest), BF16),
            pltpu.VMEM((STATE, inner), F32),
            pltpu.VMEM((STATE, inner), F32),
            pltpu.VMEM((width, rest), F32),
            pltpu.VMEM((width, BLOCK), BF16),
            pltpu.VMEM((8, LANES), F32),
            pltpu.VMEM((8, inner), F32),
            pltpu.VMEM((2 * LANES, inner), BF16),
            pltpu.VMEM((inner, LANES), BF16),
        ],
    )
    shapes = [
        jax.ShapeDtypeStruct((nseq, length, width), BF16),
        jax.ShapeDtypeStruct((width, rest), BF16),
        jax.ShapeDtypeStruct((8, chan), F32),
    ]
    return pl.pallas_call(
        functools.partial(bwd_kernel, inner, heads),
        grid_spec=grid_spec,
        out_shape=shapes,
        compiler_params=pltpu.CompilerParams(
            dimension_semantics=("arbitrary",), vmem_limit_bytes=63 * 1024 * 1024
        ),
        cost_estimate=pl.CostEstimate(
            flops=10**11, bytes_accessed=100 << 20, transcendentals=0
        ),
        name="layer_backward",
    )(nb, tok, gain, win, cw, cb, hp, dwide, dog, dy, gp, cin, cin, raw, y, s)


def fill_expand(expand):
    owner = lax.broadcasted_iota(jnp.int32, expand.shape, 1) // HEADDIM
    head = lax.rem(lax.broadcasted_iota(jnp.int32, expand.shape, 0), LANES)
    expand[...] = (owner == head).astype(F32).astype(BF16)


def fill_collect(collect):
    owner = lax.broadcasted_iota(jnp.int32, collect.shape, 0) // HEADDIM
    head = lax.broadcasted_iota(jnp.int32, collect.shape, 1)
    collect[...] = (owner == head).astype(F32).astype(BF16)


def combine_kernel(place_ref, count_ref, base_ref, part_ref, out_ref):
    kept = count_ref[pl.program_id(0)]
    base = base_ref[0]
    row = lax.broadcasted_iota(jnp.int32, base.shape, 0)
    part = jnp.where(row < kept, part_ref[0].astype(F32), 0.0)
    out_ref[0] = (base.astype(F32) + part).astype(BF16)


def combine_call(place, kept, base, part):
    count, span, width = base.shape
    block = (1, span, width)
    return pl.pallas_call(
        combine_kernel,
        grid_spec=pltpu.PrefetchScalarGridSpec(
            num_scalar_prefetch=2,
            grid=(count,),
            in_specs=[
                pl.BlockSpec(block, lambda s, place, kept: (s, 0, 0)),
                pl.BlockSpec(block, lambda s, place, kept: (place[s], 0, 0)),
            ],
            out_specs=pl.BlockSpec(block, lambda s, place, kept: (s, 0, 0)),
        ),
        out_shape=jax.ShapeDtypeStruct(base.shape, BF16),
        name="combine",
    )(place, kept, base, part)


def peers_of(n):
    return [(away, turn) for away in range(n // 2) for turn in range(2) if away or turn]


def enter(n, me):
    barrier = pltpu.get_barrier_semaphore()
    for away, turn in peers_of(n):
        pl.semaphore_signal(barrier, inc=1, device_id={"fsdp": peer_at(n, me, away, turn)}, device_id_type=MESH)
    pl.semaphore_wait(barrier, n - 1)


def peer_at(n, me, away, turn):
    chip = lax.rem(lax.div(me, 2) + away, n // 2)
    return 2 * chip + lax.rem(lax.rem(me, 2) + turn, 2)


def sender_at(n, me, away, turn):
    chip = lax.rem(lax.div(me, 2) + n // 2 - away, n // 2)
    return 2 * chip + lax.rem(lax.rem(me, 2) + turn, 2)


def rows_at(index, size):
    return pl.ds(pl.multiple_of(index * size, size), size)


def start_kernel(
    n, source_ref, tokens, grads, shards, small, tok, win, smalls, sent_grad, rows_in, sent, w_held, s_held, here, w_send, w_recv, t_send, t_recv, f_send, f_recv, s_send, s_recv
):
    me = lax.axis_index("fsdp")
    core = lax.rem(me, 2)
    partner = 2 * lax.div(me, 2) + 1 - core
    span, rows = tokens.shape[1], shards.shape[1]
    loads = [
        pltpu.make_async_copy(tokens, rows_in, here.at[0]),
        pltpu.make_async_copy(shards.at[core], w_held, here.at[1]),
        pltpu.make_async_copy(small, s_held, here.at[2]),
    ]
    for copy in loads:
        copy.start()

    def place_rows(index):
        chosen = source_ref[index]
        step = 32

        @pl.loop(0, span // step)
        def _(i):
            at = pl.ds(pl.multiple_of(i * step, step), step)
            sent[index, at, :] = rows_in[chosen, at, :]

    enter(n, me)
    pending = []
    loads[0].wait()
    for index, (away, turn) in enumerate(peers_of(n)):
        peer = peer_at(n, me, away, turn)
        theirs = lax.rem(core + turn, 2)

        def push(src, dst, send, recv):
            copy = pltpu.make_async_remote_copy(
                src_ref=src, dst_ref=dst, send_sem=send, recv_sem=recv, device_id={"fsdp": peer}, device_id_type=MESH
            )
            copy.start()
            pending.append(copy)

        place_rows(peer)
        push(sent.at[peer], tok.at[theirs, rows_at(me, span)], t_send.at[index], t_recv.at[index])
        push(shards.at[theirs], win.at[rows_at(me, rows)], w_send.at[index], w_recv.at[index])
        push(small, smalls.at[me], s_send.at[index], s_recv.at[index])
    place_rows(me)
    for copy in loads[1:]:
        copy.wait()
    local = [
        pltpu.make_async_copy(sent.at[me], tok.at[core, rows_at(me, span)], here.at[0]),
        pltpu.make_async_copy(sent.at[partner], tok.at[1 - core, rows_at(me, span)], here.at[1]),
        pltpu.make_async_copy(w_held, win.at[rows_at(me, rows)], here.at[2]),
        pltpu.make_async_copy(s_held, smalls.at[me], here.at[3]),
    ]
    for copy in local:
        copy.start()
    more = pltpu.make_async_copy(grads, rows_in, here.at[4])
    more.start()

    def forward(index, src, owner):
        copy = pltpu.make_async_remote_copy(
            src_ref=src, dst_ref=tok.at[core, rows_at(owner, span)], send_sem=f_send.at[index],
            recv_sem=f_recv.at[index], device_id={"fsdp": partner}, device_id_type=MESH,
        )
        copy.start()
        return copy

    passed = [forward(0, sent.at[me], me)]
    for index, (away, turn) in enumerate(peers_of(n)):
        owner = sender_at(n, me, away, turn)
        block = tok.at[core, rows_at(owner, span)]
        pltpu.make_async_remote_copy(
            src_ref=block, dst_ref=block, send_sem=t_send.at[index], recv_sem=t_recv.at[index],
            device_id={"fsdp": partner}, device_id_type=MESH,
        ).wait_recv()
        if away:
            passed.append(forward(index, block, owner))
    for copy in passed:
        copy.wait()
    for copy in pending:
        copy.wait_send()
    for copy in local:
        copy.wait()
    more.wait()

    @pl.loop(0, n)
    def _(index):
        place_rows(index)

    back = pltpu.make_async_copy(sent, sent_grad, here.at[4])
    back.start()
    for index, (away, turn) in enumerate(peers_of(n)):
        owner = sender_at(n, me, away, turn)
        checks = [(win.at[rows_at(owner, rows)], w_send, w_recv), (smalls.at[owner], s_send, s_recv)]
        for block, send, recv in checks:
            pltpu.make_async_remote_copy(
                src_ref=block, dst_ref=block, send_sem=send.at[index], recv_sem=recv.at[index],
                device_id={"fsdp": partner}, device_id_type=MESH,
            ).wait_recv()
    back.wait()


def start_call(n, source, tokens, grads, shards, small):
    span, width = tokens.shape[1:]
    _, rows, wide = shards.shape
    count = n - 1
    anywhere = pl.BlockSpec(memory_space=pl.ANY)
    return pl.pallas_call(
        functools.partial(start_kernel, n),
        out_shape=[
            jax.ShapeDtypeStruct((2, n * span, width), BF16),
            jax.ShapeDtypeStruct((n * rows, wide), BF16),
            jax.ShapeDtypeStruct((n,) + small.shape, BF16),
            jax.ShapeDtypeStruct(tokens.shape, BF16),
        ],
        in_specs=[pl.BlockSpec(memory_space=pltpu.SMEM)] + [anywhere] * 4,
        out_specs=[anywhere] * 4,
        scratch_shapes=[
            pltpu.VMEM(tokens.shape, BF16), pltpu.VMEM(tokens.shape, BF16), pltpu.VMEM((rows, wide), BF16), pltpu.VMEM(small.shape, BF16),
        ]
        + [pltpu.SemaphoreType.DMA((5,))] + [pltpu.SemaphoreType.DMA((count,))] * 8,
        compiler_params=pltpu.CompilerParams(
            collective_id=0, has_side_effects=True, vmem_limit_bytes=60 * 1024 * 1024
        ),
        name="start",
    )(source, tokens, grads, shards, small)


def exchange_kernel(
    bp, ss_ref, v_ref, branch, rv_ref, mine, theirs, ss_in, v_in, here, put, b_send, b_recv, s_send, s_recv
):
    me = lax.axis_index("fsdp")
    core = lax.rem(me, 2)
    partner = 2 * lax.div(me, 2) + 1 - core
    length, width = mine.shape
    blocks = length // BLOCK
    barrier = pltpu.get_barrier_semaphore()
    pl.semaphore_signal(barrier, inc=1, device_id={"fsdp": partner}, device_id_type=MESH)
    pl.semaphore_wait(barrier, 1)

    def remote(src, dst, send, recv):
        return pltpu.make_async_remote_copy(
            src_ref=src, dst_ref=dst, send_sem=send, recv_sem=recv, device_id={"fsdp": partner}, device_id_type=MESH
        )

    load = pltpu.make_async_copy(bp.at[core], mine, here.at[0])
    load.start()
    copies = [
        remote(ss_ref, ss_in, s_send.at[0], s_recv.at[0]),
        remote(v_ref, v_in, s_send.at[1], s_recv.at[1]),
    ]
    for b in range(blocks):
        at = pl.ds(b * BLOCK, BLOCK)
        copies.append(remote(bp.at[1 - core, at], theirs.at[at], b_send.at[b], b_recv.at[b]))
    for copy in copies:
        copy.start()
    for copy in copies[:2]:
        copy.wait_recv()
    scale = lax.rsqrt((ss_ref[...] + ss_in[...]) * (1.0 / INNER) + EPS)
    coef = scale * scale * scale * (v_ref[...] + v_in[...]) * (1.0 / INNER)
    sub = lax.rem(lax.broadcasted_iota(jnp.int32, scale.shape, 0), 8)
    rv_ref[...] = jnp.where(sub == 0, scale, coef)
    load.wait()
    puts = []
    for b in range(blocks):
        at = pl.ds(b * BLOCK, BLOCK)
        copies[2 + b].wait_recv()
        rows = rv_ref[pl.ds(pl.multiple_of((core * blocks + b) * 8, 8), 8), :]
        column = jnp.concatenate([rows, jnp.zeros((LANES - 8, BLOCK), F32)], axis=0).T[:, 0:1]
        mine[at, :] = ((mine[at, :].astype(F32) + theirs[at, :].astype(F32)) * column).astype(BF16)
        copy = pltpu.make_async_copy(mine.at[at], branch.at[at], put.at[b])
        copy.start()
        puts.append(copy)
    for copy in copies:
        copy.wait_send()
    for copy in puts:
        copy.wait()


def exchange_call(bp, ss, v):
    _, length, width = bp.shape
    blocks = length // BLOCK
    vmem = pl.BlockSpec(memory_space=pltpu.VMEM)
    anywhere = pl.BlockSpec(memory_space=pl.ANY)
    dma = pltpu.SemaphoreType.DMA
    return pl.pallas_call(
        exchange_kernel,
        out_shape=[jax.ShapeDtypeStruct((length, width), BF16), jax.ShapeDtypeStruct(ss.shape, F32)],
        in_specs=[anywhere, vmem, vmem],
        out_specs=[anywhere, vmem],
        scratch_shapes=[
            pltpu.VMEM((length, width), BF16), pltpu.VMEM((length, width), BF16),
            pltpu.VMEM(ss.shape, F32), pltpu.VMEM(ss.shape, F32),
            dma((1,)), dma((blocks,)), dma((blocks,)), dma((blocks,)), dma((2,)), dma((2,)),
        ],
        compiler_params=pltpu.CompilerParams(
            collective_id=2, has_side_effects=True, vmem_limit_bytes=60 * 1024 * 1024
        ),
        name="exchange",
    )(bp, ss, v)


def pair_kernel(mine, both, own, theirs, load, put, send, recv):
    me = lax.axis_index("fsdp")
    core = lax.rem(me, 2)
    partner = 2 * lax.div(me, 2) + 1 - core
    barrier = pltpu.get_barrier_semaphore()
    pl.semaphore_signal(barrier, inc=1, device_id={"fsdp": partner}, device_id_type=MESH)
    pl.semaphore_wait(barrier, 1)
    parts = send.shape[0]
    size = mine.shape[0] // parts
    slices = [pl.ds(i * size, size) for i in range(parts)]
    loads = [pltpu.make_async_copy(mine.at[at], own.at[at], load.at[i]) for i, at in enumerate(slices)]
    copies = [
        pltpu.make_async_remote_copy(
            src_ref=mine.at[at], dst_ref=theirs.at[at], send_sem=send.at[i], recv_sem=recv.at[i],
            device_id={"fsdp": partner}, device_id_type=MESH,
        )
        for i, at in enumerate(slices)
    ]
    for copy in copies + loads:
        copy.start()
    puts = []
    for i, at in enumerate(slices):
        loads[i].wait()
        puts.append(pltpu.make_async_copy(own.at[at], both.at[core, at], put.at[i]))
        puts[-1].start()
    for i, at in enumerate(slices):
        copies[i].wait()
        puts.append(pltpu.make_async_copy(theirs.at[at], both.at[1 - core, at], put.at[parts + i]))
        puts[-1].start()
    for copy in puts:
        copy.wait()


def pair_call(mine):
    parts = 8
    anywhere = pl.BlockSpec(memory_space=pl.ANY)
    dma = pltpu.SemaphoreType.DMA
    return pl.pallas_call(
        pair_kernel,
        out_shape=jax.ShapeDtypeStruct((2,) + mine.shape, BF16),
        in_specs=[anywhere],
        out_specs=anywhere,
        scratch_shapes=[
            pltpu.VMEM(mine.shape, BF16), pltpu.VMEM(mine.shape, BF16), dma((parts,)), dma((2 * parts,)),
            dma((parts,)), dma((parts,)),
        ],
        compiler_params=pltpu.CompilerParams(
            collective_id=3, has_side_effects=True, vmem_limit_bytes=60 * 1024 * 1024
        ),
        name="pair",
    )(mine)


def finish_kernel(
    n, planes, cuts, groups, length_ref, place_ref, kept_ref, gn, tok, gain_ref, early, dwin, o_early,
    sums, base, base_grad, branch,
    output, token_grad, w_ref, o_ref, sums_ref,
    gn_mine, gn_theirs, hidden, grad, dgain, w_own, w_in, o_own, o_in, w_give, w_pair, w_chip, z_in, oz_in, z_out,
    oz_out, w_all, o_all, s_own, s_in, d_in, s_tot, s_up, back, out_buf, grad_buf, part,
    here, g_send, g_recv, b_send, b_recv, w_send, w_recv, o_send, o_recv, p_send, p_recv,
    z_send, z_recv, oz_send, oz_recv, y_send, y_recv, oy_send, oy_recv, s_send, s_recv, d_send, d_recv,
    u_send, u_recv,
):
    me = lax.axis_index("fsdp")
    level = lax.axis_index("rep")
    core = lax.rem(me, 2)
    chip = lax.div(me, 2)
    partner = 2 * chip + 1 - core
    span = back.shape[1]
    ahead = early[0].shape[1]
    first_cut = 1
    chip_rows = w_own.shape[0]
    rows = chip_rows // 2
    outs = o_own.shape[0]
    zrows, orows = rows // planes, outs // planes
    others = n // 2 - 1
    tile = 16
    barrier = pltpu.get_barrier_semaphore()
    for away, turn in peers_of(n):
        pl.semaphore_signal(barrier, inc=1, device_id={"fsdp": peer_at(n, me, away, turn)}, device_id_type=MESH)
    for up in range(1, planes):
        pl.semaphore_signal(barrier, inc=1, device_id={"rep": lax.rem(level + up, planes)}, device_id_type=MESH)
    pl.semaphore_wait(barrier, n - 1 + planes - 1)

    def remote(src, dst, send, recv, where):
        return pltpu.make_async_remote_copy(
            src_ref=src, dst_ref=dst, send_sem=send, recv_sem=recv, device_id=where, device_id_type=MESH
        )

    def arrived(block, send, recv):
        remote(block, block, send, recv, {"fsdp": partner}).wait_recv()

    pending = []

    def push(src, dst, send, recv, where):
        copy = remote(src, dst, send, recv, where)
        copy.start()
        pending.append(copy)

    def above(up):
        return lax.rem(level + up, planes)

    loads = [
        pltpu.make_async_copy(early[0], w_own.at[:, pl.ds(0, ahead)], here.at[0]),
        pltpu.make_async_copy(
            dwin.at[rows_at(chip, chip_rows)], w_own.at[:, pl.ds(ahead, dwin.shape[1])], here.at[1]
        ),
        pltpu.make_async_copy(o_early[0], o_own, here.at[2]),
        pltpu.make_async_copy(gn.at[core], gn_mine, here.at[3]),
        pltpu.make_async_copy(tok.at[core], hidden, here.at[4]),
        pltpu.make_async_copy(sums, s_own, here.at[5]),
        pltpu.make_async_copy(base, out_buf, here.at[6]),
        pltpu.make_async_copy(base_grad, grad_buf, here.at[7]),
        pltpu.make_async_copy(branch, part, here.at[8]),
    ]
    for i in range(others):
        loads.append(pltpu.make_async_copy(early[i + 1], w_in.at[i, :, pl.ds(0, ahead)], here.at[9 + 2 * i]))
        loads.append(pltpu.make_async_copy(o_early[i + 1], o_in.at[i], here.at[10 + 2 * i]))
    everyone = [(0, 0)] + peers_of(n)
    for c, cols in enumerate(cuts):
        if c >= first_cut:
            for i in range(others):
                target = {"fsdp": peer_at(n, me, i + 1, 0)}
                other = lax.rem(chip + i + 1, n // 2)
                k = c * others + i
                given = pl.ds(cols.start - ahead, cols.size)
                push(
                    dwin.at[rows_at(other, chip_rows), given], w_in.at[i, :, cols], w_send.at[k], w_recv.at[k],
                    target,
                )
    for copy in loads:
        copy.start()
    for index, (away, turn) in enumerate(everyone):
        if index:
            peer = peer_at(n, me, away, turn)
            push(sums, s_in.at[index - 1], s_send.at[index], s_recv.at[index], {"fsdp": peer})
    for index, (away, turn) in enumerate(everyone):
        block = rows_at(peer_at(n, me, away, turn), span)
        push(gn.at[1 - core, block], gn_theirs.at[block], g_send.at[index], g_recv.at[index], {"fsdp": partner})
    step = 64

    def norm_back(index):
        away, turn = everyone[index]
        target = peer_at(n, me, away, turn)
        block = rows_at(target, span)
        sender_index = everyone.index((away, 1 - turn))
        arrived(gn_theirs.at[block], g_send.at[sender_index], g_recv.at[sender_index])
        first = target * span

        @pl.loop(0, span // step)
        def _(i):
            at = pl.ds(pl.multiple_of(first + i * step, step), step)
            position = first + i * step + lax.broadcasted_iota(jnp.int32, (step, gn_mine.shape[1]), 0)
            total = gn_mine[at, :].astype(F32) + gn_theirs[at, :].astype(F32)
            total = jnp.where(position < length_ref[0], total, 0.0)
            h = hidden[at, :].astype(F32)
            inv = lax.rsqrt(jnp.mean(h * h, axis=1, keepdims=True) + EPS)
            normal = h * inv
            dgain[0:1, :] += jnp.sum(total * normal, axis=0, keepdims=True)
            scaled = total * gain_ref[0:1, :]
            mean = jnp.mean(scaled * normal, axis=1, keepdims=True)
            grad[at, :] = (inv * (scaled - normal * mean)).astype(BF16)

    def give_back(index):
        away, turn = everyone[index]
        peer = peer_at(n, me, away, turn)
        push(grad.at[rows_at(peer, span)], back.at[me], b_send.at[index], b_recv.at[index], {"fsdp": peer})

    def add_up(own, pieces, at, cols):
        total = own[at, cols].astype(F32)
        for i in range(pieces.shape[0]):
            total = total + pieces[i, at, cols].astype(F32)
        return total.astype(BF16)

    def stage_sum(c):
        cols = cuts[c]
        if c >= first_cut:
            for i in range(others):
                k = c * others + i
                arrived(w_in.at[i, :, cols], w_send.at[k], w_recv.at[k])

        @pl.loop(0, rows // tile)
        def _(i):
            at = pl.ds(pl.multiple_of((1 - core) * rows + i * tile, tile), tile)
            w_give[pl.ds(pl.multiple_of(i * tile, tile), tile), cols] = add_up(w_own, w_in, at, cols)

        push(w_give.at[:, cols], w_pair.at[:, cols], p_send.at[c], p_recv.at[c], {"fsdp": partner})

        @pl.loop(0, rows // tile)
        def _(i):
            at = pl.ds(pl.multiple_of(core * rows + i * tile, tile), tile)
            w_chip[core, pl.ds(pl.multiple_of(i * tile, tile), tile), cols] = add_up(w_own, w_in, at, cols)

    def stage_up(c):
        cols = cuts[c]
        arrived(w_pair.at[:, cols], p_send.at[c], p_recv.at[c])
        w_chip[1 - core, :, cols] = w_pair[:, cols]
        for up in range(1, planes):
            k = c * (planes - 1) + up - 1
            push(
                w_chip.at[:, rows_at(above(up), zrows), cols], z_in.at[up - 1, :, :, cols],
                z_send.at[k], z_recv.at[k], {"rep": above(up)},
            )

    def stage_total(c):
        cols = cuts[c]
        for up in range(1, planes):
            k = c * (planes - 1) + up - 1
            arrived(z_in.at[up - 1, :, :, cols], z_send.at[k], z_recv.at[k])
        at = rows_at(level, zrows)
        for q in range(2):
            total = w_chip[q, at, cols].astype(F32)
            for k in range(planes - 1):
                total = total + z_in[k, q, :, cols].astype(F32)
            z_out[q, :, cols] = total.astype(BF16)
            w_all[q, at, cols] = total.astype(BF16)
        for up in range(1, planes):
            k = c * (planes - 1) + up - 1
            push(z_out.at[:, :, cols], w_all.at[:, at, cols], y_send.at[k], y_recv.at[k], {"rep": above(up)})

    def finish_rows(buf, pieces, s):
        kept = kept_ref[s]
        chosen = place_ref[s]

        @pl.loop(0, span // step)
        def _(i):
            at = pl.ds(pl.multiple_of(i * step, step), step)
            row = i * step + lax.broadcasted_iota(jnp.int32, (step, buf.shape[2]), 0)
            added = jnp.where(row < kept, pieces[chosen, at, :].astype(F32), 0.0)
            buf[s, at, :] = (buf[s, at, :].astype(F32) + added).astype(BF16)

    for copy in loads[:3] + loads[9:]:
        copy.wait()
    stage_sum(0)

    @pl.loop(0, outs // tile)
    def _(i):
        at = pl.ds(pl.multiple_of(i * tile, tile), tile)
        o_own[at, :] = add_up(o_own, o_in, at, slice(None))

    for up in range(1, planes):
        push(
            o_own.at[rows_at(above(up), orows)], oz_in.at[up - 1], oz_send.at[up - 1], oz_recv.at[up - 1],
            {"rep": above(up)},
        )
    stage_up(0)
    for copy in loads[3:6]:
        copy.wait()
    dgain[...] = jnp.zeros_like(dgain)
    for index in range(n):
        norm_back(index)
    seg = dgain.shape[1] // n
    for index, (away, turn) in enumerate(everyone):
        if index:
            peer = peer_at(n, me, away, turn)
            cols = pl.ds(pl.multiple_of(peer * seg, seg), seg)
            push(dgain.at[:, cols], d_in.at[index - 1], d_send.at[index], d_recv.at[index], {"fsdp": peer})
    s_tot[core] = s_own[...]
    s_tot[1 - core] = jnp.zeros_like(s_own)
    for index, (away, turn) in enumerate(everyone):
        if index:
            arrived(s_in.at[index - 1], s_send.at[index], s_recv.at[index])
            arrived(d_in.at[index - 1], d_send.at[index], d_recv.at[index])
            theirs = lax.rem(core + turn, 2)
            s_tot[theirs] = s_tot[theirs] + s_in[index - 1]
    mine = dgain[:, pl.ds(pl.multiple_of(me * seg, seg), seg)]
    for index in range(n - 1):
        mine = mine + d_in[index]
    s_tot[0, CONV + 3 : CONV + 4, 0:seg] = mine[0:1]
    for up in range(1, planes):
        push(s_tot, s_up.at[up - 1], u_send.at[up - 1], u_recv.at[up - 1], {"rep": above(up)})
    count = len(cuts)
    waiting = list(range(1, n))
    for c in range(1, count):
        stage_sum(c)
        for index in waiting[: 2 if c < count - 1 else n]:
            give_back(index)
        del waiting[:2]
        stage_up(c)
        stage_total(c - 1)
        if c == 1:
            for i in range(planes - 1):
                arrived(oz_in.at[i], oz_send.at[i], oz_recv.at[i])
            at = rows_at(level, orows)
            total = o_own[at, :].astype(F32)
            for k in range(planes - 1):
                total = total + oz_in[k].astype(F32)
            oz_out[...] = total.astype(BF16)
            o_all[at, :] = total.astype(BF16)
            for up in range(1, planes):
                push(oz_out, o_all.at[at], oy_send.at[up - 1], oy_recv.at[up - 1], {"rep": above(up)})
    for copy in loads[6:9]:
        copy.wait()
    for s in range(n):
        finish_rows(out_buf, part, s)
    stores = [pltpu.make_async_copy(out_buf, output, here.at[6])]
    stores[0].start()
    stage_total(count - 1)

    for i in range(planes - 1):
        arrived(s_up.at[i], u_send.at[i], u_recv.at[i])
    total = s_tot[...]
    for k in range(planes - 1):
        total = total + s_up[k]
    sums_ref[...] = total
    for c, cols in enumerate(cuts):
        for up in range(1, planes):
            below = lax.rem(level + planes - up, planes)
            k = c * (planes - 1) + up - 1
            arrived(w_all.at[:, rows_at(below, zrows), cols], y_send.at[k], y_recv.at[k])
    inner, group, heads = groups
    for g in range(2 * inner // group):
        q, at = g % 2, g // 2 * group
        w_ref[:, g * group : (g + 1) * group] = w_all[q, :, at : at + group].astype(F32)
        w_ref[:, 2 * inner + g * group : 2 * inner + (g + 1) * group] = (
            w_all[q, :, inner + at : inner + at + group].astype(F32)
        )
    both = w_all[0, :, 2 * inner : 2 * inner + 2 * STATE].astype(F32)
    both = both + w_all[1, :, 2 * inner : 2 * inner + 2 * STATE].astype(F32)
    w_ref[:, 4 * inner : 4 * inner + 2 * STATE] = both
    first = 2 * inner + 2 * STATE
    tails = [w_all[q, :, first : first + LANES].astype(F32) for q in range(2)]
    size = group // HEADDIM
    pieces = [tails[g % 2][:, g // 2 * size : (g // 2 + 1) * size] for g in range(2 * inner // group)]
    w_ref[:, 4 * inner + 2 * STATE :] = jnp.concatenate(pieces, axis=1)
    for up in range(1, planes):
        below = lax.rem(level + planes - up, planes)
        arrived(o_all.at[rows_at(below, orows)], oy_send.at[up - 1], oy_recv.at[up - 1])
    o_ref[...] = o_all[...].astype(F32)
    for index, (away, turn) in enumerate(everyone):
        if index:
            owner = sender_at(n, me, away, turn)
            arrived(back.at[owner], b_send.at[index], b_recv.at[index])
    back[me] = grad[rows_at(me, span), :]
    for s in range(n):
        finish_rows(grad_buf, back, s)
    stores.append(pltpu.make_async_copy(grad_buf, token_grad, here.at[7]))
    stores[1].start()
    for copy in pending:
        copy.wait_send()
    for copy in stores:
        copy.wait()


def finish_call(
    n, planes, group, length, place, kept, gn, tok, gain, early, dwin, o_early, sums, base, base_grad, branch,
):
    _, total, width = gn.shape
    span = total // n
    ahead = early[0].shape[1]
    wide = ahead + dwin.shape[1]
    inner = (n // 2) * o_early[0].shape[0]
    heads = inner // HEADDIM
    chip_rows, outs = dwin.shape[0] // (n // 2), inner // (n // 2)
    rows = chip_rows // 2
    others = n // 2 - 1
    lane_tiles = dwin.shape[1] // LANES
    late = 3
    bounds = [ahead + (lane_tiles * i + late - 1) // late * LANES for i in range(late + 1)]
    cuts = [pl.ds(0, ahead)] + [pl.ds(bounds[i], bounds[i + 1] - bounds[i]) for i in range(late)]
    pieces = late + 1
    anywhere = pl.BlockSpec(memory_space=pl.ANY)
    vmem = pl.BlockSpec(memory_space=pltpu.VMEM)
    smem = pl.BlockSpec(memory_space=pltpu.SMEM)
    dma = pltpu.SemaphoreType.DMA
    up = planes - 1
    return pl.pallas_call(
        functools.partial(finish_kernel, n, planes, cuts, (inner, group, heads)),
        out_shape=[
            jax.ShapeDtypeStruct((n, span, width), BF16),
            jax.ShapeDtypeStruct((n, span, width), BF16),
            jax.ShapeDtypeStruct((rows, 4 * inner + 2 * STATE + 2 * heads), F32),
            jax.ShapeDtypeStruct((outs, width), F32),
            jax.ShapeDtypeStruct((2,) + sums.shape, F32),
        ],
        in_specs=[smem, smem, smem, anywhere, anywhere, vmem, [anywhere] * len(early), anywhere]
        + [[anywhere] * len(early), anywhere, anywhere, anywhere, anywhere],
        out_specs=[anywhere, anywhere, vmem, vmem, vmem],
        scratch_shapes=[
            pltpu.VMEM((total, width), BF16), pltpu.VMEM((total, width), BF16), pltpu.VMEM((total, width), BF16),
            pltpu.VMEM((total, width), BF16), pltpu.VMEM((8, width), F32),
            pltpu.VMEM((chip_rows, wide), BF16), pltpu.VMEM((others, chip_rows, wide), BF16),
            pltpu.VMEM((outs, width), BF16), pltpu.VMEM((others, outs, width), BF16),
            pltpu.VMEM((rows, wide), BF16), pltpu.VMEM((rows, wide), BF16), pltpu.VMEM((2, rows, wide), BF16),
            pltpu.VMEM((up, 2, rows // planes, wide), BF16), pltpu.VMEM((up, outs // planes, width), BF16),
            pltpu.VMEM((2, rows // planes, wide), BF16), pltpu.VMEM((outs // planes, width), BF16),
            pltpu.VMEM((2, rows, wide), BF16), pltpu.VMEM((outs, width), BF16),
            pltpu.VMEM(sums.shape, F32), pltpu.VMEM((n - 1,) + sums.shape, F32),
            pltpu.VMEM((n - 1, 8, LANES), F32), pltpu.VMEM((2,) + sums.shape, F32),
            pltpu.VMEM((up, 2) + sums.shape, F32),
            pltpu.VMEM((n, span, width), BF16), pltpu.VMEM((n, span, width), BF16),
            pltpu.VMEM((n, span, width), BF16), pltpu.VMEM((n, span, width), BF16),
            dma((9 + 2 * others,)), dma((n,)), dma((n,)), dma((n,)), dma((n,)),
            dma((pieces * others,)), dma((pieces * others,)), dma((others,)), dma((others,)),
            dma((pieces,)), dma((pieces,)), dma((pieces * up,)), dma((pieces * up,)), dma((up,)), dma((up,)),
            dma((pieces * up,)), dma((pieces * up,)), dma((up,)), dma((up,)),
            dma((n,)), dma((n,)), dma((n,)), dma((n,)), dma((up,)), dma((up,)),
        ],
        compiler_params=pltpu.CompilerParams(
            collective_id=1, has_side_effects=True, vmem_limit_bytes=60 * 1024 * 1024
        ),
        name="finish",
    )(length, place, kept, gn, tok, gain, early, dwin, o_early, sums, base, base_grad, branch)


def pairs_of(n):
    return [[2 * c, 2 * c + 1] for c in range(n // 2)]


def columns_of(n):
    return [list(range(q, n, 2)) for q in range(2)]


def halves(array, axis, group):
    shape = array.shape
    view = array.reshape(shape[:axis] + (shape[axis] // (2 * group), 2, group) + shape[axis + 1 :])
    out = []
    for q in range(2):
        part = lax.index_in_dim(view, q, axis + 1, keepdims=False)
        out.append(part.reshape(shape[:axis] + (shape[axis] // 2,) + shape[axis + 1 :]))
    return out


def interleave(first, second, axis, group):
    shape = first.shape
    views = [
        part.reshape(shape[:axis] + (shape[axis] // group, 1, group) + shape[axis + 1 :]) for part in (first, second)
    ]
    return jnp.concatenate(views, axis=axis + 1).reshape(shape[:axis] + (2 * shape[axis],) + shape[axis + 1 :])


def body(
    tokens, cotangent, lengths, dealing, norm_gain, in_weight, conv_weight, conv_bias, dt_bias, a_log, skip_gain,
    out_gain, out_weight,
):
    n = lax.axis_size("fsdp")
    me = lax.axis_index("fsdp")
    core = lax.rem(me, 2)
    pairs, columns = pairs_of(n), columns_of(n)
    local_tokens, local_grad = tokens[0], cotangent[0]
    count, span, width = local_tokens.shape
    length = span * n
    inner = INNER // 2
    heads = HEADS // 2
    group = max(HEADDIM, INNER // n)
    blocks = length // BLOCK
    rows = in_weight.shape[0]

    slots = jnp.arange(count, dtype=jnp.int32)
    own = jnp.sum(jnp.where(dealing[0][:, None] == slots[None, :], lengths[0][None, :], 0), axis=1)
    ahead = (own[None, :] > own[:, None]) | ((own[None, :] == own[:, None]) & (slots[None, :] < slots[:, None]))
    rank = jnp.sum(ahead.astype(jnp.int32), axis=1)
    place = jnp.where(rank < count // 2, 2 * rank, 2 * (count - 1 - rank) + 1)
    source = jnp.sum(jnp.where(place[None, :] == slots[:, None], slots[None, :], 0), axis=1)
    placed = jnp.sum(jnp.where(place[None, :] == slots[:, None], own[None, :], 0), axis=1)
    chip_lens = lax.dynamic_slice_in_dim(placed, me - core, 2)
    chip_blocks = (chip_lens + BLOCK - 1) // BLOCK
    grid_steps = most_blocks(count, length)

    main = INNER + INNER + 2 * STATE
    gates = halves(in_weight[:, :INNER], 1, group)
    vals = halves(in_weight[:, INNER : 2 * INNER], 1, group)
    both = in_weight[:, 2 * INNER : main]
    steps = halves(in_weight[:, main:], 1, group // HEADDIM)
    pad = jnp.zeros((rows, LANES - heads), BF16)
    shards = jnp.stack([jnp.concatenate([gates[q], vals[q], both, steps[q], pad], axis=1) for q in range(2)])
    aligned = INNER // n >= HEADDIM
    small = jnp.concatenate([norm_gain, conv_weight.reshape(-1), conv_bias, out_gain])
    room = -(-small.shape[0] // (16 * LANES)) * 16
    small = jnp.pad(small, (0, room * LANES - small.shape[0])).reshape(room, LANES)
    tok, win, smalls, sent_grad = start_call(n, source, local_tokens, local_grad, shards, small)
    tok, sent_grad, out_weight = lax.optimization_barrier((tok, sent_grad, out_weight))
    smalls = smalls.reshape(n, -1).astype(F32)
    own_grad = lax.all_to_all(sent_grad, "fsdp", split_axis=0, concat_axis=0, tiled=True)
    if aligned:
        wout = lax.all_gather(out_weight, "fsdp", axis=0, tiled=True, axis_index_groups=columns)
    else:
        whole = lax.all_gather(out_weight, "fsdp", axis=0, tiled=True)
        wout = lax.dynamic_index_in_dim(jnp.stack(halves(whole, 0, group)), core, 0, keepdims=False)
    cuts = [norm_gain.shape[0], conv_weight.size, conv_bias.shape[0], out_gain.shape[0]]
    ends = [sum(cuts[: i + 1]) for i in range(4)]
    first_gain = smalls[:, : ends[0]].reshape(-1)
    conv_w = smalls[:, ends[0] : ends[1]].reshape(n, CONV, -1).transpose(1, 0, 2).reshape(CONV, -1)
    conv_b = smalls[:, ends[1] : ends[2]].reshape(1, -1)
    gated_gain = smalls[:, ends[2] : ends[3]].reshape(1, -1)

    def half_of(array, axis, size):
        return lax.dynamic_index_in_dim(jnp.stack(halves(array, axis, size)), core, 0, keepdims=False)

    conv_all = jnp.concatenate([conv_w, conv_b, jnp.zeros((3, conv_w.shape[1]), F32)], axis=0)
    conv_all = jnp.concatenate([half_of(conv_all[:, :INNER], 1, group), conv_all[:, INNER:]], axis=1)
    head_rows = jnp.stack([dt_bias, jnp.exp(a_log), skip_gain] + [jnp.zeros_like(dt_bias)] * 5)
    head_rows = half_of(head_rows, 1, group // HEADDIM)
    dwide = jnp.repeat(head_rows[2:3], HEADDIM, axis=1)
    hp = jnp.concatenate([head_rows, jnp.zeros((8, LANES - heads), F32)], axis=1)
    og = half_of(gated_gain, 1, group)
    gain = first_gain[None, :]
    cb = conv_all[CONV : CONV + 1]
    args = (gain, win, conv_all, cb, hp, dwide, og)
    gate, cin, raw, y, states, ss, mixing = fwd_call(grid_steps, chip_blocks, tok, *args)

    own_grad, mixing = lax.optimization_barrier((own_grad, mixing))
    cot = pair_call(own_grad.reshape(length, width))
    gm, v, bp = mid_call(grid_steps, chip_blocks, chip_lens, cot, mixing, wout)
    branch, rv = exchange_call(bp, ss, v)

    def restore(part):
        return lax.all_to_all(part.reshape(n, span, width), "fsdp", split_axis=0, concat_axis=0, tiled=True)

    kept = jnp.clip(own - me * span, 0, span)
    branch = restore(branch)
    parts = n // 2
    planes = lax.axis_size("rep")
    fused = aligned and rows % (16 * planes) == 0 and out_weight.shape[0] % (16 * planes) == 0
    chip = (me // 2 if fused else me * 0).reshape(1)
    dy, gp, dog, *early = gate_call(
        grid_steps, chip_blocks, chip_lens, chip, parts, tok, cot, gain, win, gm, og, gate, y, rv
    )
    early, dwout = early[:parts], early[parts:]
    if fused:

        def move(pieces):
            return [pieces[0]] + [
                lax.ppermute(pieces[away], "fsdp", [(d, (d + 2 * away) % n) for d in range(n)])
                for away in range(1, parts)
            ]

        early, dwout = move(early), move(dwout)
    gn, dwin, sums = bwd_call(
        grid_steps, chip_blocks, tok, gain, win, *args[2:6], dog, dy, gp, cin, raw, y, states
    )
    def widen(half, axis, size):
        zero = jnp.zeros_like(half)
        return interleave(jnp.where(core == 0, half, zero), jnp.where(core == 1, half, zero), axis, size)

    own_len = lax.dynamic_slice_in_dim(chip_lens, core, 1)
    if fused:
        output, token_grad, dwin, dwout, sums = finish_call(
            n, planes, group, own_len, place, kept, gn, tok, gain, early, dwin, dwout, sums, local_tokens, local_grad,
            branch,
        )
        dgain = sums[0, CONV + 3, : width // n]
        halves_of = [sums[0], sums[1]]
    else:
        halves_of = [jnp.where(core == q, sums, jnp.zeros_like(sums)) for q in range(2)]
    first, second = halves_of
    dconv = jnp.concatenate(
        [
            interleave(first[: CONV + 1, :inner], second[: CONV + 1, :inner], 1, group),
            first[: CONV + 1, inner:] + second[: CONV + 1, inner:],
        ],
        axis=1,
    )
    dheads = jnp.concatenate(
        [
            interleave(
                first[CONV + 2 : CONV + 3, at : at + heads], second[CONV + 2 : CONV + 3, at : at + heads], 1,
                group // HEADDIM,
            )
            for at in range(0, 3 * LANES, LANES)
        ],
        axis=0,
    )
    dog = interleave(first[CONV + 1, :inner], second[CONV + 1, :inner], 0, group)
    if not fused:
        other = lax.dynamic_index_in_dim(gn, 1 - core, 0, keepdims=False)
        other = lax.ppermute(other, "fsdp", [(2 * c + q, 2 * c + 1 - q) for c in range(n // 2) for q in range(2)])
        mine = lax.dynamic_index_in_dim(gn, core, 0, keepdims=False)
        hidden = lax.dynamic_index_in_dim(tok, core, 0, keepdims=False).astype(F32)
        inv = lax.rsqrt(jnp.mean(hidden * hidden, axis=-1, keepdims=True) + EPS)
        position = jnp.arange(length, dtype=jnp.int32)[:, None]
        grad_normed = jnp.where(position < own_len[0], mine.astype(F32) + other.astype(F32), 0.0)
        dgain = jnp.sum(grad_normed * hidden * inv, axis=0)
        scaled = grad_normed * first_gain[None, :]
        grad_hidden = inv * scaled - hidden * (inv * inv * inv) * jnp.mean(scaled * hidden, axis=-1, keepdims=True)
        back = restore(grad_hidden.astype(BF16))
        dwin = jnp.concatenate([jnp.concatenate(early, axis=0), dwin], axis=1)
        dwout = jnp.concatenate(dwout, axis=0)
        dwin = lax.psum_scatter(
            dwin.astype(F32), "fsdp", scatter_dimension=0, tiled=True, axis_index_groups=columns
        )
        dwin = lax.psum(dwin, "rep").reshape(2, rows, -1)
        dwin = lax.all_to_all(dwin, "fsdp", split_axis=0, concat_axis=0, tiled=True, axis_index_groups=pairs)
        if aligned:
            dwout = lax.psum_scatter(
                dwout.astype(F32), "fsdp", scatter_dimension=0, tiled=True, axis_index_groups=columns
            )
        else:
            wide_grad = widen(dwout.astype(F32), 0, group)
            dwout = lax.psum_scatter(wide_grad, "fsdp", scatter_dimension=0, tiled=True)
        dwout = lax.psum(dwout, "rep")
        c0, c1, c2 = inner, 2 * inner, 2 * inner + 2 * STATE
        dwin = jnp.concatenate(
            [
                interleave(dwin[0, :, :c0], dwin[1, :, :c0], 1, group),
                interleave(dwin[0, :, c0:c1], dwin[1, :, c0:c1], 1, group),
                dwin[0, :, c1:c2] + dwin[1, :, c1:c2],
                interleave(dwin[0, :, c2 : c2 + heads], dwin[1, :, c2 : c2 + heads], 1, group // HEADDIM),
            ],
            axis=1,
        )
        dconv, dheads, dog, dgain = lax.psum((dconv, dheads, dog, dgain), ("rep", "fsdp"))
        dgain = lax.dynamic_slice_in_dim(dgain, me * (width // n), width // n)
        output = combine_call(place, kept, local_tokens, branch)
        token_grad = combine_call(place, kept, local_grad, back)

    def shard(array):
        size = array.shape[-1] // n
        return lax.dynamic_slice_in_dim(array, me * size, size, axis=array.ndim - 1)

    dconv = shard(dconv)
    return (
        output[None], token_grad[None], dgain, dwin, dconv[:CONV], dconv[CONV], dheads[1], dheads[2], dheads[0],
        shard(dog), dwout,
    )


def solution(mesh):
    row = P("rep", None, "fsdp", None)
    per = P("rep", None)
    in_specs = (
        row, row, per, per, P("fsdp"), P("fsdp", None), P(None, "fsdp"), P("fsdp"), P(), P(), P(), P("fsdp"),
        P("fsdp", None),
    )
    out_specs = (
        row, row, P("fsdp"), P("fsdp", None), P(None, "fsdp"), P("fsdp"), P(), P(), P(), P("fsdp"), P("fsdp", None),
    )
    return jax.shard_map(body, mesh=mesh, in_specs=in_specs, out_specs=out_specs, check_vma=False)
```

```python
import functools
import jax
import jax.numpy as jnp
from jax import lax
from jax.experimental import pallas as pl
from jax.experimental.pallas import tpu as pltpu
from jax.sharding import PartitionSpec as P

STATE = 128
HEADDIM = 64
HEADS = 32
INNER = 2048
CONV = 4
BLOCK = 256
CHUNK = 128
LANES = 128
MESH = pl.DeviceIdType.MESH
EPS = 1e-05
F32 = jnp.float32
BF16 = jnp.bfloat16
FAR = -1e9
TILE = 32
NT = (((1,), (1,)), ((), ()))
TN = (((0,), (0,)), ((), ()))


def mm(a, b, dims=(((1,), (0,)), ((), ()))):
    return lax.dot_general(a, b, dims, preferred_element_type=F32)


def two_parts(v):
    high = v.astype(BF16)
    return high, (v - high.astype(F32)).astype(BF16)


def spread(v, expand):
    high, low = two_parts(v)
    return mm(jnp.concatenate([high, low], axis=1), expand)


def gather_heads(v, collect):
    high, low = two_parts(v)
    return mm(high, collect) + mm(low, collect)


def sigmoid(v):
    return 0.5 + 0.5 * jnp.tanh(0.5 * v)


def mm_state(rows, state):
    return mm(jnp.concatenate([rows, rows], axis=1), jnp.concatenate(two_parts(state), axis=0))


def softplus(v):
    return jnp.maximum(v, 0.0) + jnp.log1p(jnp.exp(-jnp.abs(v)))


def three_parts(v):
    high = v.astype(BF16)
    rest = v - high.astype(F32)
    middle = rest.astype(BF16)
    return jnp.concatenate([high, middle, (rest - middle.astype(F32)).astype(BF16)], axis=0)


def triangle(backward):
    rows = lax.broadcasted_iota(jnp.int32, (BLOCK, BLOCK), 0)
    cols = lax.broadcasted_iota(jnp.int32, (BLOCK, BLOCK), 1)
    keep = (cols >= rows) if backward else (rows >= cols)
    tri = (keep & (rows // CHUNK == cols // CHUNK)).astype(F32).astype(BF16)
    return jnp.concatenate([tri, tri, tri], axis=1)


def chunk_rows(c):
    return slice(c * CHUNK, (c + 1) * CHUNK)


def each_last(cum):
    return jnp.concatenate(
        [
            jnp.broadcast_to(cum[(c + 1) * CHUNK - 1 : (c + 1) * CHUNK], (CHUNK, cum.shape[1]))
            for c in range(BLOCK // CHUNK)
        ],
        axis=0,
    )


def causal_sum(log_decay):
    return mm(triangle(False), three_parts(log_decay))


def reverse_sum(v):
    return mm(triangle(True), three_parts(v))


def convolve(cbuf, cw_ref, cb_ref, cols):
    total = cb_ref[0:1, cols] + cw_ref[3:4, cols] * cbuf[8 : 8 + BLOCK, cols]
    for k in range(CONV - 1):
        total = total + cw_ref[k : k + 1, cols] * cbuf[5 + k : 5 + k + BLOCK, cols]
    return total


def where_at(i, nb):
    i = jnp.minimum(i, nb[0] + nb[1] - 1)
    seq = (i >= nb[0]).astype(jnp.int32)
    return seq, i - seq * nb[0]


def most_blocks(count, length):
    blocks, best = length // BLOCK, 0
    for r in range(count // 2):
        for a in range(1, blocks + 1):
            for b in range(1, a + 1):
                upper, lower = (a - 1) * BLOCK + 1, (b - 1) * BLOCK + 1
                if length + r * upper + (count - 1 - 2 * r) * lower + r <= count // 2 * length and (r or a == blocks):
                    best = max(best, a + b)
    return best


def normalize(tok_ref, gain_ref):
    hidden = tok_ref[0].astype(F32)
    scale = lax.rsqrt(jnp.mean(hidden * hidden, axis=1, keepdims=True) + EPS)
    return (hidden * scale * gain_ref[0:1, :]).astype(BF16)


def fwd_kernel(
    inner, heads,
    nb_ref, tok_ref, gain_ref, win_ref, cw_ref, cb_ref, hp_ref, dwide_ref, og_ref,
    gate_ref, cin_ref, raw_ref, y_ref, s_ref, ss_ref, sc_ref,
    cbuf, xbuf, state, expand_ref,
):
    step_id = pl.program_id(0)
    _, blk = where_at(step_id, nb_ref)
    chan = inner + 2 * STATE

    @pl.when(step_id == 0)
    def _():
        fill_expand(expand_ref)

    @pl.when(step_id < nb_ref[0] + nb_ref[1])
    def _():
        @pl.when(blk == 0)
        def _():
            cbuf[0:8, :] = jnp.zeros((8, chan), F32)
            state[...] = jnp.zeros_like(state)

        @pl.when(blk > 0)
        def _():
            cbuf[0:8, :] = cbuf[BLOCK : BLOCK + 8, :]

        normed = normalize(tok_ref, gain_ref)
        for j in range(0, inner, 256):
            gate_ref[0, :, j : j + 256] = mm(normed, win_ref[:, j : j + 256])
        for j in range(0, chan, 256):
            part = mm(normed, win_ref[:, inner + j : inner + j + 256])
            cin_ref[0, :, j : j + 256] = part
            cbuf[8 : 8 + BLOCK, j : j + 256] = part
        raw = mm(normed, win_ref[:, inner + chan :])
        raw_ref[0] = raw
        for j in range(0, chan, 256):
            u = convolve(cbuf, cw_ref, cb_ref, slice(j, j + 256))
            xbuf[:, j : j + 256] = u * sigmoid(u)
        step = softplus(raw + hp_ref[0:1, :])
        log_decay = -step * hp_ref[1:2, :]
        rows = lax.broadcasted_iota(jnp.int32, (CHUNK, CHUNK), 0)
        cols = lax.broadcasted_iota(jnp.int32, (CHUNK, CHUNK), 1)
        causal = rows >= cols
        left = cols < HEADDIM
        cum = causal_sum(log_decay)
        cum_t = cum.T
        three = jnp.concatenate([jnp.exp(cum), step, jnp.exp(each_last(cum) - cum) * step], axis=0)
        wide = spread(three, expand_ref[...])
        e_wide, dt_wide, w_wide = wide[:BLOCK], wide[BLOCK : 2 * BLOCK], wide[2 * BLOCK :]
        all_in = xbuf[:, inner : inner + STATE].astype(BF16)
        all_out = xbuf[:, inner + STATE :].astype(BF16)
        x = xbuf[:, :inner]
        xd = (x * dt_wide).astype(BF16)
        xw = (x * w_wide).astype(BF16)
        crosses = []
        for c in range(BLOCK // CHUNK):
            at = chunk_rows(c)
            crosses.append(mm(all_out[at], all_in[at], NT))
        for p in range(heads // 2):
            lanes = slice(p * 128, (p + 1) * 128)
            for c in range(BLOCK // CHUNK):
                at = chunk_rows(c)
                pair = xd[at, lanes]
                zero = jnp.zeros_like(pair)
                both = jnp.concatenate([jnp.where(left, pair, zero), jnp.where(left, zero, pair)], axis=0)
                parts = []
                for h in (2 * p, 2 * p + 1):
                    gap = cum[at, h : h + 1] - cum_t[h : h + 1, at]
                    parts.append((crosses[c] * jnp.exp(jnp.where(causal, gap, FAR))).astype(BF16))
                y_ref[0, at, lanes] = mm(jnp.concatenate(parts, axis=1), both)
        for c in range(BLOCK // CHUNK):
            at = chunk_rows(c)
            held = state[...]
            s_ref[0, c] = held
            y_ref[0, at, :] += e_wide[at] * mm_state(all_out[at], held)
            last = e_wide[(c + 1) * CHUNK - 1 : (c + 1) * CHUNK]
            state[...] = last * held + mm(all_in[at], xw[at], TN)
        total = jnp.zeros((BLOCK, 1), F32)
        for j in range(0, inner, 256):
            at = slice(j, j + 256)
            gate = gate_ref[0, :, at]
            summed = y_ref[0, :, at] + dwide_ref[0:1, at] * xbuf[:, at]
            y_ref[0, :, at] = summed
            gated = summed * (gate * sigmoid(gate))
            total = total + jnp.sum(gated * gated, axis=1, keepdims=True)
            sc_ref[0, :, at] = (gated * og_ref[0:1, at]).astype(BF16)
        ss_ref[...] = jnp.broadcast_to(total, (BLOCK, 8)).T


def fixed(shape):
    return pl.BlockSpec(shape, lambda *_: (0,) * len(shape), pipeline_mode=pl.Buffered(1))


def fwd_call(steps, nb, tok, gain, win, cw, cb, hp, dwide, og):
    nseq, length, width = tok.shape
    inner = dwide.shape[1]
    heads = inner // HEADDIM
    chan = inner + 2 * STATE
    blocks = length // BLOCK

    def rows(i, nb):
        seq, blk = where_at(i, nb)
        return (seq, blk, 0)

    def srows(i, nb):
        seq, blk = where_at(i, nb)
        return (seq, blk, 0, 0)

    def ssrows(i, nb):
        seq, blk = where_at(i, nb)
        return (seq * blocks + blk, 0)

    grid_spec = pltpu.PrefetchScalarGridSpec(
        num_scalar_prefetch=1,
        grid=(steps,),
        in_specs=[
            pl.BlockSpec((1, BLOCK, width), rows),
            fixed(gain.shape), fixed(win.shape), fixed(cw.shape), fixed(cb.shape),
            fixed(hp.shape), fixed(dwide.shape), fixed(og.shape),
        ],
        out_specs=[
            pl.BlockSpec((1, BLOCK, inner), rows),
            pl.BlockSpec((1, BLOCK, chan), rows),
            pl.BlockSpec((1, BLOCK, LANES), rows),
            pl.BlockSpec((1, BLOCK, inner), rows),
            pl.BlockSpec((1, BLOCK // CHUNK, STATE, inner), srows),
            pl.BlockSpec((8, BLOCK), ssrows),
            pl.BlockSpec((1, BLOCK, inner), rows),
        ],
        scratch_shapes=[
            pltpu.VMEM((BLOCK + 8, chan), F32),
            pltpu.VMEM((BLOCK, chan), F32),
            pltpu.VMEM((STATE, inner), F32),
            pltpu.VMEM((2 * LANES, inner), BF16),
        ],
    )
    shapes = [
        jax.ShapeDtypeStruct((nseq, length, inner), F32),
        jax.ShapeDtypeStruct((nseq, length, chan), F32),
        jax.ShapeDtypeStruct((nseq, length, LANES), F32),
        jax.ShapeDtypeStruct((nseq, length, inner), F32),
        jax.ShapeDtypeStruct((nseq, length // CHUNK, STATE, inner), F32),
        jax.ShapeDtypeStruct((nseq * blocks * 8, BLOCK), F32),
        jax.ShapeDtypeStruct((nseq, length, inner), BF16),
    ]
    return pl.pallas_call(
        functools.partial(fwd_kernel, inner, heads),
        grid_spec=grid_spec,
        out_shape=shapes,
        compiler_params=pltpu.CompilerParams(
            dimension_semantics=("arbitrary",), vmem_limit_bytes=60 * 1024 * 1024
        ),
        cost_estimate=pl.CostEstimate(
            flops=nseq * length * width * (3 * inner + 400), bytes_accessed=60 << 20, transcendentals=0
        ),
        name="layer_forward",
    )(nb, tok, gain, win, cw, cb, hp, dwide, og)


def mid_kernel(nb_ref, len_ref, cot_ref, sc_ref, wout_ref, gm_ref, v_ref, bp_ref):
    seq, blk = where_at(pl.program_id(0), nb_ref)

    @pl.when(pl.program_id(0) < nb_ref[0] + nb_ref[1])
    def _():
        cot = cot_ref[0]
        position = blk * BLOCK + lax.broadcasted_iota(jnp.int32, cot.shape, 0)
        gb = jnp.where(position < len_ref[seq], cot, jnp.zeros_like(cot))
        total = jnp.zeros((BLOCK, 1), F32)
        for j in range(0, sc_ref.shape[2], 256):
            at = slice(j, j + 256)
            gm = mm(gb, wout_ref[at, :], NT)
            gm_ref[0, :, at] = gm
            total = total + jnp.sum(gm * sc_ref[0, :, at].astype(F32), axis=1, keepdims=True)
        v_ref[...] = jnp.broadcast_to(total, (BLOCK, 8)).T
        scaled = sc_ref[0]
        for j in range(0, cot.shape[1], 256):
            bp_ref[0, :, j : j + 256] = mm(scaled, wout_ref[:, j : j + 256]).astype(BF16)


def mid_call(steps, nb, lens, cot, scaled, wout):
    nseq, length, width = cot.shape
    inner = wout.shape[0]
    blocks = length // BLOCK

    def rows(i, nb, lens):
        seq, blk = where_at(i, nb)
        return (seq, blk, 0)

    def vrows(i, nb, lens):
        seq, blk = where_at(i, nb)
        return (seq * blocks + blk, 0)

    return pl.pallas_call(
        mid_kernel,
        grid_spec=pltpu.PrefetchScalarGridSpec(
            num_scalar_prefetch=2,
            grid=(steps,),
            in_specs=[pl.BlockSpec((1, BLOCK, width), rows), pl.BlockSpec((1, BLOCK, inner), rows), fixed(wout.shape)],
            out_specs=[
                pl.BlockSpec((1, BLOCK, inner), rows), pl.BlockSpec((8, BLOCK), vrows),
                pl.BlockSpec((1, BLOCK, width), rows),
            ],
        ),
        out_shape=[
            jax.ShapeDtypeStruct((nseq, length, inner), F32),
            jax.ShapeDtypeStruct((nseq * blocks * 8, BLOCK), F32),
            jax.ShapeDtypeStruct((nseq, length, width), BF16),
        ],
        compiler_params=pltpu.CompilerParams(
            dimension_semantics=("arbitrary",), vmem_limit_bytes=60 * 1024 * 1024
        ),
        cost_estimate=pl.CostEstimate(flops=10**10, bytes_accessed=30 << 20, transcendentals=0),
        name="layer_middle",
    )(nb, lens, cot, scaled, wout)


def gate_kernel(
    parts,
    nb_ref, len_ref, chip_ref, tok_ref, cot_ref, gain_ref, wgate_ref, gm_ref, og_ref, gate_ref, y_ref, rv_ref,
    dy_ref, gp_ref, dog_ref, *refs,
):
    wgate_out, wout_out = refs[:parts], refs[parts : 2 * parts]
    normed_t, dgate_buf, mixed_buf, dwgate, dwout = refs[2 * parts :]
    step_id = pl.program_id(0)
    seq, blk = where_at(step_id, nb_ref)
    inner = gm_ref.shape[2]
    width = tok_ref.shape[2]

    @pl.when(step_id == 0)
    def _():
        dwgate[...] = jnp.zeros_like(dwgate)
        dwout[...] = jnp.zeros_like(dwout)
        dog_ref[...] = jnp.zeros_like(dog_ref)

    @pl.when(step_id < nb_ref[0] + nb_ref[1])
    def _():
        position = blk * BLOCK + lax.broadcasted_iota(jnp.int32, (BLOCK, width), 0)
        cot = cot_ref[0]
        gb = jnp.where(position < len_ref[seq], cot, jnp.zeros_like(cot))
        rv = rv_ref[...].T
        scale, coef = rv[:, 0:1], rv[:, 1:2]
        normed_t[...] = normalize(tok_ref, gain_ref).T
        for j in range(0, inner, 256):
            at = slice(j, j + 256)
            gain = og_ref[0:1, at]
            total = jnp.zeros((8, 256), F32)
            for r in range(0, BLOCK, TILE):
                row = slice(r, r + TILE)
                gm = gm_ref[0, row, at]
                gate = gate_ref[0, row, at]
                sig = sigmoid(gate)
                ysum = y_ref[0, row, at]
                silu = gate * sig
                gated = ysum * silu
                normal = gated * scale[row]
                mixed_buf[row, at] = (normal * gain).astype(BF16)
                product = gm * normal
                for k in range(0, TILE, 8):
                    total = total + product[k : k + 8]
                dgated = scale[row] * (gm * gain) - gated * coef[row]
                dgate_buf[row, at] = (dgated * ysum * (sig + silu * (1.0 - sig))).astype(BF16)
                dy_ref[0, row, at] = dgated * silu
            dog_ref[0:1, at] += jnp.sum(total, axis=0, keepdims=True)
            dwout[at, :] += mm(mixed_buf[:, at], gb, TN)
            dwgate[:, at] += mm(normed_t[...], dgate_buf[:, at])
        for j in range(0, width, 256):
            gp_ref[0, :, j : j + 256] = mm(dgate_buf[...], wgate_ref[j : j + 256, :], NT).astype(BF16)

    @pl.when(step_id == pl.num_programs(0) - 1)
    def _():
        for i in range(parts):
            chip = lax.rem(chip_ref[0] + i, parts)
            for out, total in ((wgate_out[i], dwgate), (wout_out[i], dwout)):
                size = out.shape[0]
                out[...] = total[pl.ds(pl.multiple_of(chip * size, size), size), :].astype(BF16)


def gate_call(steps, nb, lens, chip, parts, tok, cot, gain, win, gm, og, gate, y, rv):
    nseq, length, width = tok.shape
    inner = gm.shape[2]
    blocks = length // BLOCK

    def rows(i, nb, lens, chip):
        seq, blk = where_at(i, nb)
        return (seq, blk, 0)

    def rvrows(i, nb, lens, chip):
        seq, blk = where_at(i, nb)
        return (seq * blocks + blk, 0)

    tall, deep = pl.BlockSpec((1, BLOCK, width), rows), pl.BlockSpec((1, BLOCK, inner), rows)
    return pl.pallas_call(
        functools.partial(gate_kernel, parts),
        grid_spec=pltpu.PrefetchScalarGridSpec(
            num_scalar_prefetch=3,
            grid=(steps,),
            in_specs=[
                tall, tall, fixed(gain.shape), fixed((width, inner)), deep, fixed(og.shape), deep, deep,
                pl.BlockSpec((8, BLOCK), rvrows),
            ],
            out_specs=[deep, tall, fixed((8, inner))]
            + [fixed((width // parts, inner))] * parts
            + [fixed((inner // parts, width))] * parts,
            scratch_shapes=[
                pltpu.VMEM((width, BLOCK), BF16), pltpu.VMEM((BLOCK, inner), BF16), pltpu.VMEM((BLOCK, inner), BF16),
                pltpu.VMEM((width, inner), F32), pltpu.VMEM((inner, width), F32),
            ],
        ),
        out_shape=[
            jax.ShapeDtypeStruct((nseq, length, inner), F32),
            jax.ShapeDtypeStruct((nseq, length, width), BF16),
            jax.ShapeDtypeStruct((8, inner), F32),
        ]
        + [jax.ShapeDtypeStruct((width // parts, inner), BF16)] * parts
        + [jax.ShapeDtypeStruct((inner // parts, width), BF16)] * parts,
        compiler_params=pltpu.CompilerParams(
            dimension_semantics=("arbitrary",), vmem_limit_bytes=60 * 1024 * 1024
        ),
        cost_estimate=pl.CostEstimate(flops=2 * 10**10, bytes_accessed=60 << 20, transcendentals=0),
        name="layer_gate",
    )(nb, lens, chip, tok, cot, gain, win, gm, og, gate, y, rv)


def bwd_kernel(
    inner, heads,
    nb_ref,
    tok_ref, gain_ref, win_ref, cw_ref, cb_ref, hp_ref, dwide_ref, dog_ref, dy_ref, gp_ref, cin_ref, halo_ref, raw_ref, y_ref, s_ref,
    gn_ref, win_out, dcw_ref,
    cbuf, ubuf, dbuf, xbuf, dybuf, dproj, dstate, later, dwin_ref, normed_t, dhp_ref, ddw_ref, expand_ref, collect_ref,
):
    grid_id = pl.program_id(0)
    seq, step_id = where_at(grid_id, nb_ref)
    chan = inner + 2 * STATE
    width = tok_ref.shape[2]
    nb = nb_ref[seq]
    blk = nb - 1 - step_id

    @pl.when(grid_id == 0)
    def _():
        fill_expand(expand_ref)
        fill_collect(collect_ref)
        dwin_ref[...] = jnp.zeros_like(dwin_ref)
        dcw_ref[...] = jnp.zeros_like(dcw_ref)
        dhp_ref[...] = jnp.zeros_like(dhp_ref)
        ddw_ref[...] = jnp.zeros_like(ddw_ref)

    @pl.when(grid_id < nb_ref[0] + nb_ref[1])
    def _():
        @pl.when(step_id == 0)
        def _():
            dbuf[BLOCK : BLOCK + 8, :] = jnp.zeros((8, chan), F32)
            dstate[...] = jnp.zeros_like(dstate)
            later[...] = jnp.zeros_like(later)

        @pl.when(step_id > 0)
        def _():
            dbuf[BLOCK : BLOCK + 8, :] = dbuf[0:8, :]

        @pl.when(blk == 0)
        def _():
            cbuf[0:8, :] = jnp.zeros((8, chan), F32)

        @pl.when(blk > 0)
        def _():
            cbuf[0:8, :] = halo_ref[0]

        cbuf[8 : 8 + BLOCK, :] = cin_ref[0]
        normed_t[...] = normalize(tok_ref, gain_ref).T
        for j in range(0, chan, 256):
            at = slice(j, j + 256)
            u = convolve(cbuf, cw_ref, cb_ref, at)
            sig = sigmoid(u)
            xbuf[:, at] = u * sig
            ubuf[:, at] = sig * (1.0 + u * (1.0 - sig))
        raw = raw_ref[0] + hp_ref[0:1, :]
        step = softplus(raw)
        log_decay = -step * hp_ref[1:2, :]
        rows = lax.broadcasted_iota(jnp.int32, (CHUNK, CHUNK), 0)
        cols = lax.broadcasted_iota(jnp.int32, (CHUNK, CHUNK), 1)
        causal = cols >= rows
        left = cols < HEADDIM
        cum = causal_sum(log_decay)
        cum_t = cum.T
        four = jnp.concatenate([jnp.exp(cum), step, jnp.exp(each_last(cum) - cum)], axis=0)
        wide = spread(four, expand_ref[...])
        e_wide, dt_wide, t_wide = wide[:BLOCK], wide[BLOCK : 2 * BLOCK], wide[2 * BLOCK :]
        all_in = xbuf[:, inner : inner + STATE].astype(BF16)
        all_out = xbuf[:, inner + STATE :].astype(BF16)
        x = xbuf[:, :inner]
        dy = dy_ref[0]
        dy16 = dy.astype(BF16)
        ddw_ref[0:1, :] += jnp.sum(dy * x, axis=0, keepdims=True)
        xd32 = x * dt_wide
        xd = xd32.astype(BF16)
        xw = (xd32 * t_wide).astype(BF16)
        edy = (e_wide * dy).astype(BF16)
        count = BLOCK // CHUNK
        crosses, reaches, outers = [], [], []
        for c in range(count):
            at = chunk_rows(c)
            crosses.append(mm(all_in[at], all_out[at], NT))
            reaches.append(mm_state(all_out[at], s_ref[0, c]))
            outers.append(mm(all_out[at], edy[at], TN))
        dcrosses = [jnp.zeros((CHUNK, CHUNK), F32)] * count
        insides = [[] for _ in range(count)]
        for p in range(heads // 2):
            lanes = slice(p * 128, (p + 1) * 128)
            for c in range(count):
                at = chunk_rows(c)
                pair = xd[at, lanes]
                dpair = dy16[at, lanes]
                zero = jnp.zeros_like(pair)
                both = jnp.concatenate([jnp.where(left, dpair, zero), jnp.where(left, zero, dpair)], axis=0)
                dweights = mm(pair, both, NT)
                parts = []
                for i, h in enumerate((2 * p, 2 * p + 1)):
                    gap = cum_t[h : h + 1, at] - cum[at, h : h + 1]
                    decay = jnp.exp(jnp.where(causal, gap, FAR))
                    parts.append((crosses[c] * decay).astype(BF16))
                    dcrosses[c] = dcrosses[c] + dweights[:, i * CHUNK : (i + 1) * CHUNK] * decay
                insides[c].append(mm(jnp.concatenate(parts, axis=1), both))
        backs, folds = [None] * count, [None] * count
        for c in reversed(range(count)):
            at = chunk_rows(c)
            dheld = dstate[...]
            backs[c] = mm_state(all_in[at], dheld)
            folds[c] = jnp.sum(dheld * later[...], axis=0, keepdims=True)
            later[...] = s_ref[0, c]
            dstate[...] = e_wide[(c + 1) * CHUNK - 1 : (c + 1) * CHUNK] * dheld + outers[c]
            dcross16 = dcrosses[c].astype(BF16)
            ds_in = mm(dcross16, all_out[at]) + mm(xw[at], dheld.astype(BF16), NT)
            ds_out = mm(dcross16, all_in[at], TN) + mm(edy[at], s_ref[0, c].astype(BF16), NT)
            dbuf[at, inner : inner + STATE] = ds_in
            dbuf[at, inner + STATE :] = ds_out
        back = jnp.concatenate(backs, axis=0)
        reach = jnp.concatenate(reaches, axis=0)
        inside = jnp.concatenate([jnp.concatenate(part, axis=1) for part in insides], axis=0)
        dxd = inside + t_wide * back
        dybuf[...] = dt_wide * dxd + dwide_ref[0:1, :] * dy
        scanned = (y_ref[0] - dwide_ref[0:1, :] * x - e_wide * reach) * dy16.astype(F32) + edy.astype(F32) * reach
        scanned = scanned - xd.astype(F32) * inside - xw.astype(F32) * back
        high, low = two_parts(scanned)
        direct_high, direct_low = two_parts(x * dxd)
        rest = [part for fold in folds for part in two_parts(jnp.broadcast_to(fold, (16, inner)))]
        stacked = jnp.concatenate([direct_high, direct_low, high, low] + rest, axis=0)
        small = mm(stacked, collect_ref[...])
        ddirect = small[:BLOCK] + small[BLOCK : 2 * BLOCK]
        dcum = small[2 * BLOCK : 3 * BLOCK] + small[3 * BLOCK : 4 * BLOCK]
        dfold = jnp.concatenate(
            [
                jnp.broadcast_to(
                    small[4 * BLOCK + 32 * c : 4 * BLOCK + 32 * c + 1]
                    + small[4 * BLOCK + 32 * c + 16 : 4 * BLOCK + 32 * c + 17],
                    (CHUNK, LANES),
                )
                for c in range(count)
            ],
            axis=0,
        )
        dlog = reverse_sum(dcum) + dfold
        draw = (ddirect - dlog * hp_ref[1:2, :]) * sigmoid(raw)
        dhp_ref[0:1, :] += jnp.sum(draw, axis=0, keepdims=True)
        dhp_ref[1:2, :] += jnp.sum(dlog * log_decay, axis=0, keepdims=True)
        dproj[:, chan:] = draw.astype(BF16)
        for j in range(0, chan, 256):
            at = slice(j, j + 256)
            grad = dybuf[:, at] if j < inner else dbuf[0:BLOCK, at]
            du = grad * ubuf[:, at]
            dbuf[0:BLOCK, at] = du
            dcw_ref[CONV : CONV + 1, at] += jnp.sum(du, axis=0, keepdims=True)
            for k in range(CONV):
                dcw_ref[k : k + 1, at] += jnp.sum(du * cbuf[5 + k : 5 + k + BLOCK, at], axis=0, keepdims=True)
            dcin = cw_ref[CONV - 1 : CONV, at] * du
            for k in range(CONV - 1):
                dcin = dcin + cw_ref[k : k + 1, at] * dbuf[3 - k : 3 - k + BLOCK, at]
            dcin = dcin.astype(BF16)
            dproj[:, at] = dcin
            dwin_ref[:, at] += mm(normed_t[...], dcin)
        dwin_ref[:, chan:] += mm(normed_t[...], dproj[:, chan:])
        for j in range(0, width, 256):
            at = slice(j, j + 256)
            gn_ref[0, :, at] = (gp_ref[0, :, at].astype(F32) + mm(dproj[...], win_ref[at, inner:], NT)).astype(BF16)

    @pl.when(grid_id == pl.num_programs(0) - 1)
    def _():
        win_out[...] = dwin_ref[...].astype(BF16)
        dcw_ref[CONV + 1 : CONV + 2, :inner] = dog_ref[0:1, :]
        dcw_ref[CONV + 2 : CONV + 3, :LANES] = gather_heads(ddw_ref[...], collect_ref[...])[0:1]
        dcw_ref[CONV + 2 : CONV + 3, LANES : 2 * LANES] = dhp_ref[0:1, :]
        dcw_ref[CONV + 2 : CONV + 3, 2 * LANES : 3 * LANES] = dhp_ref[1:2, :]


def bwd_call(steps, nb, tok, gain, win, cw, cb, hp, dwide, dog, dy, gp, cin, raw, y, s):
    nseq, length, width = tok.shape
    inner = dy.shape[2]
    rest = win.shape[1] - inner
    heads = inner // HEADDIM
    chan = inner + 2 * STATE

    def place(i, nb):
        seq, back = where_at(i, nb)
        return seq, nb[seq] - 1 - back

    def rows(i, nb):
        seq, blk = place(i, nb)
        return (seq, blk, 0)

    def srows(i, nb):
        seq, blk = place(i, nb)
        return (seq, blk, 0, 0)

    def halo(i, nb):
        seq, blk = place(i, nb)
        return (seq, jnp.maximum(blk * (BLOCK // 8) - 1, 0), 0)

    def whole(shape):
        return pl.BlockSpec(shape, lambda *_: (0,) * len(shape), pipeline_mode=pl.Buffered(1))

    grid_spec = pltpu.PrefetchScalarGridSpec(
        num_scalar_prefetch=1,
        grid=(steps,),
        in_specs=[
            pl.BlockSpec((1, BLOCK, width), rows),
            fixed(gain.shape), fixed(win.shape), fixed(cw.shape), fixed(cb.shape),
            fixed(hp.shape), fixed(dwide.shape), fixed(dog.shape),
            pl.BlockSpec((1, BLOCK, inner), rows),
            pl.BlockSpec((1, BLOCK, width), rows),
            pl.BlockSpec((1, BLOCK, chan), rows),
            pl.BlockSpec((1, 8, chan), halo),
            pl.BlockSpec((1, BLOCK, LANES), rows),
            pl.BlockSpec((1, BLOCK, inner), rows),
            pl.BlockSpec((1, BLOCK // CHUNK, STATE, inner), srows),
        ],
        out_specs=[
            pl.BlockSpec((1, BLOCK, width), rows),
            whole((width, rest)), whole((8, chan)),
        ],
        scratch_shapes=[
            pltpu.VMEM((BLOCK + 8, chan), F32),
            pltpu.VMEM((BLOCK, chan), F32),
            pltpu.VMEM((BLOCK + 8, chan), F32),
            pltpu.VMEM((BLOCK, chan), F32),
            pltpu.VMEM((BLOCK, inner), F32),
            pltpu.VMEM((BLOCK, rest), BF16),
            pltpu.VMEM((STATE, inner), F32),
            pltpu.VMEM((STATE, inner), F32),
            pltpu.VMEM((width, rest), F32),
            pltpu.VMEM((width, BLOCK), BF16),
            pltpu.VMEM((8, LANES), F32),
            pltpu.VMEM((8, inner), F32),
            pltpu.VMEM((2 * LANES, inner), BF16),
            pltpu.VMEM((inner, LANES), BF16),
        ],
    )
    shapes = [
        jax.ShapeDtypeStruct((nseq, length, width), BF16),
        jax.ShapeDtypeStruct((width, rest), BF16),
        jax.ShapeDtypeStruct((8, chan), F32),
    ]
    return pl.pallas_call(
        functools.partial(bwd_kernel, inner, heads),
        grid_spec=grid_spec,
        out_shape=shapes,
        compiler_params=pltpu.CompilerParams(
            dimension_semantics=("arbitrary",), vmem_limit_bytes=63 * 1024 * 1024
        ),
        cost_estimate=pl.CostEstimate(
            flops=10**11, bytes_accessed=100 << 20, transcendentals=0
        ),
        name="layer_backward",
    )(nb, tok, gain, win, cw, cb, hp, dwide, dog, dy, gp, cin, cin, raw, y, s)


def fill_expand(expand):
    owner = lax.broadcasted_iota(jnp.int32, expand.shape, 1) // HEADDIM
    head = lax.rem(lax.broadcasted_iota(jnp.int32, expand.shape, 0), LANES)
    expand[...] = (owner == head).astype(F32).astype(BF16)


def fill_collect(collect):
    owner = lax.broadcasted_iota(jnp.int32, collect.shape, 0) // HEADDIM
    head = lax.broadcasted_iota(jnp.int32, collect.shape, 1)
    collect[...] = (owner == head).astype(F32).astype(BF16)


def combine_kernel(place_ref, count_ref, base_ref, part_ref, out_ref):
    kept = count_ref[pl.program_id(0)]
    base = base_ref[0]
    row = lax.broadcasted_iota(jnp.int32, base.shape, 0)
    part = jnp.where(row < kept, part_ref[0].astype(F32), 0.0)
    out_ref[0] = (base.astype(F32) + part).astype(BF16)


def combine_call(place, kept, base, part):
    count, span, width = base.shape
    block = (1, span, width)
    return pl.pallas_call(
        combine_kernel,
        grid_spec=pltpu.PrefetchScalarGridSpec(
            num_scalar_prefetch=2,
            grid=(count,),
            in_specs=[
                pl.BlockSpec(block, lambda s, place, kept: (s, 0, 0)),
                pl.BlockSpec(block, lambda s, place, kept: (place[s], 0, 0)),
            ],
            out_specs=pl.BlockSpec(block, lambda s, place, kept: (s, 0, 0)),
        ),
        out_shape=jax.ShapeDtypeStruct(base.shape, BF16),
        name="combine",
    )(place, kept, base, part)


def peers_of(n):
    return [(away, turn) for away in range(n // 2) for turn in range(2) if away or turn]


def enter(n, me):
    barrier = pltpu.get_barrier_semaphore()
    for away, turn in peers_of(n):
        pl.semaphore_signal(barrier, inc=1, device_id={"fsdp": peer_at(n, me, away, turn)}, device_id_type=MESH)
    pl.semaphore_wait(barrier, n - 1)


def peer_at(n, me, away, turn):
    chip = lax.rem(lax.div(me, 2) + away, n // 2)
    return 2 * chip + lax.rem(lax.rem(me, 2) + turn, 2)


def sender_at(n, me, away, turn):
    chip = lax.rem(lax.div(me, 2) + n // 2 - away, n // 2)
    return 2 * chip + lax.rem(lax.rem(me, 2) + turn, 2)


def rows_at(index, size):
    return pl.ds(pl.multiple_of(index * size, size), size)


def start_kernel(
    n, source_ref, tokens, grads, shards, small, tok, win, smalls, sent_grad, rows_in, sent, given, w_held, s_held, here, w_send, w_recv, t_send, t_recv, f_send, f_recv, s_send, s_recv
):
    me = lax.axis_index("fsdp")
    core = lax.rem(me, 2)
    partner = 2 * lax.div(me, 2) + 1 - core
    span, rows = tokens.shape[1], shards.shape[1]
    loads = [
        pltpu.make_async_copy(tokens, rows_in, here.at[0]),
        pltpu.make_async_copy(shards.at[core], w_held, here.at[1]),
        pltpu.make_async_copy(small, s_held, here.at[2]),
    ]
    for copy in loads:
        copy.start()

    def place_rows(index, sent=sent):
        chosen = source_ref[index]
        step = 32

        @pl.loop(0, span // step)
        def _(i):
            at = pl.ds(pl.multiple_of(i * step, step), step)
            sent[index, at, :] = rows_in[chosen, at, :]

    enter(n, me)
    pending = []
    loads[0].wait()
    for index, (away, turn) in enumerate(peers_of(n)):
        peer = peer_at(n, me, away, turn)
        theirs = lax.rem(core + turn, 2)

        def push(src, dst, send, recv):
            copy = pltpu.make_async_remote_copy(
                src_ref=src, dst_ref=dst, send_sem=send, recv_sem=recv, device_id={"fsdp": peer}, device_id_type=MESH
            )
            copy.start()
            pending.append(copy)

        place_rows(peer)
        push(sent.at[peer], tok.at[theirs, rows_at(me, span)], t_send.at[index], t_recv.at[index])
        push(shards.at[theirs], win.at[rows_at(me, rows)], w_send.at[index], w_recv.at[index])
        push(small, smalls.at[me], s_send.at[index], s_recv.at[index])
    place_rows(me)
    for copy in loads[1:]:
        copy.wait()
    local = [
        pltpu.make_async_copy(sent.at[me], tok.at[core, rows_at(me, span)], here.at[0]),
        pltpu.make_async_copy(sent.at[partner], tok.at[1 - core, rows_at(me, span)], here.at[1]),
        pltpu.make_async_copy(w_held, win.at[rows_at(me, rows)], here.at[2]),
        pltpu.make_async_copy(s_held, smalls.at[me], here.at[3]),
    ]
    for copy in local:
        copy.start()
    more = pltpu.make_async_copy(grads, rows_in, here.at[4])
    more.start()

    def forward(index, src, owner):
        copy = pltpu.make_async_remote_copy(
            src_ref=src, dst_ref=tok.at[core, rows_at(owner, span)], send_sem=f_send.at[index],
            recv_sem=f_recv.at[index], device_id={"fsdp": partner}, device_id_type=MESH,
        )
        copy.start()
        return copy

    passed = [forward(0, sent.at[me], me)]
    for index, (away, turn) in enumerate(peers_of(n)):
        owner = sender_at(n, me, away, turn)
        block = tok.at[core, rows_at(owner, span)]
        pltpu.make_async_remote_copy(
            src_ref=block, dst_ref=block, send_sem=t_send.at[index], recv_sem=t_recv.at[index],
            device_id={"fsdp": partner}, device_id_type=MESH,
        ).wait_recv()
        if away:
            passed.append(forward(index, block, owner))
    more.wait()

    @pl.loop(0, n)
    def _(index):
        place_rows(index, given)

    back = pltpu.make_async_copy(given, sent_grad, here.at[4])
    back.start()
    for copy in passed:
        copy.wait()
    for copy in pending:
        copy.wait_send()
    for copy in local:
        copy.wait()
    for index, (away, turn) in enumerate(peers_of(n)):
        owner = sender_at(n, me, away, turn)
        checks = [(win.at[rows_at(owner, rows)], w_send, w_recv), (smalls.at[owner], s_send, s_recv)]
        for block, send, recv in checks:
            pltpu.make_async_remote_copy(
                src_ref=block, dst_ref=block, send_sem=send.at[index], recv_sem=recv.at[index],
                device_id={"fsdp": partner}, device_id_type=MESH,
            ).wait_recv()
    back.wait()


def start_call(n, source, tokens, grads, shards, small):
    span, width = tokens.shape[1:]
    _, rows, wide = shards.shape
    count = n - 1
    anywhere = pl.BlockSpec(memory_space=pl.ANY)
    return pl.pallas_call(
        functools.partial(start_kernel, n),
        out_shape=[
            jax.ShapeDtypeStruct((2, n * span, width), BF16),
            jax.ShapeDtypeStruct((n * rows, wide), BF16),
            jax.ShapeDtypeStruct((n,) + small.shape, BF16),
            jax.ShapeDtypeStruct(tokens.shape, BF16),
        ],
        in_specs=[pl.BlockSpec(memory_space=pltpu.SMEM)] + [anywhere] * 4,
        out_specs=[anywhere] * 4,
        scratch_shapes=[
            pltpu.VMEM(tokens.shape, BF16), pltpu.VMEM(tokens.shape, BF16), pltpu.VMEM(tokens.shape, BF16),
            pltpu.VMEM((rows, wide), BF16), pltpu.VMEM(small.shape, BF16),
        ]
        + [pltpu.SemaphoreType.DMA((5,))] + [pltpu.SemaphoreType.DMA((count,))] * 8,
        compiler_params=pltpu.CompilerParams(
            collective_id=0, has_side_effects=True, vmem_limit_bytes=60 * 1024 * 1024
        ),
        name="start",
    )(source, tokens, grads, shards, small)


def exchange_kernel(
    bp, ss_ref, v_ref, branch, rv_ref, mine, theirs, ss_in, v_in, here, put, b_send, b_recv, s_send, s_recv
):
    me = lax.axis_index("fsdp")
    core = lax.rem(me, 2)
    partner = 2 * lax.div(me, 2) + 1 - core
    length, width = mine.shape
    blocks = length // BLOCK
    barrier = pltpu.get_barrier_semaphore()
    pl.semaphore_signal(barrier, inc=1, device_id={"fsdp": partner}, device_id_type=MESH)
    pl.semaphore_wait(barrier, 1)

    def remote(src, dst, send, recv):
        return pltpu.make_async_remote_copy(
            src_ref=src, dst_ref=dst, send_sem=send, recv_sem=recv, device_id={"fsdp": partner}, device_id_type=MESH
        )

    load = pltpu.make_async_copy(bp.at[core], mine, here.at[0])
    load.start()
    copies = [
        remote(ss_ref, ss_in, s_send.at[0], s_recv.at[0]),
        remote(v_ref, v_in, s_send.at[1], s_recv.at[1]),
    ]
    for b in range(blocks):
        at = pl.ds(b * BLOCK, BLOCK)
        copies.append(remote(bp.at[1 - core, at], theirs.at[at], b_send.at[b], b_recv.at[b]))
    for copy in copies:
        copy.start()
    for copy in copies[:2]:
        copy.wait_recv()
    scale = lax.rsqrt((ss_ref[...] + ss_in[...]) * (1.0 / INNER) + EPS)
    coef = scale * scale * scale * (v_ref[...] + v_in[...]) * (1.0 / INNER)
    sub = lax.rem(lax.broadcasted_iota(jnp.int32, scale.shape, 0), 8)
    rv_ref[...] = jnp.where(sub == 0, scale, coef)
    load.wait()
    puts = []
    for b in range(blocks):
        at = pl.ds(b * BLOCK, BLOCK)
        copies[2 + b].wait_recv()
        rows = rv_ref[pl.ds(pl.multiple_of((core * blocks + b) * 8, 8), 8), :]
        column = jnp.concatenate([rows, jnp.zeros((LANES - 8, BLOCK), F32)], axis=0).T[:, 0:1]
        mine[at, :] = ((mine[at, :].astype(F32) + theirs[at, :].astype(F32)) * column).astype(BF16)
        copy = pltpu.make_async_copy(mine.at[at], branch.at[at], put.at[b])
        copy.start()
        puts.append(copy)
    for copy in copies:
        copy.wait_send()
    for copy in puts:
        copy.wait()


def exchange_call(bp, ss, v):
    _, length, width = bp.shape
    blocks = length // BLOCK
    vmem = pl.BlockSpec(memory_space=pltpu.VMEM)
    anywhere = pl.BlockSpec(memory_space=pl.ANY)
    dma = pltpu.SemaphoreType.DMA
    return pl.pallas_call(
        exchange_kernel,
        out_shape=[jax.ShapeDtypeStruct((length, width), BF16), jax.ShapeDtypeStruct(ss.shape, F32)],
        in_specs=[anywhere, vmem, vmem],
        out_specs=[anywhere, vmem],
        scratch_shapes=[
            pltpu.VMEM((length, width), BF16), pltpu.VMEM((length, width), BF16),
            pltpu.VMEM(ss.shape, F32), pltpu.VMEM(ss.shape, F32),
            dma((1,)), dma((blocks,)), dma((blocks,)), dma((blocks,)), dma((2,)), dma((2,)),
        ],
        compiler_params=pltpu.CompilerParams(
            collective_id=2, has_side_effects=True, vmem_limit_bytes=60 * 1024 * 1024
        ),
        name="exchange",
    )(bp, ss, v)


def pair_kernel(mine, both, own, theirs, load, put, send, recv):
    me = lax.axis_index("fsdp")
    core = lax.rem(me, 2)
    partner = 2 * lax.div(me, 2) + 1 - core
    barrier = pltpu.get_barrier_semaphore()
    pl.semaphore_signal(barrier, inc=1, device_id={"fsdp": partner}, device_id_type=MESH)
    pl.semaphore_wait(barrier, 1)
    parts = send.shape[0]
    size = mine.shape[0] // parts
    slices = [pl.ds(i * size, size) for i in range(parts)]
    loads = [pltpu.make_async_copy(mine.at[at], own.at[at], load.at[i]) for i, at in enumerate(slices)]
    copies = [
        pltpu.make_async_remote_copy(
            src_ref=mine.at[at], dst_ref=theirs.at[at], send_sem=send.at[i], recv_sem=recv.at[i],
            device_id={"fsdp": partner}, device_id_type=MESH,
        )
        for i, at in enumerate(slices)
    ]
    for copy in copies + loads:
        copy.start()
    puts = []
    for i, at in enumerate(slices):
        loads[i].wait()
        puts.append(pltpu.make_async_copy(own.at[at], both.at[core, at], put.at[i]))
        puts[-1].start()
    for i, at in enumerate(slices):
        copies[i].wait()
        puts.append(pltpu.make_async_copy(theirs.at[at], both.at[1 - core, at], put.at[parts + i]))
        puts[-1].start()
    for copy in puts:
        copy.wait()


def pair_call(mine):
    parts = 8
    anywhere = pl.BlockSpec(memory_space=pl.ANY)
    dma = pltpu.SemaphoreType.DMA
    return pl.pallas_call(
        pair_kernel,
        out_shape=jax.ShapeDtypeStruct((2,) + mine.shape, BF16),
        in_specs=[anywhere],
        out_specs=anywhere,
        scratch_shapes=[
            pltpu.VMEM(mine.shape, BF16), pltpu.VMEM(mine.shape, BF16), dma((parts,)), dma((2 * parts,)),
            dma((parts,)), dma((parts,)),
        ],
        compiler_params=pltpu.CompilerParams(
            collective_id=3, has_side_effects=True, vmem_limit_bytes=60 * 1024 * 1024
        ),
        name="pair",
    )(mine)


def finish_kernel(
    n, planes, cuts, groups, length_ref, place_ref, kept_ref, gn, tok, gain_ref, early, dwin, o_early,
    sums, base, base_grad, branch,
    output, token_grad, w_ref, o_ref, sums_ref,
    gn_mine, gn_theirs, hidden, grad, dgain, w_own, w_in, o_own, o_in, w_give, w_pair, w_chip, w_above, w_half, w_cross,
    w_all, o_above, o_half, o_cross, o_all, s_own, s_in, d_in, s_tot, s_above, s_half, s_cross, s_all, back, out_buf, grad_buf, part,
    here, g_send, g_recv, b_send, b_recv, w_send, w_recv, o_send, o_recv, p_send, p_recv,
    s_send, s_recv, d_send, d_recv, a_send, a_recv, c_send, c_recv, f_send, f_recv,
):
    me = lax.axis_index("fsdp")
    level = lax.axis_index("rep")
    core = lax.rem(me, 2)
    chip = lax.div(me, 2)
    partner = 2 * chip + 1 - core
    span = back.shape[1]
    ahead = early[0].shape[1]
    first_cut = 1
    chip_rows = w_own.shape[0]
    rows = chip_rows // 2
    outs = o_own.shape[0]
    middle = (level > 0) & (level < planes - 1)
    inward = jnp.where(level == 0, 1, planes - 2)
    outward = jnp.where(level == 1, 0, planes - 1)
    others = n // 2 - 1
    tile = 16
    barrier = pltpu.get_barrier_semaphore()
    for away, turn in peers_of(n):
        pl.semaphore_signal(barrier, inc=1, device_id={"fsdp": peer_at(n, me, away, turn)}, device_id_type=MESH)
    for up in range(1, planes):
        pl.semaphore_signal(barrier, inc=1, device_id={"rep": lax.rem(level + up, planes)}, device_id_type=MESH)
    pl.semaphore_wait(barrier, n - 1 + planes - 1)

    def remote(src, dst, send, recv, where):
        return pltpu.make_async_remote_copy(
            src_ref=src, dst_ref=dst, send_sem=send, recv_sem=recv, device_id=where, device_id_type=MESH
        )

    def arrived(block, send, recv):
        remote(block, block, send, recv, {"fsdp": partner}).wait_recv()

    pending = []

    def push(src, dst, send, recv, where):
        copy = remote(src, dst, send, recv, where)
        copy.start()
        pending.append(copy)

    chain = []

    def chain_up(k, own, above, half, cross, out, add):
        chain.append((k, own, above, half, cross, out, add))

        @pl.when(jnp.logical_not(middle))
        def _():
            remote(own, above, a_send.at[k], a_recv.at[k], {"rep": inward}).start()

    def chain_cross(k):
        _, own, above, half, cross, _, add = next(item for item in chain if item[0] == k)

        @pl.when(middle)
        def _():
            arrived(above, a_send.at[k], a_recv.at[k])
            add(half, own, above)
            remote(half, cross, c_send.at[k], c_recv.at[k], {"rep": planes - 1 - level}).start()

    def chain_out(k):
        _, _, _, half, cross, out, add = next(item for item in chain if item[0] == k)

        @pl.when(middle)
        def _():
            arrived(cross, c_send.at[k], c_recv.at[k])
            add(out, half, cross)
            remote(out, out, f_send.at[k], f_recv.at[k], {"rep": outward}).start()

    def chain_end(k):
        _, own, above, half, cross, out, _ = next(item for item in chain if item[0] == k)

        @pl.when(middle)
        def _():
            remote(half, cross, c_send.at[k], c_recv.at[k], {"rep": planes - 1 - level}).wait_send()
            remote(out, out, f_send.at[k], f_recv.at[k], {"rep": outward}).wait_send()

        @pl.when(jnp.logical_not(middle))
        def _():
            remote(own, above, a_send.at[k], a_recv.at[k], {"rep": inward}).wait_send()
            arrived(out, f_send.at[k], f_recv.at[k])

    def add_wide(out, x, y):
        @pl.loop(0, rows // 16)
        def _(i):
            at = pl.ds(pl.multiple_of(i * 16, 16), 16)
            for q in range(2):
                out[q, at, :] = (x[q, at, :].astype(F32) + y[q, at, :].astype(F32)).astype(BF16)

    def add_flat(out, x, y):
        @pl.loop(0, outs // 16)
        def _(i):
            at = pl.ds(pl.multiple_of(i * 16, 16), 16)
            out[at, :] = (x[at, :].astype(F32) + y[at, :].astype(F32)).astype(BF16)

    def add_small(out, x, y):
        out[...] = x[...] + y[...]

    loads = [
        pltpu.make_async_copy(early[0], w_own.at[:, pl.ds(0, ahead)], here.at[0]),
        pltpu.make_async_copy(
            dwin.at[rows_at(chip, chip_rows)], w_own.at[:, pl.ds(ahead, dwin.shape[1])], here.at[1]
        ),
        pltpu.make_async_copy(o_early[0], o_own, here.at[2]),
        pltpu.make_async_copy(gn.at[core], gn_mine, here.at[3]),
        pltpu.make_async_copy(tok.at[core], hidden, here.at[4]),
        pltpu.make_async_copy(sums, s_own, here.at[5]),
        pltpu.make_async_copy(base, out_buf, here.at[6]),
        pltpu.make_async_copy(base_grad, grad_buf, here.at[7]),
        pltpu.make_async_copy(branch, part, here.at[8]),
    ]
    for i in range(others):
        loads.append(pltpu.make_async_copy(early[i + 1], w_in.at[i, :, pl.ds(0, ahead)], here.at[9 + 2 * i]))
        loads.append(pltpu.make_async_copy(o_early[i + 1], o_in.at[i], here.at[10 + 2 * i]))
    everyone = [(0, 0)] + peers_of(n)
    for c, cols in enumerate(cuts):
        if c >= first_cut:
            for i in range(others):
                target = {"fsdp": peer_at(n, me, i + 1, 0)}
                other = lax.rem(chip + i + 1, n // 2)
                k = c * others + i
                given = pl.ds(cols.start - ahead, cols.size)
                push(
                    dwin.at[rows_at(other, chip_rows), given], w_in.at[i, :, cols], w_send.at[k], w_recv.at[k],
                    target,
                )
    for copy in loads:
        copy.start()
    for index, (away, turn) in enumerate(everyone):
        if index:
            peer = peer_at(n, me, away, turn)
            push(sums, s_in.at[index - 1], s_send.at[index], s_recv.at[index], {"fsdp": peer})
    for index, (away, turn) in enumerate(everyone):
        block = rows_at(peer_at(n, me, away, turn), span)
        push(gn.at[1 - core, block], gn_theirs.at[block], g_send.at[index], g_recv.at[index], {"fsdp": partner})
    step = 64

    def norm_back(index):
        away, turn = everyone[index]
        target = peer_at(n, me, away, turn)
        block = rows_at(target, span)
        sender_index = everyone.index((away, 1 - turn))
        arrived(gn_theirs.at[block], g_send.at[sender_index], g_recv.at[sender_index])
        first = target * span

        @pl.loop(0, span // step)
        def _(i):
            at = pl.ds(pl.multiple_of(first + i * step, step), step)
            position = first + i * step + lax.broadcasted_iota(jnp.int32, (step, gn_mine.shape[1]), 0)
            total = gn_mine[at, :].astype(F32) + gn_theirs[at, :].astype(F32)
            total = jnp.where(position < length_ref[0], total, 0.0)
            h = hidden[at, :].astype(F32)
            inv = lax.rsqrt(jnp.mean(h * h, axis=1, keepdims=True) + EPS)
            normal = h * inv
            dgain[0:1, :] += jnp.sum(total * normal, axis=0, keepdims=True)
            scaled = total * gain_ref[0:1, :]
            mean = jnp.mean(scaled * normal, axis=1, keepdims=True)
            grad[at, :] = (inv * (scaled - normal * mean)).astype(BF16)

    def give_back(index):
        away, turn = everyone[index]
        peer = peer_at(n, me, away, turn)
        push(grad.at[rows_at(peer, span)], back.at[me], b_send.at[index], b_recv.at[index], {"fsdp": peer})

    def add_up(own, pieces, at, cols):
        total = own[at, cols].astype(F32)
        for i in range(pieces.shape[0]):
            total = total + pieces[i, at, cols].astype(F32)
        return total.astype(BF16)

    def stage_sum(c):
        cols = cuts[c]
        if c >= first_cut:
            for i in range(others):
                k = c * others + i
                arrived(w_in.at[i, :, cols], w_send.at[k], w_recv.at[k])

        @pl.loop(0, rows // tile)
        def _(i):
            at = pl.ds(pl.multiple_of((1 - core) * rows + i * tile, tile), tile)
            w_give[pl.ds(pl.multiple_of(i * tile, tile), tile), cols] = add_up(w_own, w_in, at, cols)

        push(w_give.at[:, cols], w_pair.at[:, cols], p_send.at[c], p_recv.at[c], {"fsdp": partner})

        @pl.loop(0, rows // tile)
        def _(i):
            at = pl.ds(pl.multiple_of(core * rows + i * tile, tile), tile)
            w_chip[core, pl.ds(pl.multiple_of(i * tile, tile), tile), cols] = add_up(w_own, w_in, at, cols)

    def stage_up(c):
        cols = cuts[c]
        arrived(w_pair.at[:, cols], p_send.at[c], p_recv.at[c])
        w_chip[1 - core, :, cols] = w_pair[:, cols]
        chain_up(
            c, w_chip.at[:, :, cols], w_above.at[:, :, cols], w_half.at[:, :, cols], w_cross.at[:, :, cols],
            w_all.at[:, :, cols], add_wide,
        )

    def finish_rows(buf, pieces, s):
        kept = kept_ref[s]
        chosen = place_ref[s]

        @pl.loop(0, span // step)
        def _(i):
            at = pl.ds(pl.multiple_of(i * step, step), step)
            row = i * step + lax.broadcasted_iota(jnp.int32, (step, buf.shape[2]), 0)
            added = jnp.where(row < kept, pieces[chosen, at, :].astype(F32), 0.0)
            buf[s, at, :] = (buf[s, at, :].astype(F32) + added).astype(BF16)

    for copy in loads[:3] + loads[9:]:
        copy.wait()
    stage_sum(0)

    @pl.loop(0, outs // tile)
    def _(i):
        at = pl.ds(pl.multiple_of(i * tile, tile), tile)
        o_own[at, :] = add_up(o_own, o_in, at, slice(None))

    count = len(cuts)
    chain_up(count, o_own, o_above, o_half, o_cross, o_all, add_flat)
    stage_up(0)
    for copy in loads[3:6]:
        copy.wait()
    dgain[...] = jnp.zeros_like(dgain)
    for index in range(n):
        norm_back(index)
    seg = dgain.shape[1] // n
    for index, (away, turn) in enumerate(everyone):
        if index:
            peer = peer_at(n, me, away, turn)
            cols = pl.ds(pl.multiple_of(peer * seg, seg), seg)
            push(dgain.at[:, cols], d_in.at[index - 1], d_send.at[index], d_recv.at[index], {"fsdp": peer})
    chain_cross(count)
    chain_cross(0)
    s_tot[core] = s_own[...]
    s_tot[1 - core] = jnp.zeros_like(s_own)
    for index, (away, turn) in enumerate(everyone):
        if index:
            arrived(s_in.at[index - 1], s_send.at[index], s_recv.at[index])
            arrived(d_in.at[index - 1], d_send.at[index], d_recv.at[index])
            theirs = lax.rem(core + turn, 2)
            s_tot[theirs] = s_tot[theirs] + s_in[index - 1]
    mine = dgain[:, pl.ds(pl.multiple_of(me * seg, seg), seg)]
    for index in range(n - 1):
        mine = mine + d_in[index]
    s_tot[0, CONV + 3 : CONV + 4, 0:seg] = mine[0:1]
    chain_up(count + 1, s_tot, s_above, s_half, s_cross, s_all, add_small)
    waiting = list(range(1, n))
    for c in range(1, count):
        stage_sum(c)
        for index in waiting[: 2 if c < count - 1 else n]:
            give_back(index)
        del waiting[:2]
        stage_up(c)
        if c == 1:
            chain_out(count)
            chain_out(0)
            chain_cross(count + 1)
        else:
            chain_cross(c - 1)
            chain_out(count + 1 if c == 2 else c - 2)
    for copy in loads[6:9]:
        copy.wait()
    for s in range(n):
        finish_rows(out_buf, part, s)
    stores = [pltpu.make_async_copy(out_buf, output, here.at[6])]
    stores[0].start()
    chain_cross(count - 1)
    if count > 2:
        chain_out(count - 2)
    chain_out(count - 1)
    for k in range(count + 2):
        chain_end(k)
    sums_ref[...] = s_all[...]
    inner, group, heads = groups
    for g in range(2 * inner // group):
        q, at = g % 2, g // 2 * group
        w_ref[:, g * group : (g + 1) * group] = w_all[q, :, at : at + group].astype(F32)
        w_ref[:, 2 * inner + g * group : 2 * inner + (g + 1) * group] = (
            w_all[q, :, inner + at : inner + at + group].astype(F32)
        )
    both = w_all[0, :, 2 * inner : 2 * inner + 2 * STATE].astype(F32)
    both = both + w_all[1, :, 2 * inner : 2 * inner + 2 * STATE].astype(F32)
    w_ref[:, 4 * inner : 4 * inner + 2 * STATE] = both
    first = 2 * inner + 2 * STATE
    tails = [w_all[q, :, first : first + LANES].astype(F32) for q in range(2)]
    size = group // HEADDIM
    pieces = [tails[g % 2][:, g // 2 * size : (g // 2 + 1) * size] for g in range(2 * inner // group)]
    w_ref[:, 4 * inner + 2 * STATE :] = jnp.concatenate(pieces, axis=1)
    o_ref[...] = o_all[...].astype(F32)
    for index, (away, turn) in enumerate(everyone):
        if index:
            owner = sender_at(n, me, away, turn)
            arrived(back.at[owner], b_send.at[index], b_recv.at[index])
    back[me] = grad[rows_at(me, span), :]
    for s in range(n):
        finish_rows(grad_buf, back, s)
    stores.append(pltpu.make_async_copy(grad_buf, token_grad, here.at[7]))
    stores[1].start()
    for copy in pending:
        copy.wait_send()
    for copy in stores:
        copy.wait()


def finish_call(
    n, planes, group, length, place, kept, gn, tok, gain, early, dwin, o_early, sums, base, base_grad, branch,
):
    _, total, width = gn.shape
    span = total // n
    ahead = early[0].shape[1]
    wide = ahead + dwin.shape[1]
    inner = (n // 2) * o_early[0].shape[0]
    heads = inner // HEADDIM
    chip_rows, outs = dwin.shape[0] // (n // 2), inner // (n // 2)
    rows = chip_rows // 2
    others = n // 2 - 1
    lane_tiles = dwin.shape[1] // LANES
    late = 3
    bounds = [ahead + (lane_tiles * i + late - 1) // late * LANES for i in range(late + 1)]
    cuts = [pl.ds(0, ahead)] + [pl.ds(bounds[i], bounds[i + 1] - bounds[i]) for i in range(late)]
    pieces = late + 1
    anywhere = pl.BlockSpec(memory_space=pl.ANY)
    vmem = pl.BlockSpec(memory_space=pltpu.VMEM)
    smem = pl.BlockSpec(memory_space=pltpu.SMEM)
    dma = pltpu.SemaphoreType.DMA
    return pl.pallas_call(
        functools.partial(finish_kernel, n, planes, cuts, (inner, group, heads)),
        out_shape=[
            jax.ShapeDtypeStruct((n, span, width), BF16),
            jax.ShapeDtypeStruct((n, span, width), BF16),
            jax.ShapeDtypeStruct((rows, 4 * inner + 2 * STATE + 2 * heads), F32),
            jax.ShapeDtypeStruct((outs, width), F32),
            jax.ShapeDtypeStruct((2,) + sums.shape, F32),
        ],
        in_specs=[smem, smem, smem, anywhere, anywhere, vmem, [anywhere] * len(early), anywhere]
        + [[anywhere] * len(early), anywhere, anywhere, anywhere, anywhere],
        out_specs=[anywhere, anywhere, vmem, vmem, vmem],
        scratch_shapes=[
            pltpu.VMEM((total, width), BF16), pltpu.VMEM((total, width), BF16), pltpu.VMEM((total, width), BF16),
            pltpu.VMEM((total, width), BF16), pltpu.VMEM((8, width), F32),
            pltpu.VMEM((chip_rows, wide), BF16), pltpu.VMEM((others, chip_rows, wide), BF16),
            pltpu.VMEM((outs, width), BF16), pltpu.VMEM((others, outs, width), BF16),
            pltpu.VMEM((rows, wide), BF16), pltpu.VMEM((rows, wide), BF16), pltpu.VMEM((2, rows, wide), BF16),
            pltpu.VMEM((2, rows, wide), BF16), pltpu.VMEM((2, rows, wide), BF16), pltpu.VMEM((2, rows, wide), BF16),
            pltpu.VMEM((2, rows, wide), BF16),
            pltpu.VMEM((outs, width), BF16), pltpu.VMEM((outs, width), BF16), pltpu.VMEM((outs, width), BF16),
            pltpu.VMEM((outs, width), BF16),
            pltpu.VMEM(sums.shape, F32), pltpu.VMEM((n - 1,) + sums.shape, F32),
            pltpu.VMEM((n - 1, 8, LANES), F32), pltpu.VMEM((2,) + sums.shape, F32),
            pltpu.VMEM((2,) + sums.shape, F32), pltpu.VMEM((2,) + sums.shape, F32),
            pltpu.VMEM((2,) + sums.shape, F32), pltpu.VMEM((2,) + sums.shape, F32),
            pltpu.VMEM((n, span, width), BF16), pltpu.VMEM((n, span, width), BF16),
            pltpu.VMEM((n, span, width), BF16), pltpu.VMEM((n, span, width), BF16),
            dma((9 + 2 * others,)), dma((n,)), dma((n,)), dma((n,)), dma((n,)),
            dma((pieces * others,)), dma((pieces * others,)), dma((others,)), dma((others,)),
            dma((pieces,)), dma((pieces,)), dma((n,)), dma((n,)), dma((n,)), dma((n,)),
            dma((pieces + 2,)), dma((pieces + 2,)), dma((pieces + 2,)), dma((pieces + 2,)),
            dma((pieces + 2,)), dma((pieces + 2,)),
        ],
        compiler_params=pltpu.CompilerParams(
            collective_id=1, has_side_effects=True, vmem_limit_bytes=60 * 1024 * 1024
        ),
        name="finish",
    )(length, place, kept, gn, tok, gain, early, dwin, o_early, sums, base, base_grad, branch)


def pairs_of(n):
    return [[2 * c, 2 * c + 1] for c in range(n // 2)]


def columns_of(n):
    return [list(range(q, n, 2)) for q in range(2)]


def halves(array, axis, group):
    shape = array.shape
    view = array.reshape(shape[:axis] + (shape[axis] // (2 * group), 2, group) + shape[axis + 1 :])
    out = []
    for q in range(2):
        part = lax.index_in_dim(view, q, axis + 1, keepdims=False)
        out.append(part.reshape(shape[:axis] + (shape[axis] // 2,) + shape[axis + 1 :]))
    return out


def interleave(first, second, axis, group):
    shape = first.shape
    views = [
        part.reshape(shape[:axis] + (shape[axis] // group, 1, group) + shape[axis + 1 :]) for part in (first, second)
    ]
    return jnp.concatenate(views, axis=axis + 1).reshape(shape[:axis] + (2 * shape[axis],) + shape[axis + 1 :])


def body(
    tokens, cotangent, lengths, dealing, norm_gain, in_weight, conv_weight, conv_bias, dt_bias, a_log, skip_gain,
    out_gain, out_weight,
):
    n = lax.axis_size("fsdp")
    me = lax.axis_index("fsdp")
    core = lax.rem(me, 2)
    pairs, columns = pairs_of(n), columns_of(n)
    local_tokens, local_grad = tokens[0], cotangent[0]
    count, span, width = local_tokens.shape
    length = span * n
    inner = INNER // 2
    heads = HEADS // 2
    group = max(HEADDIM, INNER // n)
    blocks = length // BLOCK
    rows = in_weight.shape[0]

    slots = jnp.arange(count, dtype=jnp.int32)
    own = jnp.sum(jnp.where(dealing[0][:, None] == slots[None, :], lengths[0][None, :], 0), axis=1)
    ahead = (own[None, :] > own[:, None]) | ((own[None, :] == own[:, None]) & (slots[None, :] < slots[:, None]))
    rank = jnp.sum(ahead.astype(jnp.int32), axis=1)
    place = jnp.where(rank < count // 2, 2 * rank, 2 * (count - 1 - rank) + 1)
    source = jnp.sum(jnp.where(place[None, :] == slots[:, None], slots[None, :], 0), axis=1)
    placed = jnp.sum(jnp.where(place[None, :] == slots[:, None], own[None, :], 0), axis=1)
    chip_lens = lax.dynamic_slice_in_dim(placed, me - core, 2)
    chip_blocks = (chip_lens + BLOCK - 1) // BLOCK
    grid_steps = most_blocks(count, length)

    main = INNER + INNER + 2 * STATE
    gates = halves(in_weight[:, :INNER], 1, group)
    vals = halves(in_weight[:, INNER : 2 * INNER], 1, group)
    both = in_weight[:, 2 * INNER : main]
    steps = halves(in_weight[:, main:], 1, group // HEADDIM)
    pad = jnp.zeros((rows, LANES - heads), BF16)
    shards = jnp.stack([jnp.concatenate([gates[q], vals[q], both, steps[q], pad], axis=1) for q in range(2)])
    aligned = INNER // n >= HEADDIM
    small = jnp.concatenate([norm_gain, conv_weight.reshape(-1), conv_bias, out_gain])
    room = -(-small.shape[0] // (16 * LANES)) * 16
    small = jnp.pad(small, (0, room * LANES - small.shape[0])).reshape(room, LANES)
    tok, win, smalls, sent_grad = start_call(n, source, local_tokens, local_grad, shards, small)
    tok, sent_grad, out_weight = lax.optimization_barrier((tok, sent_grad, out_weight))
    smalls = smalls.reshape(n, -1).astype(F32)
    own_grad = lax.all_to_all(sent_grad, "fsdp", split_axis=0, concat_axis=0, tiled=True)
    if aligned:
        wout = lax.all_gather(out_weight, "fsdp", axis=0, tiled=True, axis_index_groups=columns)
    else:
        whole = lax.all_gather(out_weight, "fsdp", axis=0, tiled=True)
        wout = lax.dynamic_index_in_dim(jnp.stack(halves(whole, 0, group)), core, 0, keepdims=False)
    cuts = [norm_gain.shape[0], conv_weight.size, conv_bias.shape[0], out_gain.shape[0]]
    ends = [sum(cuts[: i + 1]) for i in range(4)]
    first_gain = smalls[:, : ends[0]].reshape(-1)
    conv_w = smalls[:, ends[0] : ends[1]].reshape(n, CONV, -1).transpose(1, 0, 2).reshape(CONV, -1)
    conv_b = smalls[:, ends[1] : ends[2]].reshape(1, -1)
    gated_gain = smalls[:, ends[2] : ends[3]].reshape(1, -1)

    def half_of(array, axis, size):
        return lax.dynamic_index_in_dim(jnp.stack(halves(array, axis, size)), core, 0, keepdims=False)

    conv_all = jnp.concatenate([conv_w, conv_b, jnp.zeros((3, conv_w.shape[1]), F32)], axis=0)
    conv_all = jnp.concatenate([half_of(conv_all[:, :INNER], 1, group), conv_all[:, INNER:]], axis=1)
    head_rows = jnp.stack([dt_bias, jnp.exp(a_log), skip_gain] + [jnp.zeros_like(dt_bias)] * 5)
    head_rows = half_of(head_rows, 1, group // HEADDIM)
    dwide = jnp.repeat(head_rows[2:3], HEADDIM, axis=1)
    hp = jnp.concatenate([head_rows, jnp.zeros((8, LANES - heads), F32)], axis=1)
    og = half_of(gated_gain, 1, group)
    gain = first_gain[None, :]
    cb = conv_all[CONV : CONV + 1]
    args = (gain, win, conv_all, cb, hp, dwide, og)
    gate, cin, raw, y, states, ss, mixing = fwd_call(grid_steps, chip_blocks, tok, *args)

    own_grad, mixing = lax.optimization_barrier((own_grad, mixing))
    cot = pair_call(own_grad.reshape(length, width))
    gm, v, bp = mid_call(grid_steps, chip_blocks, chip_lens, cot, mixing, wout)
    branch, rv = exchange_call(bp, ss, v)

    def restore(part):
        return lax.all_to_all(part.reshape(n, span, width), "fsdp", split_axis=0, concat_axis=0, tiled=True)

    kept = jnp.clip(own - me * span, 0, span)
    branch = restore(branch)
    parts = n // 2
    planes = lax.axis_size("rep")
    fused = aligned and planes == 4 and rows % (16 * planes) == 0 and out_weight.shape[0] % (16 * planes) == 0
    chip = (me // 2 if fused else me * 0).reshape(1)
    dy, gp, dog, *early = gate_call(
        grid_steps, chip_blocks, chip_lens, chip, parts, tok, cot, gain, win, gm, og, gate, y, rv
    )
    early, dwout = early[:parts], early[parts:]
    if fused:

        def move(pieces):
            return [pieces[0]] + [
                lax.ppermute(pieces[away], "fsdp", [(d, (d + 2 * away) % n) for d in range(n)])
                for away in range(1, parts)
            ]

        early, dwout = move(early), move(dwout)
    gn, dwin, sums = bwd_call(
        grid_steps, chip_blocks, tok, gain, win, *args[2:6], dog, dy, gp, cin, raw, y, states
    )
    def widen(half, axis, size):
        zero = jnp.zeros_like(half)
        return interleave(jnp.where(core == 0, half, zero), jnp.where(core == 1, half, zero), axis, size)

    own_len = lax.dynamic_slice_in_dim(chip_lens, core, 1)
    if fused:
        output, token_grad, dwin, dwout, sums = finish_call(
            n, planes, group, own_len, place, kept, gn, tok, gain, early, dwin, dwout, sums, local_tokens, local_grad,
            branch,
        )
        dgain = sums[0, CONV + 3, : width // n]
        halves_of = [sums[0], sums[1]]
    else:
        halves_of = [jnp.where(core == q, sums, jnp.zeros_like(sums)) for q in range(2)]
    first, second = halves_of
    dconv = jnp.concatenate(
        [
            interleave(first[: CONV + 1, :inner], second[: CONV + 1, :inner], 1, group),
            first[: CONV + 1, inner:] + second[: CONV + 1, inner:],
        ],
        axis=1,
    )
    dheads = jnp.concatenate(
        [
            interleave(
                first[CONV + 2 : CONV + 3, at : at + heads], second[CONV + 2 : CONV + 3, at : at + heads], 1,
                group // HEADDIM,
            )
            for at in range(0, 3 * LANES, LANES)
        ],
        axis=0,
    )
    dog = interleave(first[CONV + 1, :inner], second[CONV + 1, :inner], 0, group)
    if not fused:
        other = lax.dynamic_index_in_dim(gn, 1 - core, 0, keepdims=False)
        other = lax.ppermute(other, "fsdp", [(2 * c + q, 2 * c + 1 - q) for c in range(n // 2) for q in range(2)])
        mine = lax.dynamic_index_in_dim(gn, core, 0, keepdims=False)
        hidden = lax.dynamic_index_in_dim(tok, core, 0, keepdims=False).astype(F32)
        inv = lax.rsqrt(jnp.mean(hidden * hidden, axis=-1, keepdims=True) + EPS)
        position = jnp.arange(length, dtype=jnp.int32)[:, None]
        grad_normed = jnp.where(position < own_len[0], mine.astype(F32) + other.astype(F32), 0.0)
        dgain = jnp.sum(grad_normed * hidden * inv, axis=0)
        scaled = grad_normed * first_gain[None, :]
        grad_hidden = inv * scaled - hidden * (inv * inv * inv) * jnp.mean(scaled * hidden, axis=-1, keepdims=True)
        back = restore(grad_hidden.astype(BF16))
        dwin = jnp.concatenate([jnp.concatenate(early, axis=0), dwin], axis=1)
        dwout = jnp.concatenate(dwout, axis=0)
        dwin = lax.psum_scatter(
            dwin.astype(F32), "fsdp", scatter_dimension=0, tiled=True, axis_index_groups=columns
        )
        dwin = lax.psum(dwin, "rep").reshape(2, rows, -1)
        dwin = lax.all_to_all(dwin, "fsdp", split_axis=0, concat_axis=0, tiled=True, axis_index_groups=pairs)
        if aligned:
            dwout = lax.psum_scatter(
                dwout.astype(F32), "fsdp", scatter_dimension=0, tiled=True, axis_index_groups=columns
            )
        else:
            wide_grad = widen(dwout.astype(F32), 0, group)
            dwout = lax.psum_scatter(wide_grad, "fsdp", scatter_dimension=0, tiled=True)
        dwout = lax.psum(dwout, "rep")
        c0, c1, c2 = inner, 2 * inner, 2 * inner + 2 * STATE
        dwin = jnp.concatenate(
            [
                interleave(dwin[0, :, :c0], dwin[1, :, :c0], 1, group),
                interleave(dwin[0, :, c0:c1], dwin[1, :, c0:c1], 1, group),
                dwin[0, :, c1:c2] + dwin[1, :, c1:c2],
                interleave(dwin[0, :, c2 : c2 + heads], dwin[1, :, c2 : c2 + heads], 1, group // HEADDIM),
            ],
            axis=1,
        )
        dconv, dheads, dog, dgain = lax.psum((dconv, dheads, dog, dgain), ("rep", "fsdp"))
        dgain = lax.dynamic_slice_in_dim(dgain, me * (width // n), width // n)
        output = combine_call(place, kept, local_tokens, branch)
        token_grad = combine_call(place, kept, local_grad, back)

    def shard(array):
        size = array.shape[-1] // n
        return lax.dynamic_slice_in_dim(array, me * size, size, axis=array.ndim - 1)

    dconv = shard(dconv)
    return (
        output[None], token_grad[None], dgain, dwin, dconv[:CONV], dconv[CONV], dheads[1], dheads[2], dheads[0],
        shard(dog), dwout,
    )


def solution(mesh):
    row = P("rep", None, "fsdp", None)
    per = P("rep", None)
    in_specs = (
        row, row, per, per, P("fsdp"), P("fsdp", None), P(None, "fsdp"), P("fsdp"), P(), P(), P(), P("fsdp"),
        P("fsdp", None),
    )
    out_specs = (
        row, row, P("fsdp"), P("fsdp", None), P(None, "fsdp"), P("fsdp"), P(), P(), P(), P("fsdp"), P("fsdp", None),
    )
    return jax.shard_map(body, mesh=mesh, in_specs=in_specs, out_specs=out_specs, check_vma=False)
```

```python
import functools
import jax
import jax.numpy as jnp
from jax import lax
from jax.experimental import pallas as pl
from jax.experimental.pallas import tpu as pltpu
from jax.sharding import PartitionSpec as P

STATE = 128
HEADDIM = 64
HEADS = 32
INNER = 2048
CONV = 4
BLOCK = 256
CHUNK = 128
LANES = 128
MESH = pl.DeviceIdType.MESH
EPS = 1e-05
F32 = jnp.float32
BF16 = jnp.bfloat16
FAR = -1e9
TILE = 32
NT = (((1,), (1,)), ((), ()))
TN = (((0,), (0,)), ((), ()))


def mm(a, b, dims=(((1,), (0,)), ((), ()))):
    return lax.dot_general(a, b, dims, preferred_element_type=F32)


def two_parts(v):
    high = v.astype(BF16)
    return high, (v - high.astype(F32)).astype(BF16)


def spread(v, expand):
    high, low = two_parts(v)
    return mm(jnp.concatenate([high, low], axis=1), expand)


def gather_heads(v, collect):
    high, low = two_parts(v)
    return mm(high, collect) + mm(low, collect)


def sigmoid(v):
    return 0.5 + 0.5 * jnp.tanh(0.5 * v)


def mm_state(rows, state):
    return mm(jnp.concatenate([rows, rows], axis=1), jnp.concatenate(two_parts(state), axis=0))


def softplus(v):
    return jnp.maximum(v, 0.0) + jnp.log1p(jnp.exp(-jnp.abs(v)))


def three_parts(v):
    high = v.astype(BF16)
    rest = v - high.astype(F32)
    middle = rest.astype(BF16)
    return jnp.concatenate([high, middle, (rest - middle.astype(F32)).astype(BF16)], axis=0)


def triangle(backward):
    rows = lax.broadcasted_iota(jnp.int32, (BLOCK, BLOCK), 0)
    cols = lax.broadcasted_iota(jnp.int32, (BLOCK, BLOCK), 1)
    keep = (cols >= rows) if backward else (rows >= cols)
    tri = (keep & (rows // CHUNK == cols // CHUNK)).astype(F32).astype(BF16)
    return jnp.concatenate([tri, tri, tri], axis=1)


def chunk_rows(c):
    return slice(c * CHUNK, (c + 1) * CHUNK)


def each_last(cum):
    return jnp.concatenate(
        [
            jnp.broadcast_to(cum[(c + 1) * CHUNK - 1 : (c + 1) * CHUNK], (CHUNK, cum.shape[1]))
            for c in range(BLOCK // CHUNK)
        ],
        axis=0,
    )


def causal_sum(log_decay):
    return mm(triangle(False), three_parts(log_decay))


def reverse_sum(v):
    return mm(triangle(True), three_parts(v))


def convolve(cbuf, cw_ref, cb_ref, cols):
    total = cb_ref[0:1, cols] + cw_ref[3:4, cols] * cbuf[8 : 8 + BLOCK, cols]
    for k in range(CONV - 1):
        total = total + cw_ref[k : k + 1, cols] * cbuf[5 + k : 5 + k + BLOCK, cols]
    return total


def where_at(i, nb):
    i = jnp.minimum(i, nb[0] + nb[1] - 1)
    seq = (i >= nb[0]).astype(jnp.int32)
    return seq, i - seq * nb[0]


def most_blocks(count, length):
    blocks, best = length // BLOCK, 0
    for r in range(count // 2):
        for a in range(1, blocks + 1):
            for b in range(1, a + 1):
                upper, lower = (a - 1) * BLOCK + 1, (b - 1) * BLOCK + 1
                if length + r * upper + (count - 1 - 2 * r) * lower + r <= count // 2 * length and (r or a == blocks):
                    best = max(best, a + b)
    return best


def normalize(tok_ref, gain_ref):
    hidden = tok_ref[0].astype(F32)
    scale = lax.rsqrt(jnp.mean(hidden * hidden, axis=1, keepdims=True) + EPS)
    return (hidden * scale * gain_ref[0:1, :]).astype(BF16)


def fwd_kernel(
    inner, heads,
    nb_ref, tok_ref, gain_ref, win_ref, cw_ref, cb_ref, hp_ref, dwide_ref, og_ref,
    gate_ref, cin_ref, raw_ref, y_ref, s_ref, ss_ref, sc_ref,
    cbuf, xbuf, state, expand_ref,
):
    step_id = pl.program_id(0)
    _, blk = where_at(step_id, nb_ref)
    chan = inner + 2 * STATE

    @pl.when(step_id == 0)
    def _():
        fill_expand(expand_ref)

    @pl.when(step_id < nb_ref[0] + nb_ref[1])
    def _():
        @pl.when(blk == 0)
        def _():
            cbuf[0:8, :] = jnp.zeros((8, chan), F32)
            state[...] = jnp.zeros_like(state)

        @pl.when(blk > 0)
        def _():
            cbuf[0:8, :] = cbuf[BLOCK : BLOCK + 8, :]

        normed = normalize(tok_ref, gain_ref)
        for j in range(0, inner, 256):
            gate_ref[0, :, j : j + 256] = mm(normed, win_ref[:, j : j + 256])
        for j in range(0, chan, 256):
            part = mm(normed, win_ref[:, inner + j : inner + j + 256])
            cin_ref[0, :, j : j + 256] = part
            cbuf[8 : 8 + BLOCK, j : j + 256] = part
        raw = mm(normed, win_ref[:, inner + chan :])
        raw_ref[0] = raw
        for j in range(0, chan, 256):
            u = convolve(cbuf, cw_ref, cb_ref, slice(j, j + 256))
            xbuf[:, j : j + 256] = u * sigmoid(u)
        step = softplus(raw + hp_ref[0:1, :])
        log_decay = -step * hp_ref[1:2, :]
        rows = lax.broadcasted_iota(jnp.int32, (CHUNK, CHUNK), 0)
        cols = lax.broadcasted_iota(jnp.int32, (CHUNK, CHUNK), 1)
        causal = rows >= cols
        left = cols < HEADDIM
        cum = causal_sum(log_decay)
        cum_t = cum.T
        three = jnp.concatenate([jnp.exp(cum), step, jnp.exp(each_last(cum) - cum) * step], axis=0)
        wide = spread(three, expand_ref[...])
        e_wide, dt_wide, w_wide = wide[:BLOCK], wide[BLOCK : 2 * BLOCK], wide[2 * BLOCK :]
        all_in = xbuf[:, inner : inner + STATE].astype(BF16)
        all_out = xbuf[:, inner + STATE :].astype(BF16)
        x = xbuf[:, :inner]
        xd = (x * dt_wide).astype(BF16)
        xw = (x * w_wide).astype(BF16)
        crosses = []
        for c in range(BLOCK // CHUNK):
            at = chunk_rows(c)
            crosses.append(mm(all_out[at], all_in[at], NT))
        for p in range(heads // 2):
            lanes = slice(p * 128, (p + 1) * 128)
            for c in range(BLOCK // CHUNK):
                at = chunk_rows(c)
                pair = xd[at, lanes]
                zero = jnp.zeros_like(pair)
                both = jnp.concatenate([jnp.where(left, pair, zero), jnp.where(left, zero, pair)], axis=0)
                parts = []
                for h in (2 * p, 2 * p + 1):
                    gap = cum[at, h : h + 1] - cum_t[h : h + 1, at]
                    parts.append((crosses[c] * jnp.exp(jnp.where(causal, gap, FAR))).astype(BF16))
                y_ref[0, at, lanes] = mm(jnp.concatenate(parts, axis=1), both)
        for c in range(BLOCK // CHUNK):
            at = chunk_rows(c)
            held = state[...]
            s_ref[0, c] = held
            y_ref[0, at, :] += e_wide[at] * mm_state(all_out[at], held)
            last = e_wide[(c + 1) * CHUNK - 1 : (c + 1) * CHUNK]
            state[...] = last * held + mm(all_in[at], xw[at], TN)
        total = jnp.zeros((BLOCK, 1), F32)
        for j in range(0, inner, 256):
            at = slice(j, j + 256)
            gate = gate_ref[0, :, at]
            summed = y_ref[0, :, at] + dwide_ref[0:1, at] * xbuf[:, at]
            y_ref[0, :, at] = summed
            gated = summed * (gate * sigmoid(gate))
            total = total + jnp.sum(gated * gated, axis=1, keepdims=True)
            sc_ref[0, :, at] = (gated * og_ref[0:1, at]).astype(BF16)
        ss_ref[...] = jnp.broadcast_to(total, (BLOCK, 8)).T


def fixed(shape):
    return pl.BlockSpec(shape, lambda *_: (0,) * len(shape), pipeline_mode=pl.Buffered(1))


def fwd_call(steps, nb, tok, gain, win, cw, cb, hp, dwide, og):
    nseq, length, width = tok.shape
    inner = dwide.shape[1]
    heads = inner // HEADDIM
    chan = inner + 2 * STATE
    blocks = length // BLOCK

    def rows(i, nb):
        seq, blk = where_at(i, nb)
        return (seq, blk, 0)

    def srows(i, nb):
        seq, blk = where_at(i, nb)
        return (seq, blk, 0, 0)

    def ssrows(i, nb):
        seq, blk = where_at(i, nb)
        return (seq * blocks + blk, 0)

    grid_spec = pltpu.PrefetchScalarGridSpec(
        num_scalar_prefetch=1,
        grid=(steps,),
        in_specs=[
            pl.BlockSpec((1, BLOCK, width), rows),
            fixed(gain.shape), fixed(win.shape), fixed(cw.shape), fixed(cb.shape),
            fixed(hp.shape), fixed(dwide.shape), fixed(og.shape),
        ],
        out_specs=[
            pl.BlockSpec((1, BLOCK, inner), rows),
            pl.BlockSpec((1, BLOCK, chan), rows),
            pl.BlockSpec((1, BLOCK, LANES), rows),
            pl.BlockSpec((1, BLOCK, inner), rows),
            pl.BlockSpec((1, BLOCK // CHUNK, STATE, inner), srows),
            pl.BlockSpec((8, BLOCK), ssrows),
            pl.BlockSpec((1, BLOCK, inner), rows),
        ],
        scratch_shapes=[
            pltpu.VMEM((BLOCK + 8, chan), F32),
            pltpu.VMEM((BLOCK, chan), F32),
            pltpu.VMEM((STATE, inner), F32),
            pltpu.VMEM((2 * LANES, inner), BF16),
        ],
    )
    shapes = [
        jax.ShapeDtypeStruct((nseq, length, inner), F32),
        jax.ShapeDtypeStruct((nseq, length, chan), F32),
        jax.ShapeDtypeStruct((nseq, length, LANES), F32),
        jax.ShapeDtypeStruct((nseq, length, inner), F32),
        jax.ShapeDtypeStruct((nseq, length // CHUNK, STATE, inner), F32),
        jax.ShapeDtypeStruct((nseq * blocks * 8, BLOCK), F32),
        jax.ShapeDtypeStruct((nseq, length, inner), BF16),
    ]
    return pl.pallas_call(
        functools.partial(fwd_kernel, inner, heads),
        grid_spec=grid_spec,
        out_shape=shapes,
        compiler_params=pltpu.CompilerParams(
            dimension_semantics=("arbitrary",), vmem_limit_bytes=60 * 1024 * 1024
        ),
        cost_estimate=pl.CostEstimate(
            flops=nseq * length * width * (3 * inner + 400), bytes_accessed=60 << 20, transcendentals=0
        ),
        name="layer_forward",
    )(nb, tok, gain, win, cw, cb, hp, dwide, og)


def mid_kernel(nb_ref, len_ref, cot_ref, sc_ref, wout_ref, gm_ref, v_ref, bp_ref):
    seq, blk = where_at(pl.program_id(0), nb_ref)

    @pl.when(pl.program_id(0) < nb_ref[0] + nb_ref[1])
    def _():
        cot = cot_ref[0]
        position = blk * BLOCK + lax.broadcasted_iota(jnp.int32, cot.shape, 0)
        gb = jnp.where(position < len_ref[seq], cot, jnp.zeros_like(cot))
        total = jnp.zeros((BLOCK, 1), F32)
        for j in range(0, sc_ref.shape[2], 256):
            at = slice(j, j + 256)
            gm = mm(gb, wout_ref[at, :], NT)
            gm_ref[0, :, at] = gm
            total = total + jnp.sum(gm * sc_ref[0, :, at].astype(F32), axis=1, keepdims=True)
        v_ref[...] = jnp.broadcast_to(total, (BLOCK, 8)).T
        scaled = sc_ref[0]
        for j in range(0, cot.shape[1], 256):
            bp_ref[0, :, j : j + 256] = mm(scaled, wout_ref[:, j : j + 256]).astype(BF16)


def mid_call(steps, nb, lens, cot, scaled, wout):
    nseq, length, width = cot.shape
    inner = wout.shape[0]
    blocks = length // BLOCK

    def rows(i, nb, lens):
        seq, blk = where_at(i, nb)
        return (seq, blk, 0)

    def vrows(i, nb, lens):
        seq, blk = where_at(i, nb)
        return (seq * blocks + blk, 0)

    return pl.pallas_call(
        mid_kernel,
        grid_spec=pltpu.PrefetchScalarGridSpec(
            num_scalar_prefetch=2,
            grid=(steps,),
            in_specs=[pl.BlockSpec((1, BLOCK, width), rows), pl.BlockSpec((1, BLOCK, inner), rows), fixed(wout.shape)],
            out_specs=[
                pl.BlockSpec((1, BLOCK, inner), rows), pl.BlockSpec((8, BLOCK), vrows),
                pl.BlockSpec((1, BLOCK, width), rows),
            ],
        ),
        out_shape=[
            jax.ShapeDtypeStruct((nseq, length, inner), F32),
            jax.ShapeDtypeStruct((nseq * blocks * 8, BLOCK), F32),
            jax.ShapeDtypeStruct((nseq, length, width), BF16),
        ],
        compiler_params=pltpu.CompilerParams(
            dimension_semantics=("arbitrary",), vmem_limit_bytes=60 * 1024 * 1024
        ),
        cost_estimate=pl.CostEstimate(flops=10**10, bytes_accessed=30 << 20, transcendentals=0),
        name="layer_middle",
    )(nb, lens, cot, scaled, wout)


def gate_kernel(
    parts,
    nb_ref, len_ref, chip_ref, tok_ref, cot_ref, gain_ref, wgate_ref, gm_ref, og_ref, gate_ref, y_ref, rv_ref,
    dy_ref, gp_ref, dog_ref, *refs,
):
    wgate_out, wout_out = refs[:parts], refs[parts : 2 * parts]
    normed_t, dgate_buf, mixed_buf, dwgate, dwout = refs[2 * parts :]
    step_id = pl.program_id(0)
    seq, blk = where_at(step_id, nb_ref)
    inner = gm_ref.shape[2]
    width = tok_ref.shape[2]

    @pl.when(step_id == 0)
    def _():
        dwgate[...] = jnp.zeros_like(dwgate)
        dwout[...] = jnp.zeros_like(dwout)
        dog_ref[...] = jnp.zeros_like(dog_ref)

    @pl.when(step_id < nb_ref[0] + nb_ref[1])
    def _():
        position = blk * BLOCK + lax.broadcasted_iota(jnp.int32, (BLOCK, width), 0)
        cot = cot_ref[0]
        gb = jnp.where(position < len_ref[seq], cot, jnp.zeros_like(cot))
        rv = rv_ref[...].T
        scale, coef = rv[:, 0:1], rv[:, 1:2]
        normed_t[...] = normalize(tok_ref, gain_ref).T
        for j in range(0, inner, 256):
            at = slice(j, j + 256)
            gain = og_ref[0:1, at]
            total = jnp.zeros((8, 256), F32)
            for r in range(0, BLOCK, TILE):
                row = slice(r, r + TILE)
                gm = gm_ref[0, row, at]
                gate = gate_ref[0, row, at]
                sig = sigmoid(gate)
                ysum = y_ref[0, row, at]
                silu = gate * sig
                gated = ysum * silu
                normal = gated * scale[row]
                mixed_buf[row, at] = (normal * gain).astype(BF16)
                product = gm * normal
                for k in range(0, TILE, 8):
                    total = total + product[k : k + 8]
                dgated = scale[row] * (gm * gain) - gated * coef[row]
                dgate_buf[row, at] = (dgated * ysum * (sig + silu * (1.0 - sig))).astype(BF16)
                dy_ref[0, row, at] = dgated * silu
            dog_ref[0:1, at] += jnp.sum(total, axis=0, keepdims=True)
            dwout[at, :] += mm(mixed_buf[:, at], gb, TN)
            dwgate[:, at] += mm(normed_t[...], dgate_buf[:, at])
        for j in range(0, width, 256):
            gp_ref[0, :, j : j + 256] = mm(dgate_buf[...], wgate_ref[j : j + 256, :], NT).astype(BF16)

    @pl.when(step_id == pl.num_programs(0) - 1)
    def _():
        for i in range(parts):
            chip = lax.rem(chip_ref[0] + i, parts)
            for out, total in ((wgate_out[i], dwgate), (wout_out[i], dwout)):
                size = out.shape[0]
                out[...] = total[pl.ds(pl.multiple_of(chip * size, size), size), :].astype(BF16)


def gate_call(steps, nb, lens, chip, parts, tok, cot, gain, win, gm, og, gate, y, rv):
    nseq, length, width = tok.shape
    inner = gm.shape[2]
    blocks = length // BLOCK

    def rows(i, nb, lens, chip):
        seq, blk = where_at(i, nb)
        return (seq, blk, 0)

    def rvrows(i, nb, lens, chip):
        seq, blk = where_at(i, nb)
        return (seq * blocks + blk, 0)

    tall, deep = pl.BlockSpec((1, BLOCK, width), rows), pl.BlockSpec((1, BLOCK, inner), rows)
    return pl.pallas_call(
        functools.partial(gate_kernel, parts),
        grid_spec=pltpu.PrefetchScalarGridSpec(
            num_scalar_prefetch=3,
            grid=(steps,),
            in_specs=[
                tall, tall, fixed(gain.shape), fixed((width, inner)), deep, fixed(og.shape), deep, deep,
                pl.BlockSpec((8, BLOCK), rvrows),
            ],
            out_specs=[deep, tall, fixed((8, inner))]
            + [fixed((width // parts, inner))] * parts
            + [fixed((inner // parts, width))] * parts,
            scratch_shapes=[
                pltpu.VMEM((width, BLOCK), BF16), pltpu.VMEM((BLOCK, inner), BF16), pltpu.VMEM((BLOCK, inner), BF16),
                pltpu.VMEM((width, inner), F32), pltpu.VMEM((inner, width), F32),
            ],
        ),
        out_shape=[
            jax.ShapeDtypeStruct((nseq, length, inner), F32),
            jax.ShapeDtypeStruct((nseq, length, width), BF16),
            jax.ShapeDtypeStruct((8, inner), F32),
        ]
        + [jax.ShapeDtypeStruct((width // parts, inner), BF16)] * parts
        + [jax.ShapeDtypeStruct((inner // parts, width), BF16)] * parts,
        compiler_params=pltpu.CompilerParams(
            dimension_semantics=("arbitrary",), vmem_limit_bytes=60 * 1024 * 1024
        ),
        cost_estimate=pl.CostEstimate(flops=2 * 10**10, bytes_accessed=60 << 20, transcendentals=0),
        name="layer_gate",
    )(nb, lens, chip, tok, cot, gain, win, gm, og, gate, y, rv)


def bwd_kernel(
    inner, heads,
    nb_ref,
    tok_ref, gain_ref, win_ref, cw_ref, cb_ref, hp_ref, dwide_ref, dog_ref, dy_ref, gp_ref, cin_ref, halo_ref, raw_ref, y_ref, s_ref,
    gn_ref, win_out, dcw_ref,
    cbuf, ubuf, dbuf, xbuf, dybuf, dproj, dstate, later, dwin_ref, normed_t, dhp_ref, ddw_ref, expand_ref, collect_ref,
):
    grid_id = pl.program_id(0)
    seq, step_id = where_at(grid_id, nb_ref)
    chan = inner + 2 * STATE
    width = tok_ref.shape[2]
    nb = nb_ref[seq]
    blk = nb - 1 - step_id

    @pl.when(grid_id == 0)
    def _():
        fill_expand(expand_ref)
        fill_collect(collect_ref)
        dwin_ref[...] = jnp.zeros_like(dwin_ref)
        dcw_ref[...] = jnp.zeros_like(dcw_ref)
        dhp_ref[...] = jnp.zeros_like(dhp_ref)
        ddw_ref[...] = jnp.zeros_like(ddw_ref)

    @pl.when(grid_id < nb_ref[0] + nb_ref[1])
    def _():
        @pl.when(step_id == 0)
        def _():
            dbuf[BLOCK : BLOCK + 8, :] = jnp.zeros((8, chan), F32)
            dstate[...] = jnp.zeros_like(dstate)
            later[...] = jnp.zeros_like(later)

        @pl.when(step_id > 0)
        def _():
            dbuf[BLOCK : BLOCK + 8, :] = dbuf[0:8, :]

        @pl.when(blk == 0)
        def _():
            cbuf[0:8, :] = jnp.zeros((8, chan), F32)

        @pl.when(blk > 0)
        def _():
            cbuf[0:8, :] = halo_ref[0]

        cbuf[8 : 8 + BLOCK, :] = cin_ref[0]
        normed_t[...] = normalize(tok_ref, gain_ref).T
        for j in range(0, chan, 256):
            at = slice(j, j + 256)
            u = convolve(cbuf, cw_ref, cb_ref, at)
            sig = sigmoid(u)
            xbuf[:, at] = u * sig
            ubuf[:, at] = sig * (1.0 + u * (1.0 - sig))
        raw = raw_ref[0] + hp_ref[0:1, :]
        step = softplus(raw)
        log_decay = -step * hp_ref[1:2, :]
        rows = lax.broadcasted_iota(jnp.int32, (CHUNK, CHUNK), 0)
        cols = lax.broadcasted_iota(jnp.int32, (CHUNK, CHUNK), 1)
        causal = cols >= rows
        left = cols < HEADDIM
        cum = causal_sum(log_decay)
        cum_t = cum.T
        four = jnp.concatenate([jnp.exp(cum), step, jnp.exp(each_last(cum) - cum)], axis=0)
        wide = spread(four, expand_ref[...])
        e_wide, dt_wide, t_wide = wide[:BLOCK], wide[BLOCK : 2 * BLOCK], wide[2 * BLOCK :]
        all_in = xbuf[:, inner : inner + STATE].astype(BF16)
        all_out = xbuf[:, inner + STATE :].astype(BF16)
        x = xbuf[:, :inner]
        dy = dy_ref[0]
        dy16 = dy.astype(BF16)
        ddw_ref[0:1, :] += jnp.sum(dy * x, axis=0, keepdims=True)
        xd32 = x * dt_wide
        xd = xd32.astype(BF16)
        xw = (xd32 * t_wide).astype(BF16)
        edy = (e_wide * dy).astype(BF16)
        count = BLOCK // CHUNK
        crosses, reaches, outers = [], [], []
        for c in range(count):
            at = chunk_rows(c)
            crosses.append(mm(all_in[at], all_out[at], NT))
            reaches.append(mm_state(all_out[at], s_ref[0, c]))
            outers.append(mm(all_out[at], edy[at], TN))
        dcrosses = [jnp.zeros((CHUNK, CHUNK), F32)] * count
        insides = [[] for _ in range(count)]
        for p in range(heads // 2):
            lanes = slice(p * 128, (p + 1) * 128)
            for c in range(count):
                at = chunk_rows(c)
                pair = xd[at, lanes]
                dpair = dy16[at, lanes]
                zero = jnp.zeros_like(pair)
                both = jnp.concatenate([jnp.where(left, dpair, zero), jnp.where(left, zero, dpair)], axis=0)
                dweights = mm(pair, both, NT)
                parts = []
                for i, h in enumerate((2 * p, 2 * p + 1)):
                    gap = cum_t[h : h + 1, at] - cum[at, h : h + 1]
                    decay = jnp.exp(jnp.where(causal, gap, FAR))
                    parts.append((crosses[c] * decay).astype(BF16))
                    dcrosses[c] = dcrosses[c] + dweights[:, i * CHUNK : (i + 1) * CHUNK] * decay
                insides[c].append(mm(jnp.concatenate(parts, axis=1), both))
        backs, folds = [None] * count, [None] * count
        for c in reversed(range(count)):
            at = chunk_rows(c)
            dheld = dstate[...]
            backs[c] = mm_state(all_in[at], dheld)
            folds[c] = jnp.sum(dheld * later[...], axis=0, keepdims=True)
            later[...] = s_ref[0, c]
            dstate[...] = e_wide[(c + 1) * CHUNK - 1 : (c + 1) * CHUNK] * dheld + outers[c]
            dcross16 = dcrosses[c].astype(BF16)
            ds_in = mm(dcross16, all_out[at]) + mm(xw[at], dheld.astype(BF16), NT)
            ds_out = mm(dcross16, all_in[at], TN) + mm(edy[at], s_ref[0, c].astype(BF16), NT)
            dbuf[at, inner : inner + STATE] = ds_in
            dbuf[at, inner + STATE :] = ds_out
        back = jnp.concatenate(backs, axis=0)
        reach = jnp.concatenate(reaches, axis=0)
        inside = jnp.concatenate([jnp.concatenate(part, axis=1) for part in insides], axis=0)
        dxd = inside + t_wide * back
        dybuf[...] = dt_wide * dxd + dwide_ref[0:1, :] * dy
        scanned = (y_ref[0] - dwide_ref[0:1, :] * x - e_wide * reach) * dy16.astype(F32) + edy.astype(F32) * reach
        scanned = scanned - xd.astype(F32) * inside - xw.astype(F32) * back
        high, low = two_parts(scanned)
        direct_high, direct_low = two_parts(x * dxd)
        rest = [part for fold in folds for part in two_parts(jnp.broadcast_to(fold, (16, inner)))]
        stacked = jnp.concatenate([direct_high, direct_low, high, low] + rest, axis=0)
        small = mm(stacked, collect_ref[...])
        ddirect = small[:BLOCK] + small[BLOCK : 2 * BLOCK]
        dcum = small[2 * BLOCK : 3 * BLOCK] + small[3 * BLOCK : 4 * BLOCK]
        dfold = jnp.concatenate(
            [
                jnp.broadcast_to(
                    small[4 * BLOCK + 32 * c : 4 * BLOCK + 32 * c + 1]
                    + small[4 * BLOCK + 32 * c + 16 : 4 * BLOCK + 32 * c + 17],
                    (CHUNK, LANES),
                )
                for c in range(count)
            ],
            axis=0,
        )
        dlog = reverse_sum(dcum) + dfold
        draw = (ddirect - dlog * hp_ref[1:2, :]) * sigmoid(raw)
        dhp_ref[0:1, :] += jnp.sum(draw, axis=0, keepdims=True)
        dhp_ref[1:2, :] += jnp.sum(dlog * log_decay, axis=0, keepdims=True)
        dproj[:, chan:] = draw.astype(BF16)
        for j in range(0, chan, 256):
            at = slice(j, j + 256)
            grad = dybuf[:, at] if j < inner else dbuf[0:BLOCK, at]
            du = grad * ubuf[:, at]
            dbuf[0:BLOCK, at] = du
            dcw_ref[CONV : CONV + 1, at] += jnp.sum(du, axis=0, keepdims=True)
            for k in range(CONV):
                dcw_ref[k : k + 1, at] += jnp.sum(du * cbuf[5 + k : 5 + k + BLOCK, at], axis=0, keepdims=True)
            dcin = cw_ref[CONV - 1 : CONV, at] * du
            for k in range(CONV - 1):
                dcin = dcin + cw_ref[k : k + 1, at] * dbuf[3 - k : 3 - k + BLOCK, at]
            dcin = dcin.astype(BF16)
            dproj[:, at] = dcin
            dwin_ref[:, at] += mm(normed_t[...], dcin)
        dwin_ref[:, chan:] += mm(normed_t[...], dproj[:, chan:])
        for j in range(0, width, 256):
            at = slice(j, j + 256)
            gn_ref[0, :, at] = (gp_ref[0, :, at].astype(F32) + mm(dproj[...], win_ref[at, inner:], NT)).astype(BF16)

    @pl.when(grid_id == pl.num_programs(0) - 1)
    def _():
        win_out[...] = dwin_ref[...].astype(BF16)
        dcw_ref[CONV + 1 : CONV + 2, :inner] = dog_ref[0:1, :]
        dcw_ref[CONV + 2 : CONV + 3, :LANES] = gather_heads(ddw_ref[...], collect_ref[...])[0:1]
        dcw_ref[CONV + 2 : CONV + 3, LANES : 2 * LANES] = dhp_ref[0:1, :]
        dcw_ref[CONV + 2 : CONV + 3, 2 * LANES : 3 * LANES] = dhp_ref[1:2, :]


def bwd_call(steps, nb, tok, gain, win, cw, cb, hp, dwide, dog, dy, gp, cin, raw, y, s):
    nseq, length, width = tok.shape
    inner = dy.shape[2]
    rest = win.shape[1] - inner
    heads = inner // HEADDIM
    chan = inner + 2 * STATE

    def place(i, nb):
        seq, back = where_at(i, nb)
        return seq, nb[seq] - 1 - back

    def rows(i, nb):
        seq, blk = place(i, nb)
        return (seq, blk, 0)

    def srows(i, nb):
        seq, blk = place(i, nb)
        return (seq, blk, 0, 0)

    def halo(i, nb):
        seq, blk = place(i, nb)
        return (seq, jnp.maximum(blk * (BLOCK // 8) - 1, 0), 0)

    def whole(shape):
        return pl.BlockSpec(shape, lambda *_: (0,) * len(shape), pipeline_mode=pl.Buffered(1))

    grid_spec = pltpu.PrefetchScalarGridSpec(
        num_scalar_prefetch=1,
        grid=(steps,),
        in_specs=[
            pl.BlockSpec((1, BLOCK, width), rows),
            fixed(gain.shape), fixed(win.shape), fixed(cw.shape), fixed(cb.shape),
            fixed(hp.shape), fixed(dwide.shape), fixed(dog.shape),
            pl.BlockSpec((1, BLOCK, inner), rows),
            pl.BlockSpec((1, BLOCK, width), rows),
            pl.BlockSpec((1, BLOCK, chan), rows),
            pl.BlockSpec((1, 8, chan), halo),
            pl.BlockSpec((1, BLOCK, LANES), rows),
            pl.BlockSpec((1, BLOCK, inner), rows),
            pl.BlockSpec((1, BLOCK // CHUNK, STATE, inner), srows),
        ],
        out_specs=[
            pl.BlockSpec((1, BLOCK, width), rows),
            whole((width, rest)), whole((8, chan)),
        ],
        scratch_shapes=[
            pltpu.VMEM((BLOCK + 8, chan), F32),
            pltpu.VMEM((BLOCK, chan), F32),
            pltpu.VMEM((BLOCK + 8, chan), F32),
            pltpu.VMEM((BLOCK, chan), F32),
            pltpu.VMEM((BLOCK, inner), F32),
            pltpu.VMEM((BLOCK, rest), BF16),
            pltpu.VMEM((STATE, inner), F32),
            pltpu.VMEM((STATE, inner), F32),
            pltpu.VMEM((width, rest), F32),
            pltpu.VMEM((width, BLOCK), BF16),
            pltpu.VMEM((8, LANES), F32),
            pltpu.VMEM((8, inner), F32),
            pltpu.VMEM((2 * LANES, inner), BF16),
            pltpu.VMEM((inner, LANES), BF16),
        ],
    )
    shapes = [
        jax.ShapeDtypeStruct((nseq, length, width), BF16),
        jax.ShapeDtypeStruct((width, rest), BF16),
        jax.ShapeDtypeStruct((8, chan), F32),
    ]
    return pl.pallas_call(
        functools.partial(bwd_kernel, inner, heads),
        grid_spec=grid_spec,
        out_shape=shapes,
        compiler_params=pltpu.CompilerParams(
            dimension_semantics=("arbitrary",), vmem_limit_bytes=63 * 1024 * 1024
        ),
        cost_estimate=pl.CostEstimate(
            flops=10**11, bytes_accessed=100 << 20, transcendentals=0
        ),
        name="layer_backward",
    )(nb, tok, gain, win, cw, cb, hp, dwide, dog, dy, gp, cin, cin, raw, y, s)


def fill_expand(expand):
    owner = lax.broadcasted_iota(jnp.int32, expand.shape, 1) // HEADDIM
    head = lax.rem(lax.broadcasted_iota(jnp.int32, expand.shape, 0), LANES)
    expand[...] = (owner == head).astype(F32).astype(BF16)


def fill_collect(collect):
    owner = lax.broadcasted_iota(jnp.int32, collect.shape, 0) // HEADDIM
    head = lax.broadcasted_iota(jnp.int32, collect.shape, 1)
    collect[...] = (owner == head).astype(F32).astype(BF16)


def combine_kernel(place_ref, count_ref, base_ref, part_ref, out_ref):
    kept = count_ref[pl.program_id(0)]
    base = base_ref[0]
    row = lax.broadcasted_iota(jnp.int32, base.shape, 0)
    part = jnp.where(row < kept, part_ref[0].astype(F32), 0.0)
    out_ref[0] = (base.astype(F32) + part).astype(BF16)


def combine_call(place, kept, base, part):
    count, span, width = base.shape
    block = (1, span, width)
    return pl.pallas_call(
        combine_kernel,
        grid_spec=pltpu.PrefetchScalarGridSpec(
            num_scalar_prefetch=2,
            grid=(count,),
            in_specs=[
                pl.BlockSpec(block, lambda s, place, kept: (s, 0, 0)),
                pl.BlockSpec(block, lambda s, place, kept: (place[s], 0, 0)),
            ],
            out_specs=pl.BlockSpec(block, lambda s, place, kept: (s, 0, 0)),
        ),
        out_shape=jax.ShapeDtypeStruct(base.shape, BF16),
        name="combine",
    )(place, kept, base, part)


def peers_of(n):
    return [(away, turn) for away in range(n // 2) for turn in range(2) if away or turn]


def enter(n, me):
    barrier = pltpu.get_barrier_semaphore()
    for away, turn in peers_of(n):
        pl.semaphore_signal(barrier, inc=1, device_id={"fsdp": peer_at(n, me, away, turn)}, device_id_type=MESH)
    pl.semaphore_wait(barrier, n - 1)


def peer_at(n, me, away, turn):
    chip = lax.rem(lax.div(me, 2) + away, n // 2)
    return 2 * chip + lax.rem(lax.rem(me, 2) + turn, 2)


def sender_at(n, me, away, turn):
    chip = lax.rem(lax.div(me, 2) + n // 2 - away, n // 2)
    return 2 * chip + lax.rem(lax.rem(me, 2) + turn, 2)


def rows_at(index, size):
    return pl.ds(pl.multiple_of(index * size, size), size)


def start_kernel(
    n, source_ref, tokens, grads, shards, small, tok, win, smalls, sent_grad, rows_in, sent, given, w_held, s_held, here, w_send, w_recv, t_send, t_recv, f_send, f_recv, s_send, s_recv
):
    me = lax.axis_index("fsdp")
    core = lax.rem(me, 2)
    partner = 2 * lax.div(me, 2) + 1 - core
    span, rows = tokens.shape[1], shards.shape[1]
    loads = [
        pltpu.make_async_copy(tokens, rows_in, here.at[0]),
        pltpu.make_async_copy(shards.at[core], w_held, here.at[1]),
        pltpu.make_async_copy(small, s_held, here.at[2]),
    ]
    for copy in loads:
        copy.start()

    def place_rows(index, sent=sent):
        chosen = source_ref[index]
        step = 32

        @pl.loop(0, span // step)
        def _(i):
            at = pl.ds(pl.multiple_of(i * step, step), step)
            sent[index, at, :] = rows_in[chosen, at, :]

    enter(n, me)
    pending = []
    loads[0].wait()
    for index, (away, turn) in enumerate(peers_of(n)):
        peer = peer_at(n, me, away, turn)
        theirs = lax.rem(core + turn, 2)

        def push(src, dst, send, recv):
            copy = pltpu.make_async_remote_copy(
                src_ref=src, dst_ref=dst, send_sem=send, recv_sem=recv, device_id={"fsdp": peer}, device_id_type=MESH
            )
            copy.start()
            pending.append(copy)

        place_rows(peer)
        push(sent.at[peer], tok.at[theirs, rows_at(me, span)], t_send.at[index], t_recv.at[index])
        push(shards.at[theirs], win.at[rows_at(me, rows)], w_send.at[index], w_recv.at[index])
        push(small, smalls.at[me], s_send.at[index], s_recv.at[index])
    place_rows(me)
    for copy in loads[1:]:
        copy.wait()
    local = [
        pltpu.make_async_copy(sent.at[me], tok.at[core, rows_at(me, span)], here.at[0]),
        pltpu.make_async_copy(sent.at[partner], tok.at[1 - core, rows_at(me, span)], here.at[1]),
        pltpu.make_async_copy(w_held, win.at[rows_at(me, rows)], here.at[2]),
        pltpu.make_async_copy(s_held, smalls.at[me], here.at[3]),
    ]
    for copy in local:
        copy.start()
    more = pltpu.make_async_copy(grads, rows_in, here.at[4])
    more.start()

    def forward(index, src, owner):
        copy = pltpu.make_async_remote_copy(
            src_ref=src, dst_ref=tok.at[core, rows_at(owner, span)], send_sem=f_send.at[index],
            recv_sem=f_recv.at[index], device_id={"fsdp": partner}, device_id_type=MESH,
        )
        copy.start()
        return copy

    passed = [forward(0, sent.at[me], me)]
    for index, (away, turn) in enumerate(peers_of(n)):
        owner = sender_at(n, me, away, turn)
        block = tok.at[core, rows_at(owner, span)]
        pltpu.make_async_remote_copy(
            src_ref=block, dst_ref=block, send_sem=t_send.at[index], recv_sem=t_recv.at[index],
            device_id={"fsdp": partner}, device_id_type=MESH,
        ).wait_recv()
        if away:
            passed.append(forward(index, block, owner))
    more.wait()

    @pl.loop(0, n)
    def _(index):
        place_rows(index, given)

    back = pltpu.make_async_copy(given, sent_grad, here.at[4])
    back.start()
    for copy in passed:
        copy.wait()
    for copy in pending:
        copy.wait_send()
    for copy in local:
        copy.wait()
    for index, (away, turn) in enumerate(peers_of(n)):
        owner = sender_at(n, me, away, turn)
        checks = [(win.at[rows_at(owner, rows)], w_send, w_recv), (smalls.at[owner], s_send, s_recv)]
        for block, send, recv in checks:
            pltpu.make_async_remote_copy(
                src_ref=block, dst_ref=block, send_sem=send.at[index], recv_sem=recv.at[index],
                device_id={"fsdp": partner}, device_id_type=MESH,
            ).wait_recv()
    back.wait()


def start_call(n, source, tokens, grads, shards, small):
    span, width = tokens.shape[1:]
    _, rows, wide = shards.shape
    count = n - 1
    anywhere = pl.BlockSpec(memory_space=pl.ANY)
    return pl.pallas_call(
        functools.partial(start_kernel, n),
        out_shape=[
            jax.ShapeDtypeStruct((2, n * span, width), BF16),
            jax.ShapeDtypeStruct((n * rows, wide), BF16),
            jax.ShapeDtypeStruct((n,) + small.shape, BF16),
            jax.ShapeDtypeStruct(tokens.shape, BF16),
        ],
        in_specs=[pl.BlockSpec(memory_space=pltpu.SMEM)] + [anywhere] * 4,
        out_specs=[anywhere] * 4,
        scratch_shapes=[
            pltpu.VMEM(tokens.shape, BF16), pltpu.VMEM(tokens.shape, BF16), pltpu.VMEM(tokens.shape, BF16),
            pltpu.VMEM((rows, wide), BF16), pltpu.VMEM(small.shape, BF16),
        ]
        + [pltpu.SemaphoreType.DMA((5,))] + [pltpu.SemaphoreType.DMA((count,))] * 8,
        compiler_params=pltpu.CompilerParams(
            collective_id=0, has_side_effects=True, vmem_limit_bytes=60 * 1024 * 1024
        ),
        name="start",
    )(source, tokens, grads, shards, small)


def exchange_kernel(
    bp, ss_ref, v_ref, branch, rv_ref, mine, theirs, ss_in, v_in, here, put, b_send, b_recv, s_send, s_recv
):
    me = lax.axis_index("fsdp")
    core = lax.rem(me, 2)
    partner = 2 * lax.div(me, 2) + 1 - core
    length, width = mine.shape
    blocks = length // BLOCK
    barrier = pltpu.get_barrier_semaphore()
    pl.semaphore_signal(barrier, inc=1, device_id={"fsdp": partner}, device_id_type=MESH)
    pl.semaphore_wait(barrier, 1)

    def remote(src, dst, send, recv):
        return pltpu.make_async_remote_copy(
            src_ref=src, dst_ref=dst, send_sem=send, recv_sem=recv, device_id={"fsdp": partner}, device_id_type=MESH
        )

    load = pltpu.make_async_copy(bp.at[core], mine, here.at[0])
    load.start()
    copies = [
        remote(ss_ref, ss_in, s_send.at[0], s_recv.at[0]),
        remote(v_ref, v_in, s_send.at[1], s_recv.at[1]),
    ]
    for b in range(blocks):
        at = pl.ds(b * BLOCK, BLOCK)
        copies.append(remote(bp.at[1 - core, at], theirs.at[at], b_send.at[b], b_recv.at[b]))
    for copy in copies:
        copy.start()
    for copy in copies[:2]:
        copy.wait_recv()
    scale = lax.rsqrt((ss_ref[...] + ss_in[...]) * (1.0 / INNER) + EPS)
    coef = scale * scale * scale * (v_ref[...] + v_in[...]) * (1.0 / INNER)
    sub = lax.rem(lax.broadcasted_iota(jnp.int32, scale.shape, 0), 8)
    rv_ref[...] = jnp.where(sub == 0, scale, coef)
    load.wait()
    puts = []
    for b in range(blocks):
        at = pl.ds(b * BLOCK, BLOCK)
        copies[2 + b].wait_recv()
        rows = rv_ref[pl.ds(pl.multiple_of((core * blocks + b) * 8, 8), 8), :]
        column = jnp.concatenate([rows, jnp.zeros((LANES - 8, BLOCK), F32)], axis=0).T[:, 0:1]
        mine[at, :] = ((mine[at, :].astype(F32) + theirs[at, :].astype(F32)) * column).astype(BF16)
        copy = pltpu.make_async_copy(mine.at[at], branch.at[at], put.at[b])
        copy.start()
        puts.append(copy)
    for copy in copies:
        copy.wait_send()
    for copy in puts:
        copy.wait()


def exchange_call(bp, ss, v):
    _, length, width = bp.shape
    blocks = length // BLOCK
    vmem = pl.BlockSpec(memory_space=pltpu.VMEM)
    anywhere = pl.BlockSpec(memory_space=pl.ANY)
    dma = pltpu.SemaphoreType.DMA
    return pl.pallas_call(
        exchange_kernel,
        out_shape=[jax.ShapeDtypeStruct((length, width), BF16), jax.ShapeDtypeStruct(ss.shape, F32)],
        in_specs=[anywhere, vmem, vmem],
        out_specs=[anywhere, vmem],
        scratch_shapes=[
            pltpu.VMEM((length, width), BF16), pltpu.VMEM((length, width), BF16),
            pltpu.VMEM(ss.shape, F32), pltpu.VMEM(ss.shape, F32),
            dma((1,)), dma((blocks,)), dma((blocks,)), dma((blocks,)), dma((2,)), dma((2,)),
        ],
        compiler_params=pltpu.CompilerParams(
            collective_id=2, has_side_effects=True, vmem_limit_bytes=60 * 1024 * 1024
        ),
        name="exchange",
    )(bp, ss, v)


def pair_kernel(mine, both, own, theirs, load, put, send, recv):
    me = lax.axis_index("fsdp")
    core = lax.rem(me, 2)
    partner = 2 * lax.div(me, 2) + 1 - core
    barrier = pltpu.get_barrier_semaphore()
    pl.semaphore_signal(barrier, inc=1, device_id={"fsdp": partner}, device_id_type=MESH)
    pl.semaphore_wait(barrier, 1)
    parts = send.shape[0]
    size = mine.shape[0] // parts
    slices = [pl.ds(i * size, size) for i in range(parts)]
    loads = [pltpu.make_async_copy(mine.at[at], own.at[at], load.at[i]) for i, at in enumerate(slices)]
    copies = [
        pltpu.make_async_remote_copy(
            src_ref=mine.at[at], dst_ref=theirs.at[at], send_sem=send.at[i], recv_sem=recv.at[i],
            device_id={"fsdp": partner}, device_id_type=MESH,
        )
        for i, at in enumerate(slices)
    ]
    for copy in copies + loads:
        copy.start()
    puts = []
    for i, at in enumerate(slices):
        loads[i].wait()
        puts.append(pltpu.make_async_copy(own.at[at], both.at[core, at], put.at[i]))
        puts[-1].start()
    for i, at in enumerate(slices):
        copies[i].wait()
        puts.append(pltpu.make_async_copy(theirs.at[at], both.at[1 - core, at], put.at[parts + i]))
        puts[-1].start()
    for copy in puts:
        copy.wait()


def pair_call(mine):
    parts = 8
    anywhere = pl.BlockSpec(memory_space=pl.ANY)
    dma = pltpu.SemaphoreType.DMA
    return pl.pallas_call(
        pair_kernel,
        out_shape=jax.ShapeDtypeStruct((2,) + mine.shape, BF16),
        in_specs=[anywhere],
        out_specs=anywhere,
        scratch_shapes=[
            pltpu.VMEM(mine.shape, BF16), pltpu.VMEM(mine.shape, BF16), dma((parts,)), dma((2 * parts,)),
            dma((parts,)), dma((parts,)),
        ],
        compiler_params=pltpu.CompilerParams(
            collective_id=3, has_side_effects=True, vmem_limit_bytes=60 * 1024 * 1024
        ),
        name="pair",
    )(mine)


def finish_kernel(
    n, planes, cuts, groups, length_ref, place_ref, kept_ref, gn, tok, gain_ref, early, dwin, o_early,
    sums, base, base_grad, branch,
    output, token_grad, w_ref, o_ref, sums_ref,
    gn_mine, gn_theirs, hidden, grad, dgain, w_own, w_in, o_own, o_in, w_give, w_pair, w_chip, w_above, w_half, w_cross,
    w_all, o_above, o_half, o_cross, o_all, s_own, s_in, d_in, s_tot, s_above, s_half, s_cross, s_all, back, out_buf, grad_buf, part,
    here, g_send, g_recv, b_send, b_recv, w_send, w_recv, o_send, o_recv, p_send, p_recv,
    s_send, s_recv, d_send, d_recv, a_send, a_recv, c_send, c_recv, f_send, f_recv,
):
    me = lax.axis_index("fsdp")
    level = lax.axis_index("rep")
    core = lax.rem(me, 2)
    chip = lax.div(me, 2)
    partner = 2 * chip + 1 - core
    span = back.shape[1]
    ahead = early[0].shape[1]
    first_cut = 1
    chip_rows = w_own.shape[0]
    rows = chip_rows // 2
    outs = o_own.shape[0]
    middle = (level > 0) & (level < planes - 1)
    inward = jnp.where(level == 0, 1, planes - 2)
    outward = jnp.where(level == 1, 0, planes - 1)
    others = n // 2 - 1
    tile = 16
    barrier = pltpu.get_barrier_semaphore()
    for away, turn in peers_of(n):
        pl.semaphore_signal(barrier, inc=1, device_id={"fsdp": peer_at(n, me, away, turn)}, device_id_type=MESH)
    for up in range(1, planes):
        pl.semaphore_signal(barrier, inc=1, device_id={"rep": lax.rem(level + up, planes)}, device_id_type=MESH)
    pl.semaphore_wait(barrier, n - 1 + planes - 1)

    def remote(src, dst, send, recv, where):
        return pltpu.make_async_remote_copy(
            src_ref=src, dst_ref=dst, send_sem=send, recv_sem=recv, device_id=where, device_id_type=MESH
        )

    def arrived(block, send, recv):
        remote(block, block, send, recv, {"fsdp": partner}).wait_recv()

    pending = []

    def push(src, dst, send, recv, where):
        copy = remote(src, dst, send, recv, where)
        copy.start()
        pending.append(copy)

    chain = []

    def chain_up(k, own, above, half, cross, out, add):
        chain.append((k, own, above, half, cross, out, add))

        @pl.when(jnp.logical_not(middle))
        def _():
            remote(own, above, a_send.at[k], a_recv.at[k], {"rep": inward}).start()

    def chain_cross(k):
        _, own, above, half, cross, _, add = next(item for item in chain if item[0] == k)

        @pl.when(middle)
        def _():
            arrived(above, a_send.at[k], a_recv.at[k])
            add(half, own, above)
            remote(half, cross, c_send.at[k], c_recv.at[k], {"rep": planes - 1 - level}).start()

    def chain_out(k):
        _, _, _, half, cross, out, add = next(item for item in chain if item[0] == k)

        @pl.when(middle)
        def _():
            arrived(cross, c_send.at[k], c_recv.at[k])
            add(out, half, cross)
            remote(out, out, f_send.at[k], f_recv.at[k], {"rep": outward}).start()

    def chain_end(k):
        _, own, above, half, cross, out, _ = next(item for item in chain if item[0] == k)

        @pl.when(middle)
        def _():
            remote(half, cross, c_send.at[k], c_recv.at[k], {"rep": planes - 1 - level}).wait_send()
            remote(out, out, f_send.at[k], f_recv.at[k], {"rep": outward}).wait_send()

        @pl.when(jnp.logical_not(middle))
        def _():
            remote(own, above, a_send.at[k], a_recv.at[k], {"rep": inward}).wait_send()
            arrived(out, f_send.at[k], f_recv.at[k])

    def add_wide(out, x, y):
        @pl.loop(0, rows // 16)
        def _(i):
            at = pl.ds(pl.multiple_of(i * 16, 16), 16)
            for q in range(2):
                out[q, at, :] = (x[q, at, :].astype(F32) + y[q, at, :].astype(F32)).astype(BF16)

    def add_flat(out, x, y):
        @pl.loop(0, outs // 16)
        def _(i):
            at = pl.ds(pl.multiple_of(i * 16, 16), 16)
            out[at, :] = (x[at, :].astype(F32) + y[at, :].astype(F32)).astype(BF16)

    def add_small(out, x, y):
        out[...] = x[...] + y[...]

    loads = [
        pltpu.make_async_copy(early[0], w_own.at[:, pl.ds(0, ahead)], here.at[0]),
        pltpu.make_async_copy(
            dwin.at[rows_at(chip, chip_rows)], w_own.at[:, pl.ds(ahead, dwin.shape[1])], here.at[1]
        ),
        pltpu.make_async_copy(o_early[0], o_own, here.at[2]),
        pltpu.make_async_copy(gn.at[core], gn_mine, here.at[3]),
        pltpu.make_async_copy(tok.at[core], hidden, here.at[4]),
        pltpu.make_async_copy(sums, s_own, here.at[5]),
        pltpu.make_async_copy(base, out_buf, here.at[6]),
        pltpu.make_async_copy(base_grad, grad_buf, here.at[7]),
        pltpu.make_async_copy(branch, part, here.at[8]),
    ]
    for i in range(others):
        loads.append(pltpu.make_async_copy(early[i + 1], w_in.at[i, :, pl.ds(0, ahead)], here.at[9 + 2 * i]))
        loads.append(pltpu.make_async_copy(o_early[i + 1], o_in.at[i], here.at[10 + 2 * i]))
    everyone = [(0, 0)] + peers_of(n)
    for c, cols in enumerate(cuts):
        if c >= first_cut:
            for i in range(others):
                target = {"fsdp": peer_at(n, me, i + 1, 0)}
                other = lax.rem(chip + i + 1, n // 2)
                k = c * others + i
                given = pl.ds(cols.start - ahead, cols.size)
                push(
                    dwin.at[rows_at(other, chip_rows), given], w_in.at[i, :, cols], w_send.at[k], w_recv.at[k],
                    target,
                )
    for copy in loads:
        copy.start()
    for index, (away, turn) in enumerate(everyone):
        if index:
            peer = peer_at(n, me, away, turn)
            push(sums, s_in.at[index - 1], s_send.at[index], s_recv.at[index], {"fsdp": peer})
    for index, (away, turn) in enumerate(everyone):
        block = rows_at(peer_at(n, me, away, turn), span)
        push(gn.at[1 - core, block], gn_theirs.at[block], g_send.at[index], g_recv.at[index], {"fsdp": partner})
    step = 64

    def norm_back(index):
        away, turn = everyone[index]
        target = peer_at(n, me, away, turn)
        block = rows_at(target, span)
        sender_index = everyone.index((away, 1 - turn))
        arrived(gn_theirs.at[block], g_send.at[sender_index], g_recv.at[sender_index])
        first = target * span

        @pl.loop(0, span // step)
        def _(i):
            at = pl.ds(pl.multiple_of(first + i * step, step), step)
            position = first + i * step + lax.broadcasted_iota(jnp.int32, (step, gn_mine.shape[1]), 0)
            total = gn_mine[at, :].astype(F32) + gn_theirs[at, :].astype(F32)
            total = jnp.where(position < length_ref[0], total, 0.0)
            h = hidden[at, :].astype(F32)
            inv = lax.rsqrt(jnp.mean(h * h, axis=1, keepdims=True) + EPS)
            normal = h * inv
            dgain[0:1, :] += jnp.sum(total * normal, axis=0, keepdims=True)
            scaled = total * gain_ref[0:1, :]
            mean = jnp.mean(scaled * normal, axis=1, keepdims=True)
            grad[at, :] = (inv * (scaled - normal * mean)).astype(BF16)

    def give_back(index):
        away, turn = everyone[index]
        peer = peer_at(n, me, away, turn)
        push(grad.at[rows_at(peer, span)], back.at[me], b_send.at[index], b_recv.at[index], {"fsdp": peer})

    def add_up(own, pieces, at, cols):
        total = own[at, cols].astype(F32)
        for i in range(pieces.shape[0]):
            total = total + pieces[i, at, cols].astype(F32)
        return total.astype(BF16)

    def stage_sum(c):
        cols = cuts[c]
        if c >= first_cut:
            for i in range(others):
                k = c * others + i
                arrived(w_in.at[i, :, cols], w_send.at[k], w_recv.at[k])

        @pl.loop(0, rows // tile)
        def _(i):
            at = pl.ds(pl.multiple_of((1 - core) * rows + i * tile, tile), tile)
            w_give[pl.ds(pl.multiple_of(i * tile, tile), tile), cols] = add_up(w_own, w_in, at, cols)

        push(w_give.at[:, cols], w_pair.at[:, cols], p_send.at[c], p_recv.at[c], {"fsdp": partner})

        @pl.loop(0, rows // tile)
        def _(i):
            at = pl.ds(pl.multiple_of(core * rows + i * tile, tile), tile)
            w_chip[core, pl.ds(pl.multiple_of(i * tile, tile), tile), cols] = add_up(w_own, w_in, at, cols)

    def stage_up(c):
        cols = cuts[c]
        arrived(w_pair.at[:, cols], p_send.at[c], p_recv.at[c])
        w_chip[1 - core, :, cols] = w_pair[:, cols]
        chain_up(
            c, w_chip.at[:, :, cols], w_above.at[:, :, cols], w_half.at[:, :, cols], w_cross.at[:, :, cols],
            w_all.at[:, :, cols], add_wide,
        )

    def finish_rows(buf, pieces, s):
        kept = kept_ref[s]
        chosen = place_ref[s]

        @pl.loop(0, span // step)
        def _(i):
            at = pl.ds(pl.multiple_of(i * step, step), step)
            row = i * step + lax.broadcasted_iota(jnp.int32, (step, buf.shape[2]), 0)
            added = jnp.where(row < kept, pieces[chosen, at, :].astype(F32), 0.0)
            buf[s, at, :] = (buf[s, at, :].astype(F32) + added).astype(BF16)

    for copy in loads[:3] + loads[9:]:
        copy.wait()
    stage_sum(0)

    @pl.loop(0, outs // tile)
    def _(i):
        at = pl.ds(pl.multiple_of(i * tile, tile), tile)
        o_own[at, :] = add_up(o_own, o_in, at, slice(None))

    count = len(cuts)
    chain_up(count, o_own, o_above, o_half, o_cross, o_all, add_flat)
    stage_up(0)
    for copy in loads[3:6]:
        copy.wait()
    dgain[...] = jnp.zeros_like(dgain)
    for index in range(n):
        norm_back(index)
    seg = dgain.shape[1] // n
    for index, (away, turn) in enumerate(everyone):
        if index:
            peer = peer_at(n, me, away, turn)
            cols = pl.ds(pl.multiple_of(peer * seg, seg), seg)
            push(dgain.at[:, cols], d_in.at[index - 1], d_send.at[index], d_recv.at[index], {"fsdp": peer})
    chain_cross(count)
    chain_cross(0)
    s_tot[core] = s_own[...]
    s_tot[1 - core] = jnp.zeros_like(s_own)
    for index, (away, turn) in enumerate(everyone):
        if index:
            arrived(s_in.at[index - 1], s_send.at[index], s_recv.at[index])
            arrived(d_in.at[index - 1], d_send.at[index], d_recv.at[index])
            theirs = lax.rem(core + turn, 2)
            s_tot[theirs] = s_tot[theirs] + s_in[index - 1]
    mine = dgain[:, pl.ds(pl.multiple_of(me * seg, seg), seg)]
    for index in range(n - 1):
        mine = mine + d_in[index]
    s_tot[0, CONV + 3 : CONV + 4, 0:seg] = mine[0:1]
    chain_up(count + 1, s_tot, s_above, s_half, s_cross, s_all, add_small)
    for index in range(1, n):
        give_back(index)
    for c in range(1, count):
        stage_sum(c)
        stage_up(c)
        if c == 1:
            chain_out(count)
            chain_out(0)
            chain_cross(count + 1)
        else:
            chain_cross(c - 1)
            chain_out(count + 1 if c == 2 else c - 2)
    for copy in loads[6:9]:
        copy.wait()
    for s in range(n):
        finish_rows(out_buf, part, s)
    stores = [pltpu.make_async_copy(out_buf, output, here.at[6])]
    stores[0].start()
    chain_cross(count - 1)
    if count > 2:
        chain_out(count - 2)
    chain_out(count - 1)
    for k in range(count + 2):
        chain_end(k)
    sums_ref[...] = s_all[...]
    inner, group, heads = groups
    for g in range(2 * inner // group):
        q, at = g % 2, g // 2 * group
        w_ref[:, g * group : (g + 1) * group] = w_all[q, :, at : at + group].astype(F32)
        w_ref[:, 2 * inner + g * group : 2 * inner + (g + 1) * group] = (
            w_all[q, :, inner + at : inner + at + group].astype(F32)
        )
    both = w_all[0, :, 2 * inner : 2 * inner + 2 * STATE].astype(F32)
    both = both + w_all[1, :, 2 * inner : 2 * inner + 2 * STATE].astype(F32)
    w_ref[:, 4 * inner : 4 * inner + 2 * STATE] = both
    first = 2 * inner + 2 * STATE
    tails = [w_all[q, :, first : first + LANES].astype(F32) for q in range(2)]
    size = group // HEADDIM
    pieces = [tails[g % 2][:, g // 2 * size : (g // 2 + 1) * size] for g in range(2 * inner // group)]
    w_ref[:, 4 * inner + 2 * STATE :] = jnp.concatenate(pieces, axis=1)
    o_ref[...] = o_all[...].astype(F32)
    for index, (away, turn) in enumerate(everyone):
        if index:
            owner = sender_at(n, me, away, turn)
            arrived(back.at[owner], b_send.at[index], b_recv.at[index])
    back[me] = grad[rows_at(me, span), :]
    for s in range(n):
        finish_rows(grad_buf, back, s)
    stores.append(pltpu.make_async_copy(grad_buf, token_grad, here.at[7]))
    stores[1].start()
    for copy in pending:
        copy.wait_send()
    for copy in stores:
        copy.wait()


def finish_call(
    n, planes, group, length, place, kept, gn, tok, gain, early, dwin, o_early, sums, base, base_grad, branch,
):
    _, total, width = gn.shape
    span = total // n
    ahead = early[0].shape[1]
    wide = ahead + dwin.shape[1]
    inner = (n // 2) * o_early[0].shape[0]
    heads = inner // HEADDIM
    chip_rows, outs = dwin.shape[0] // (n // 2), inner // (n // 2)
    rows = chip_rows // 2
    others = n // 2 - 1
    lane_tiles = dwin.shape[1] // LANES
    late = 3
    bounds = [ahead + (lane_tiles * i + late - 1) // late * LANES for i in range(late + 1)]
    cuts = [pl.ds(0, ahead)] + [pl.ds(bounds[i], bounds[i + 1] - bounds[i]) for i in range(late)]
    pieces = late + 1
    anywhere = pl.BlockSpec(memory_space=pl.ANY)
    vmem = pl.BlockSpec(memory_space=pltpu.VMEM)
    smem = pl.BlockSpec(memory_space=pltpu.SMEM)
    dma = pltpu.SemaphoreType.DMA
    return pl.pallas_call(
        functools.partial(finish_kernel, n, planes, cuts, (inner, group, heads)),
        out_shape=[
            jax.ShapeDtypeStruct((n, span, width), BF16),
            jax.ShapeDtypeStruct((n, span, width), BF16),
            jax.ShapeDtypeStruct((rows, 4 * inner + 2 * STATE + 2 * heads), F32),
            jax.ShapeDtypeStruct((outs, width), F32),
            jax.ShapeDtypeStruct((2,) + sums.shape, F32),
        ],
        in_specs=[smem, smem, smem, anywhere, anywhere, vmem, [anywhere] * len(early), anywhere]
        + [[anywhere] * len(early), anywhere, anywhere, anywhere, anywhere],
        out_specs=[anywhere, anywhere, vmem, vmem, vmem],
        scratch_shapes=[
            pltpu.VMEM((total, width), BF16), pltpu.VMEM((total, width), BF16), pltpu.VMEM((total, width), BF16),
            pltpu.VMEM((total, width), BF16), pltpu.VMEM((8, width), F32),
            pltpu.VMEM((chip_rows, wide), BF16), pltpu.VMEM((others, chip_rows, wide), BF16),
            pltpu.VMEM((outs, width), BF16), pltpu.VMEM((others, outs, width), BF16),
            pltpu.VMEM((rows, wide), BF16), pltpu.VMEM((rows, wide), BF16), pltpu.VMEM((2, rows, wide), BF16),
            pltpu.VMEM((2, rows, wide), BF16), pltpu.VMEM((2, rows, wide), BF16), pltpu.VMEM((2, rows, wide), BF16),
            pltpu.VMEM((2, rows, wide), BF16),
            pltpu.VMEM((outs, width), BF16), pltpu.VMEM((outs, width), BF16), pltpu.VMEM((outs, width), BF16),
            pltpu.VMEM((outs, width), BF16),
            pltpu.VMEM(sums.shape, F32), pltpu.VMEM((n - 1,) + sums.shape, F32),
            pltpu.VMEM((n - 1, 8, LANES), F32), pltpu.VMEM((2,) + sums.shape, F32),
            pltpu.VMEM((2,) + sums.shape, F32), pltpu.VMEM((2,) + sums.shape, F32),
            pltpu.VMEM((2,) + sums.shape, F32), pltpu.VMEM((2,) + sums.shape, F32),
            pltpu.VMEM((n, span, width), BF16), pltpu.VMEM((n, span, width), BF16),
            pltpu.VMEM((n, span, width), BF16), pltpu.VMEM((n, span, width), BF16),
            dma((9 + 2 * others,)), dma((n,)), dma((n,)), dma((n,)), dma((n,)),
            dma((pieces * others,)), dma((pieces * others,)), dma((others,)), dma((others,)),
            dma((pieces,)), dma((pieces,)), dma((n,)), dma((n,)), dma((n,)), dma((n,)),
            dma((pieces + 2,)), dma((pieces + 2,)), dma((pieces + 2,)), dma((pieces + 2,)),
            dma((pieces + 2,)), dma((pieces + 2,)),
        ],
        compiler_params=pltpu.CompilerParams(
            collective_id=1, has_side_effects=True, vmem_limit_bytes=60 * 1024 * 1024
        ),
        name="finish",
    )(length, place, kept, gn, tok, gain, early, dwin, o_early, sums, base, base_grad, branch)


def pairs_of(n):
    return [[2 * c, 2 * c + 1] for c in range(n // 2)]


def columns_of(n):
    return [list(range(q, n, 2)) for q in range(2)]


def halves(array, axis, group):
    shape = array.shape
    view = array.reshape(shape[:axis] + (shape[axis] // (2 * group), 2, group) + shape[axis + 1 :])
    out = []
    for q in range(2):
        part = lax.index_in_dim(view, q, axis + 1, keepdims=False)
        out.append(part.reshape(shape[:axis] + (shape[axis] // 2,) + shape[axis + 1 :]))
    return out


def interleave(first, second, axis, group):
    shape = first.shape
    views = [
        part.reshape(shape[:axis] + (shape[axis] // group, 1, group) + shape[axis + 1 :]) for part in (first, second)
    ]
    return jnp.concatenate(views, axis=axis + 1).reshape(shape[:axis] + (2 * shape[axis],) + shape[axis + 1 :])


def body(
    tokens, cotangent, lengths, dealing, norm_gain, in_weight, conv_weight, conv_bias, dt_bias, a_log, skip_gain,
    out_gain, out_weight,
):
    n = lax.axis_size("fsdp")
    me = lax.axis_index("fsdp")
    core = lax.rem(me, 2)
    pairs, columns = pairs_of(n), columns_of(n)
    local_tokens, local_grad = tokens[0], cotangent[0]
    count, span, width = local_tokens.shape
    length = span * n
    inner = INNER // 2
    heads = HEADS // 2
    group = max(HEADDIM, INNER // n)
    blocks = length // BLOCK
    rows = in_weight.shape[0]

    slots = jnp.arange(count, dtype=jnp.int32)
    own = jnp.sum(jnp.where(dealing[0][:, None] == slots[None, :], lengths[0][None, :], 0), axis=1)
    ahead = (own[None, :] > own[:, None]) | ((own[None, :] == own[:, None]) & (slots[None, :] < slots[:, None]))
    rank = jnp.sum(ahead.astype(jnp.int32), axis=1)
    place = jnp.where(rank < count // 2, 2 * rank, 2 * (count - 1 - rank) + 1)
    source = jnp.sum(jnp.where(place[None, :] == slots[:, None], slots[None, :], 0), axis=1)
    placed = jnp.sum(jnp.where(place[None, :] == slots[:, None], own[None, :], 0), axis=1)
    chip_lens = lax.dynamic_slice_in_dim(placed, me - core, 2)
    chip_blocks = (chip_lens + BLOCK - 1) // BLOCK
    grid_steps = most_blocks(count, length)

    main = INNER + INNER + 2 * STATE
    gates = halves(in_weight[:, :INNER], 1, group)
    vals = halves(in_weight[:, INNER : 2 * INNER], 1, group)
    both = in_weight[:, 2 * INNER : main]
    steps = halves(in_weight[:, main:], 1, group // HEADDIM)
    pad = jnp.zeros((rows, LANES - heads), BF16)
    shards = jnp.stack([jnp.concatenate([gates[q], vals[q], both, steps[q], pad], axis=1) for q in range(2)])
    aligned = INNER // n >= HEADDIM
    small = jnp.concatenate([norm_gain, conv_weight.reshape(-1), conv_bias, out_gain])
    room = -(-small.shape[0] // (16 * LANES)) * 16
    small = jnp.pad(small, (0, room * LANES - small.shape[0])).reshape(room, LANES)
    tok, win, smalls, sent_grad = start_call(n, source, local_tokens, local_grad, shards, small)
    tok, sent_grad, out_weight = lax.optimization_barrier((tok, sent_grad, out_weight))
    smalls = smalls.reshape(n, -1).astype(F32)
    own_grad = lax.all_to_all(sent_grad, "fsdp", split_axis=0, concat_axis=0, tiled=True)
    if aligned:
        wout = lax.all_gather(out_weight, "fsdp", axis=0, tiled=True, axis_index_groups=columns)
    else:
        whole = lax.all_gather(out_weight, "fsdp", axis=0, tiled=True)
        wout = lax.dynamic_index_in_dim(jnp.stack(halves(whole, 0, group)), core, 0, keepdims=False)
    cuts = [norm_gain.shape[0], conv_weight.size, conv_bias.shape[0], out_gain.shape[0]]
    ends = [sum(cuts[: i + 1]) for i in range(4)]
    first_gain = smalls[:, : ends[0]].reshape(-1)
    conv_w = smalls[:, ends[0] : ends[1]].reshape(n, CONV, -1).transpose(1, 0, 2).reshape(CONV, -1)
    conv_b = smalls[:, ends[1] : ends[2]].reshape(1, -1)
    gated_gain = smalls[:, ends[2] : ends[3]].reshape(1, -1)

    def half_of(array, axis, size):
        return lax.dynamic_index_in_dim(jnp.stack(halves(array, axis, size)), core, 0, keepdims=False)

    conv_all = jnp.concatenate([conv_w, conv_b, jnp.zeros((3, conv_w.shape[1]), F32)], axis=0)
    conv_all = jnp.concatenate([half_of(conv_all[:, :INNER], 1, group), conv_all[:, INNER:]], axis=1)
    head_rows = jnp.stack([dt_bias, jnp.exp(a_log), skip_gain] + [jnp.zeros_like(dt_bias)] * 5)
    head_rows = half_of(head_rows, 1, group // HEADDIM)
    dwide = jnp.repeat(head_rows[2:3], HEADDIM, axis=1)
    hp = jnp.concatenate([head_rows, jnp.zeros((8, LANES - heads), F32)], axis=1)
    og = half_of(gated_gain, 1, group)
    gain = first_gain[None, :]
    cb = conv_all[CONV : CONV + 1]
    args = (gain, win, conv_all, cb, hp, dwide, og)
    gate, cin, raw, y, states, ss, mixing = fwd_call(grid_steps, chip_blocks, tok, *args)

    own_grad, mixing = lax.optimization_barrier((own_grad, mixing))
    cot = pair_call(own_grad.reshape(length, width))
    gm, v, bp = mid_call(grid_steps, chip_blocks, chip_lens, cot, mixing, wout)
    branch, rv = exchange_call(bp, ss, v)

    def restore(part):
        return lax.all_to_all(part.reshape(n, span, width), "fsdp", split_axis=0, concat_axis=0, tiled=True)

    kept = jnp.clip(own - me * span, 0, span)
    branch = restore(branch)
    parts = n // 2
    planes = lax.axis_size("rep")
    fused = aligned and planes == 4 and rows % (16 * planes) == 0 and out_weight.shape[0] % (16 * planes) == 0
    chip = (me // 2 if fused else me * 0).reshape(1)
    dy, gp, dog, *early = gate_call(
        grid_steps, chip_blocks, chip_lens, chip, parts, tok, cot, gain, win, gm, og, gate, y, rv
    )
    early, dwout = early[:parts], early[parts:]
    if fused:

        def move(pieces):
            return [pieces[0]] + [
                lax.ppermute(pieces[away], "fsdp", [(d, (d + 2 * away) % n) for d in range(n)])
                for away in range(1, parts)
            ]

        early, dwout = move(early), move(dwout)
    gn, dwin, sums = bwd_call(
        grid_steps, chip_blocks, tok, gain, win, *args[2:6], dog, dy, gp, cin, raw, y, states
    )
    def widen(half, axis, size):
        zero = jnp.zeros_like(half)
        return interleave(jnp.where(core == 0, half, zero), jnp.where(core == 1, half, zero), axis, size)

    own_len = lax.dynamic_slice_in_dim(chip_lens, core, 1)
    if fused:
        output, token_grad, dwin, dwout, sums = finish_call(
            n, planes, group, own_len, place, kept, gn, tok, gain, early, dwin, dwout, sums, local_tokens, local_grad,
            branch,
        )
        dgain = sums[0, CONV + 3, : width // n]
        halves_of = [sums[0], sums[1]]
    else:
        halves_of = [jnp.where(core == q, sums, jnp.zeros_like(sums)) for q in range(2)]
    first, second = halves_of
    dconv = jnp.concatenate(
        [
            interleave(first[: CONV + 1, :inner], second[: CONV + 1, :inner], 1, group),
            first[: CONV + 1, inner:] + second[: CONV + 1, inner:],
        ],
        axis=1,
    )
    dheads = jnp.concatenate(
        [
            interleave(
                first[CONV + 2 : CONV + 3, at : at + heads], second[CONV + 2 : CONV + 3, at : at + heads], 1,
                group // HEADDIM,
            )
            for at in range(0, 3 * LANES, LANES)
        ],
        axis=0,
    )
    dog = interleave(first[CONV + 1, :inner], second[CONV + 1, :inner], 0, group)
    if not fused:
        other = lax.dynamic_index_in_dim(gn, 1 - core, 0, keepdims=False)
        other = lax.ppermute(other, "fsdp", [(2 * c + q, 2 * c + 1 - q) for c in range(n // 2) for q in range(2)])
        mine = lax.dynamic_index_in_dim(gn, core, 0, keepdims=False)
        hidden = lax.dynamic_index_in_dim(tok, core, 0, keepdims=False).astype(F32)
        inv = lax.rsqrt(jnp.mean(hidden * hidden, axis=-1, keepdims=True) + EPS)
        position = jnp.arange(length, dtype=jnp.int32)[:, None]
        grad_normed = jnp.where(position < own_len[0], mine.astype(F32) + other.astype(F32), 0.0)
        dgain = jnp.sum(grad_normed * hidden * inv, axis=0)
        scaled = grad_normed * first_gain[None, :]
        grad_hidden = inv * scaled - hidden * (inv * inv * inv) * jnp.mean(scaled * hidden, axis=-1, keepdims=True)
        back = restore(grad_hidden.astype(BF16))
        dwin = jnp.concatenate([jnp.concatenate(early, axis=0), dwin], axis=1)
        dwout = jnp.concatenate(dwout, axis=0)
        dwin = lax.psum_scatter(
            dwin.astype(F32), "fsdp", scatter_dimension=0, tiled=True, axis_index_groups=columns
        )
        dwin = lax.psum(dwin, "rep").reshape(2, rows, -1)
        dwin = lax.all_to_all(dwin, "fsdp", split_axis=0, concat_axis=0, tiled=True, axis_index_groups=pairs)
        if aligned:
            dwout = lax.psum_scatter(
                dwout.astype(F32), "fsdp", scatter_dimension=0, tiled=True, axis_index_groups=columns
            )
        else:
            wide_grad = widen(dwout.astype(F32), 0, group)
            dwout = lax.psum_scatter(wide_grad, "fsdp", scatter_dimension=0, tiled=True)
        dwout = lax.psum(dwout, "rep")
        c0, c1, c2 = inner, 2 * inner, 2 * inner + 2 * STATE
        dwin = jnp.concatenate(
            [
                interleave(dwin[0, :, :c0], dwin[1, :, :c0], 1, group),
                interleave(dwin[0, :, c0:c1], dwin[1, :, c0:c1], 1, group),
                dwin[0, :, c1:c2] + dwin[1, :, c1:c2],
                interleave(dwin[0, :, c2 : c2 + heads], dwin[1, :, c2 : c2 + heads], 1, group // HEADDIM),
            ],
            axis=1,
        )
        dconv, dheads, dog, dgain = lax.psum((dconv, dheads, dog, dgain), ("rep", "fsdp"))
        dgain = lax.dynamic_slice_in_dim(dgain, me * (width // n), width // n)
        output = combine_call(place, kept, local_tokens, branch)
        token_grad = combine_call(place, kept, local_grad, back)

    def shard(array):
        size = array.shape[-1] // n
        return lax.dynamic_slice_in_dim(array, me * size, size, axis=array.ndim - 1)

    dconv = shard(dconv)
    return (
        output[None], token_grad[None], dgain, dwin, dconv[:CONV], dconv[CONV], dheads[1], dheads[2], dheads[0],
        shard(dog), dwout,
    )


def solution(mesh):
    row = P("rep", None, "fsdp", None)
    per = P("rep", None)
    in_specs = (
        row, row, per, per, P("fsdp"), P("fsdp", None), P(None, "fsdp"), P("fsdp"), P(), P(), P(), P("fsdp"),
        P("fsdp", None),
    )
    out_specs = (
        row, row, P("fsdp"), P("fsdp", None), P(None, "fsdp"), P("fsdp"), P(), P(), P(), P("fsdp"), P("fsdp", None),
    )
    return jax.shard_map(body, mesh=mesh, in_specs=in_specs, out_specs=out_specs, check_vma=False)
```
